32 devices in a mesh: dp: 8 (over y, x, core), fsdp: 4 (over z).
Axes of the slice: x: 2, y: 2, z: 4, core: 2. Of those that a mesh axis runs over, the one named last changes fastest.
Arguments:
- tokens: bfloat16 [30336, 768], P(('dp', 'fsdp')), may hold values from -6 to 6
- modality: int32 [30336], P(('dp', 'fsdp')), may hold values from 0 to 1, as said below
- token_mask: int32 [30336], P(('dp', 'fsdp')), may hold values from 0 to 1, as said below
- cotangent: bfloat16 [30336, 768], P(('dp', 'fsdp')), may hold values from -6 to 6
- mask_vector: bfloat16 [768], replicated, may hold values from -4 to 4
- ln_one_gain: bfloat16 [768], P(('dp', 'fsdp')), may hold values from 0.25 to 1.75
- ln_one_shift: bfloat16 [768], P(('dp', 'fsdp')), may hold values from -3 to 3
- w_qkv: bfloat16 [768, 2304], P(('dp', 'fsdp')), may hold values from -0.21875 to 0.21875
- w_out: bfloat16 [768, 768], P(('dp', 'fsdp')), may hold values from -1.75 to 1.75
- ln_two_gain: bfloat16 [768], P(('dp', 'fsdp')), may hold values from 0.25 to 1.75
- ln_two_shift: bfloat16 [768], P(('dp', 'fsdp')), may hold values from -3 to 3
- w_up: bfloat16 [2, 768, 3072], P(None, ('dp', 'fsdp')), may hold values from -0.21875 to 0.21875
- w_down: bfloat16 [2, 3072, 768], P(None, ('dp', 'fsdp')), may hold values from -0.109375 to 0.109375
Outputs:
- output: bfloat16 [30336, 768], P(('dp', 'fsdp'))
- grad_tokens: float32 [30336, 768], P(('dp', 'fsdp'))
- grad_mask_vector: float32 [768], replicated
- grad_ln_one_gain: float32 [768], P(('dp', 'fsdp'))
- grad_ln_one_shift: float32 [768], P(('dp', 'fsdp'))
- grad_w_qkv: float32 [768, 2304], P(('dp', 'fsdp'))
- grad_w_out: float32 [768, 768], P(('dp', 'fsdp'))
- grad_ln_two_gain: float32 [768], P(('dp', 'fsdp'))
- grad_ln_two_shift: float32 [768], P(('dp', 'fsdp'))
- grad_w_up: float32 [768, 3072], P(('dp', 'fsdp'))
- grad_w_down: float32 [3072, 768], P(('dp', 'fsdp'))
The draws below stay inside these ranges and needn't reach their ends.
Inputs may be any that keep to these rules, and one draw needn't show every extreme that they name: `modality`: in each of the 128 sequences of 237 consecutive tokens, either the first 197 tokens are image tokens (0) and the last 40 are text tokens (1), or all 237 are text tokens. `token_mask`: 1 only at text tokens (where modality is 1).
All inputs are finite; a program needn't handle non-finite values.
Results may differ from the reference program's by a relative error of at most 0.011.
Values may be sent and summed in bfloat16 or wider, within the bound.
No kernel may reach another device: no remote copies, remote signals or barrier semaphores. Data moves between devices by JAX's collectives and lax.ppermute only.
A program may use at most 192 MiB of HBM per device.

```python
import math
import jax
import jax.numpy as jnp
from jax import lax

D = 768
H = 12
HD = 64
FF = 3072
PATCHES = 197
SEQ_DEV = 4
LEN = 237
SEQS = 128
TOKENS = 30336
N_FSDP = 4


def sequence_kinds(key):
    return jax.random.randint(jax.random.fold_in(key, 17), (SEQS,), 0, 4)


def text_layout(sequence_type):
    position = jnp.arange(LEN, dtype=jnp.int32)
    beyond = (position[None, :] >= PATCHES).astype(jnp.int32)
    return jnp.where(sequence_type[:, None] == 0, 1, beyond).astype(jnp.int32)


def draw_modality(key, part):
    sequence_type = sequence_kinds(key)
    return text_layout(sequence_type).reshape(-1)


def draw_token_mask(key, part):
    sequence_type = sequence_kinds(key)
    key = jax.random.fold_in(key, 5)
    tier_roll = jax.random.randint(jax.random.fold_in(key, 1), (SEQS,), 0, 16)
    levels = jnp.where(tier_roll < 11, 3, jnp.where(tier_roll < 15, 7, 14))
    dice_rolls = jax.random.randint(jax.random.fold_in(key, 2), (SEQS, LEN), 0, 20)
    chosen = (dice_rolls < levels[:, None]).astype(jnp.int32)
    return (chosen * text_layout(sequence_type)).reshape(-1).astype(jnp.int32)


def level_of(key, extent, cuts, least, high):
    gain, own = 1.0, jax.random.fold_in(key, 6)
    for dim, shards_of in cuts:
        heights = jnp.exp(jax.random.uniform(jax.random.fold_in(own, dim), (shards_of,), jnp.float32, least / len(cuts), high / len(cuts)))
        gain = gain * jnp.repeat(heights, extent[dim] // shards_of).reshape([-1 if axis == dim else 1 for axis in range(len(extent))])
    return gain


def normal_values(own_key, extent, deviation, bound, split=(), kind=jnp.bfloat16):
    values = jax.random.normal(own_key, extent, jnp.float32) * deviation
    if len(split) > 0:
        values = level_of(own_key, extent, split, -0.22, 0.18) * values
    return jnp.clip(values, min=-bound, max=bound).astype(kind)


def setup_inputs(seed: int = 0) -> dict:
    splits = jax.random.split(jax.random.key(seed), 14)
    return {
        "tokens": normal_values(splits[0], (TOKENS, D), 1.0, 6.0, ((0, 32),)),
        "modality": draw_modality(jax.random.fold_in(splits[13], 71), 0),
        "token_mask": draw_token_mask(jax.random.fold_in(splits[13], 71), 0),
        "cotangent": normal_values(splits[3], (TOKENS, D), 1.0, 6.0, ((0, 32),)),
        "mask_vector": normal_values(splits[4], (D,), 1.0, 4.0),
        "ln_one_gain": jnp.clip(1.0 + 0.15 * jax.random.normal(splits[5], (D,), jnp.float32), 0.25, 1.75).astype(jnp.bfloat16),
        "ln_one_shift": normal_values(splits[6], (D,), 0.3, 3.0, ((0, 32),)),
        "w_qkv": normal_values(splits[7], (D, 3 * D), D ** -0.5, 0.21875, ((0, 32),)),
        "w_out": normal_values(splits[8], (D, D), (D // 64) ** -0.5, 1.75, ((0, 32),)),
        "ln_two_gain": jnp.clip(1.0 + 0.15 * jax.random.normal(splits[9], (D,), jnp.float32), 0.25, 1.75).astype(jnp.bfloat16),
        "ln_two_shift": normal_values(splits[10], (D,), 0.3, 3.0, ((0, 32),)),
        "w_up": normal_values(splits[11], (2, D, FF), D ** -0.5, 0.21875, ((1, 32),)),
        "w_down": normal_values(splits[12], (2, FF, D), FF ** -0.5, 0.109375, ((1, 32),)),
    }


@jax.custom_vjp
def low(v):
    return lax.optimization_barrier(v.astype(jnp.bfloat16)).astype(jnp.float32)

@jax.custom_vjp
def low_back(v):
    return v

def low_keep(v):
    return (low(v), None)

def low_pass(kept, grad):
    return (grad,)

def back_keep(v):
    return (v, None)

def back_low(kept, grad):
    return (low(grad),)
low.defvjp(low_keep, low_pass)
low_back.defvjp(back_keep, back_low)

def layer_norm(values, gain_row, shift_row):
    centred = values - lax.optimization_barrier(jnp.mean(values, -1, keepdims=True))
    spread = lax.optimization_barrier(jnp.mean(centred * centred, -1, keepdims=True))
    return centred * lax.rsqrt(spread + 1e-05) * gain_row + shift_row

def product(left, right):
    return jnp.dot(left, right, precision=lax.Precision.HIGHEST)

def forward(row_block, masked, modality, mask_vector, ln_one_gain, ln_one_shift, w_qkv, w_out, ln_two_gain, ln_two_shift, w_up, w_down):
    seq_count = row_block.shape[0] // LEN
    start = jnp.where(masked[:, None], mask_vector[None, :], row_block)
    normed_one = low(layer_norm(start, ln_one_gain, ln_one_shift))
    qkv = low_back(low(product(normed_one, w_qkv))).reshape(seq_count, LEN, 3, H, HD)
    queries = qkv[:, :, 0]
    key_rows = qkv[:, :, 1]
    values = qkv[:, :, 2]
    scores = low_back(jnp.einsum('sqhd,skhd->shqk', queries, key_rows, precision=lax.Precision.HIGHEST) * (1.0 / math.sqrt(HD)))
    attention = low(jax.nn.softmax(scores, axis=-1))
    context = low_back(low(jnp.einsum('shqk,skhd->sqhd', attention, values, precision=lax.Precision.HIGHEST)))
    context = context.reshape(seq_count * LEN, D)
    hidden = start + low_back(product(context, w_out))
    normed_two = low(layer_norm(hidden, ln_two_gain, ln_two_shift))
    outputs = []
    for expert_id in range(2):
        pre_act = low_back(product(normed_two, w_up[expert_id]))
        activated = low(jax.nn.gelu(pre_act, approximate=False))
        outputs.append(product(activated, w_down[expert_id]))
    branch = low_back(jnp.where(modality[:, None] == 0, outputs[0], outputs[1]))
    return hidden + branch

def reference(tokens, modality, token_mask, cotangent, mask_vector, ln_one_gain, ln_one_shift, w_qkv, w_out, ln_two_gain, ln_two_shift, w_up, w_down):
    params = tuple((member.astype(jnp.float32) for member in (mask_vector, ln_one_gain, ln_one_shift, w_qkv, w_out, ln_two_gain, ln_two_shift, w_up, w_down)))
    group_rows = SEQ_DEV * LEN * N_FSDP
    group_count = TOKENS // group_rows

    def step_group(totals, pieces):
        row_block, modal_block, mask_block, cot_block = pieces
        masked = mask_block == 1

        def with_inputs(row_input, *weights):
            return forward(row_input, masked, modal_block, *weights)
        result, pullback = jax.vjp(with_inputs, row_block, *params)
        gradients = pullback(cot_block * masked[:, None].astype(jnp.float32))
        totals = tuple((current + incoming for current, incoming in zip(totals, gradients[1:])))
        return (totals, (result, gradients[0]))
    zeros_start = tuple((jnp.zeros_like(member) for member in params))
    inputs = (tokens.astype(jnp.float32).reshape(group_count, group_rows, D), modality.reshape(group_count, group_rows), token_mask.reshape(group_count, group_rows), cotangent.astype(jnp.float32).reshape(group_count, group_rows, D))
    totals, (results, input_grads) = lax.scan(step_group, zeros_start, inputs)
    return (results.reshape(TOKENS, D).astype(jnp.bfloat16), input_grads.reshape(TOKENS, D), totals[0], totals[1], totals[2], totals[3], totals[4], totals[5], totals[6], totals[7][1], totals[8][1])
```

```python
import functools
import math

import jax
import jax.numpy as jnp
from jax import lax
from jax.experimental import pallas as pl
from jax.experimental.pallas import tpu as pltpu
from jax.sharding import Mesh, PartitionSpec as P

H = 12
HD = 64
LEN = 237
PATCHES = 197
HEAD = 208
TAIL = 48
SEQ = HEAD + TAIL
D = H * HD
FF = 4 * D
BLK = 256
EPS = 1e-05
F32 = jnp.float32
BF16 = jnp.bfloat16
MIB = 1 << 20
UP, DOWN, OUT, EXTRA = 0, 384, 768, 864
ROWS_ONE = 880
ROWS_TWO = 304


def dot(a, b):
    return jnp.dot(a, b, preferred_element_type=F32)


def dot_nt(a, b):
    return lax.dot_general(a, b, (((1,), (1,)), ((), ())), preferred_element_type=F32)


def dot_tn(a, b):
    return lax.dot_general(a, b, (((0,), (0,)), ((), ())), preferred_element_type=F32)


def mean(rows):
    return jnp.mean(rows, -1, keepdims=True)


def normalize(rows):
    centred = rows - mean(rows)
    inverse = lax.rsqrt(mean(centred * centred) + EPS)
    return centred * inverse, inverse


def normalize_back(grad, unit, inverse, gain):
    scaled = grad * gain
    return inverse * (scaled - mean(scaled) - unit * mean(scaled * unit))


def total(rows):
    return jnp.sum(rows, 0, keepdims=True)


def halves(pair):
    lane = lax.broadcasted_iota(jnp.int32, pair.shape, 1)
    zero = jnp.zeros_like(pair)
    return jnp.concatenate(
        [jnp.where(lane < HD, pair, zero), jnp.where(lane < HD, zero, pair)], 0
    )


def softmax_pair(queries, keys_cat):
    scores = dot_nt(queries, keys_cat)
    out = []
    for head in range(2):
        own = scores[:, head * SEQ : (head + 1) * SEQ]
        key = lax.broadcasted_iota(jnp.int32, own.shape, 1)
        valid = (key < PATCHES) | ((key >= HEAD) & (key < HEAD + LEN - PATCHES))
        own = jnp.where(valid, own, -1e30)
        peak = jnp.max(own, -1, keepdims=True)
        powers = jnp.exp(own - peak)
        out.append(powers / jnp.sum(powers, -1, keepdims=True))
    return jnp.concatenate(out, 1)


def load_pieces(where_ref, pieces, target, sems, columns):
    copies = [
        pltpu.make_async_copy(
            piece.at[:, pl.ds(columns[0], columns[1])],
            target.at[pl.ds(pl.multiple_of(where_ref[j] * 96, 96), 96), :],
            sems.at[j],
        )
        for j, piece in enumerate(pieces)
    ]
    for copy in copies:
        copy.start()
    for copy in copies:
        copy.wait()


def attention_kernel(where_ref, tokens, masked, vector, *rest):
    pieces, (qkv, context, hidden, normed_one, normed_two, params, weights, sems) = (
        rest[:8],
        rest[8:],
    )

    @pl.when(pl.program_id(0) == 0)
    def _():
        load_pieces(where_ref, pieces, weights, sems, (0, weights.shape[1]))
        columns = weights[:, 4 * D : 4 * D + 128].astype(F32)
        params[...] = jnp.transpose(columns)[:8]

    start = jnp.where(masked[...] == 1.0, vector[...], tokens[...].astype(F32))
    unit, _ = normalize(start)
    first = (unit * params[0:1] + params[1:2]).astype(BF16)
    normed_one[...] = first
    for third in range(3):
        at = pl.ds(third * D, D)
        qkv[:, at] = dot(first, weights[:, at]).astype(BF16)
    for pair in range(H // 2):
        queries = qkv[:, pl.ds(pair * 128, 128)] * BF16(1.0 / math.sqrt(HD))
        keys = halves(qkv[:, pl.ds(D + pair * 128, 128)])
        values = halves(qkv[:, pl.ds(2 * D + pair * 128, 128)])
        attention = softmax_pair(queries, keys).astype(BF16)
        context[:, pl.ds(pair * 128, 128)] = dot(attention, values).astype(BF16)
    after = start + dot(context[...], weights[:, pl.ds(3 * D, D)])
    hidden[...] = after
    unit, _ = normalize(after)
    normed_two[...] = (unit * params[2:3] + params[3:4]).astype(BF16)


def feed_back_kernel(
    where_ref, place, hidden, cotangent, context, params, up, down, *rest
):
    pieces = rest[:8]
    (keep, send, grad_context, sums) = rest[8:12]
    (high, low, rows_two, rows_cot, rows_context, rows_hidden, grad_two) = rest[12:19]
    (sum_up, sum_down, w_out, stage, sems, out_sems) = rest[19:]
    step = pl.program_id(0)
    blocks = where_ref[10]
    core = where_ref[8]

    def chosen(block):
        row = lax.broadcasted_iota(jnp.int32, (BLK, place.shape[1]), 0) + block * BLK
        return jnp.where(row == place[...], 1.0, 0.0).astype(BF16)

    def rows_of(block):
        return pl.ds(pl.multiple_of(block * BLK, BLK), BLK)

    @pl.when(step == 0)
    def _():
        load_pieces(where_ref, pieces, w_out, sems, (3 * D, D))
        high[...] = hidden[...].astype(BF16)
        low[...] = (hidden[...] - high[...].astype(F32)).astype(BF16)

        def gather(block, _):
            pick, at = chosen(block), rows_of(block)
            rows = dot(pick, high[...]) + dot(pick, low[...])
            rows_hidden[at, :] = rows
            rows_cot[at, :] = dot(pick, cotangent[...]).astype(BF16)
            rows_context[at, :] = dot(pick, context[...]).astype(BF16)
            unit, _ = normalize(rows)
            rows_two[at, :] = (unit * params[2:3] + params[3:4]).astype(BF16)
            grad_two[at, :] = jnp.zeros((BLK, D), F32)
            return 0

        lax.fori_loop(0, blocks, gather, 0)

    def expert(block, _):
        at = rows_of(block)
        rows, grads = rows_two[at, :], rows_cot[at, :]
        pre = dot(rows, up[0])
        chance = 0.5 * (1.0 + lax.erf(pre * math.sqrt(0.5)))
        activated = (pre * chance).astype(BF16)
        slope = chance + pre * (jnp.exp(-0.5 * pre * pre) * (1.0 / math.sqrt(2.0 * math.pi)))
        grad_pre = (dot_nt(grads, down[...]) * slope).astype(BF16)
        grad_two[at, :] += dot_nt(grad_pre, up[0])
        add_down = dot_tn(activated, grads)
        add_up = dot_tn(rows, grad_pre)

        @pl.when(block == 0)
        def _():
            sum_down[...] = add_down
            sum_up[...] = add_up

        @pl.when(block > 0)
        def _():
            sum_down[...] += add_down
            sum_up[...] += add_up

        return 0

    lax.fori_loop(0, blocks, expert, 0)
    up_at = pl.ds(pl.multiple_of(step * 96, 96), 96)
    mine = jnp.bitwise_xor(step, where_ref[9])
    for side in range(2):
        for j in range(4):
            source = pl.ds(pl.multiple_of(where_ref[4 * side + j] * 96, 96), 96)
            stage[side, j, up_at, :] = sum_up[source, :].astype(BF16)
        half = core if side == 0 else 1 - core
        source = pl.ds(pl.multiple_of(half * 384, 384), 384)
        stage[side, mine, pl.ds(DOWN, 384), :] = sum_down[source, :].astype(BF16)

    @pl.when(step == pl.num_programs(0) - 1)
    def _():
        grad_context[...] = jnp.zeros_like(grad_context)
        sums[...] = jnp.zeros_like(sums)
        sum_up[...] = jnp.zeros_like(sum_up)

        def back(block, _):
            pick, at = chosen(block), rows_of(block)
            unit, inverse = normalize(rows_hidden[at, :])
            grad = grad_two[at, :]
            grad_hidden = rows_cot[at, :].astype(F32) + normalize_back(
                grad, unit, inverse, params[2:3]
            )
            sums[0:1] += total(grad * unit)
            sums[1:2] += total(grad)
            sums[2:3] += total(grad_hidden)
            grad_attn = grad_hidden.astype(BF16)
            sum_up[...] += dot_tn(rows_context[at, :], grad_attn)
            rows = dot_nt(grad_attn, w_out[...]).astype(BF16)
            grad_context[...] += dot_tn(pick, rows).astype(BF16)
            return 0

        lax.fori_loop(0, blocks, back, 0)
        extra = jnp.concatenate([sums[...], jnp.zeros_like(sums[...])], 0).astype(BF16)
        for side, out in enumerate((keep, send)):
            for j in range(4):
                source = pl.ds(pl.multiple_of(where_ref[4 * side + j] * 96, 96), 96)
                stage[side, j, pl.ds(OUT, 96), :] = sum_up[source, :].astype(BF16)
                stage[side, j, pl.ds(EXTRA, 16), :] = extra
            pltpu.make_async_copy(stage.at[side], out, out_sems.at[side]).start()
        for side, out in enumerate((keep, send)):
            pltpu.make_async_copy(stage.at[side], out, out_sems.at[side]).wait()


def attention_back_kernel(
    where_ref, qkv, grad_context, normed_one, tokens, masked, vector, params, *rest
):
    pieces = rest[:8]
    keep, send, grad_tokens = rest[8:11]
    weights, sum_qkv, sums, grad_qkv, stage, sems, out_sems = rest[11:]
    step = pl.program_id(0)

    @pl.when(step == 0)
    def _():
        load_pieces(where_ref, pieces, weights, sems, (0, 3 * D))
        sums[...] = jnp.zeros_like(sums)

    inv_root = 1.0 / math.sqrt(HD)
    lane = lax.broadcasted_iota(jnp.int32, (SEQ, 128), 1)
    for pair in range(H // 2):
        at = pl.ds(pair * 128, 128)
        queries = qkv[:, pl.ds(pair * 128, 128)]
        keys = halves(qkv[:, pl.ds(D + pair * 128, 128)])
        values = halves(qkv[:, pl.ds(2 * D + pair * 128, 128)])
        grads = grad_context[:, at]
        soft = softmax_pair(queries * BF16(inv_root), keys)
        grad_soft = dot_nt(grads, values)
        parts = []
        for head in range(2):
            span = slice(head * SEQ, (head + 1) * SEQ)
            own, grad = soft[:, span], grad_soft[:, span]
            parts.append(own * (grad - jnp.sum(own * grad, -1, keepdims=True)))
        grad_scores = jnp.concatenate(parts, 1).astype(BF16)
        grad_qkv[:, at] = (dot(grad_scores, keys) * inv_root).astype(BF16)
        by_key = dot_tn(grad_scores, queries) * inv_root
        grad_qkv[:, pl.ds(D + pair * 128, 128)] = jnp.where(
            lane < HD, by_key[:SEQ], by_key[SEQ:]
        ).astype(BF16)
        by_value = dot_tn(soft.astype(BF16), grads)
        grad_qkv[:, pl.ds(2 * D + pair * 128, 128)] = jnp.where(
            lane < HD, by_value[:SEQ], by_value[SEQ:]
        ).astype(BF16)
    first = normed_one[...]
    for third in range(3):
        at = pl.ds(third * D, D)
        add = dot_tn(first, grad_qkv[:, at])

        @pl.when(step == 0)
        def _():
            sum_qkv[third] = add

        @pl.when(step > 0)
        def _():
            sum_qkv[third] += add

    grad_one = dot_nt(grad_qkv[...], weights[...])
    start = jnp.where(masked[...] == 1.0, vector[...], tokens[...].astype(F32))
    unit, inverse = normalize(start)
    grad_start = normalize_back(grad_one, unit, inverse, params[0:1])
    grad_tokens[...] = jnp.where(masked[...] == 1.0, 0.0, grad_start)
    sums[0:1] += total(grad_one * unit)
    sums[1:2] += total(grad_one)
    sums[2:3] += total(jnp.where(masked[...] == 1.0, grad_start, 0.0))

    @pl.when(step == pl.num_programs(0) - 1)
    def _():
        extra = jnp.concatenate([sums[...], jnp.zeros_like(sums[...])], 0).astype(BF16)
        for side, out in enumerate((keep, send)):
            for j in range(4):
                source = pl.ds(pl.multiple_of(where_ref[4 * side + j] * 96, 96), 96)
                for third in range(3):
                    stage[side, j, pl.ds(third * 96, 96), :] = sum_qkv[
                        third, source, :
                    ].astype(BF16)
                stage[side, j, pl.ds(288, 16), :] = extra
            pltpu.make_async_copy(stage.at[side], out, out_sems.at[side]).start()
        for side, out in enumerate((keep, send)):
            pltpu.make_async_copy(stage.at[side], out, out_sems.at[side]).wait()


def gelu(pre):
    return (pre * (0.5 * (1.0 + lax.erf(pre * math.sqrt(0.5))))).astype(BF16)


def feed_kernel(text, where_ref, rows_in, before, up, down, out, sums, *scratch):
    step = pl.program_id(0)
    seqs = rows_in.shape[0] // SEQ

    @pl.when(step == 0)
    def _():
        sums[...] = before[...]

    for seq in range(seqs):
        head = pl.ds(seq * SEQ, HEAD)

        @pl.when(where_ref[11 + seq] == int(text))
        def _():
            activated = gelu(dot(rows_in[head, :], up[0]))
            sums[head, :] += dot(activated, down[...])

    if text:
        (tails,) = scratch

        @pl.when(step == 0)
        def _():
            for seq in range(seqs):
                tails[pl.ds(seq * TAIL, TAIL), :] = rows_in[pl.ds(seq * SEQ + HEAD, TAIL), :]

        more = dot(gelu(dot(tails[...], up[0])), down[...])
        for seq in range(seqs):
            sums[pl.ds(seq * SEQ + HEAD, TAIL), :] += more[seq * TAIL : (seq + 1) * TAIL]

    @pl.when(step == pl.num_programs(0) - 1)
    def _():
        out[...] = sums[...].astype(out.dtype)


def whole(shape):
    return pl.BlockSpec(shape, lambda *_: (0,) * len(shape), pipeline_mode=pl.Buffered(1))


def by_step(shape):
    return pl.BlockSpec(shape, lambda i, *_: (i,) + (0,) * (len(shape) - 1))


ANY = pl.BlockSpec(memory_space=pl.ANY)


def call(kernel, steps, ins, in_specs, outs, out_specs, scratch, flops, name):
    read = sum(x.size * x.dtype.itemsize for x in ins)
    return pl.pallas_call(
        kernel,
        out_shape=tuple(jax.ShapeDtypeStruct(s, d) for s, d in outs),
        grid_spec=pltpu.PrefetchScalarGridSpec(
            num_scalar_prefetch=1,
            grid=(steps,),
            in_specs=in_specs,
            out_specs=out_specs,
            scratch_shapes=scratch,
        ),
        compiler_params=pltpu.CompilerParams(vmem_limit_bytes=60 * MIB),
        cost_estimate=pl.CostEstimate(
            flops=flops, bytes_accessed=read, transcendentals=0
        ),
        name=name,
    )(*ins)


def lay(rows, seqs):
    rows = rows.reshape(seqs, LEN, -1)
    return jnp.concatenate(
        [
            jnp.pad(rows[:, :PATCHES], ((0, 0), (0, HEAD - PATCHES), (0, 0))),
            jnp.pad(rows[:, PATCHES:], ((0, 0), (0, TAIL - LEN + PATCHES), (0, 0))),
        ],
        1,
    ).reshape(seqs * SEQ, -1)


def unlay(rows, seqs):
    rows = rows.reshape(seqs, SEQ, -1)
    return jnp.concatenate(
        [rows[:, :PATCHES], rows[:, HEAD : HEAD + LEN - PATCHES]], 1
    ).reshape(seqs * LEN, -1)


def gather_expert(up, down, axes):
    part = up.shape[0]
    packed = jnp.concatenate(
        [up.reshape(part, 4, D).transpose(1, 0, 2).reshape(4 * part, D), down], 0
    )
    full = lax.all_gather(packed, axes, axis=0, tiled=True).reshape(-1, 8, part, D)
    return (
        full[:, :4].transpose(1, 0, 2, 3).reshape(4, D, D),
        full[:, 4:].reshape(FF, D),
    )


class Cube:
    axes = ("y", "x", "core", "z")
    swap = [(0, 1), (1, 0)]

    def __init__(self):
        y, x, core, z = (lax.axis_index(a) for a in self.axes)
        self.z, self.core, self.flat = z, core, y * 2 + x
        self.index = ((y * 2 + x) * 2 + core) * 4 + z

    def turn(self, block, k):
        return lax.ppermute(block, "z", [(i, (i + k) % 4) for i in range(4)])

    def plane(self, j, block):
        if j == 1:
            return lax.ppermute(block, "x", self.swap)
        if j == 2:
            return lax.ppermute(block, "y", self.swap)
        return lax.ppermute(block, ("y", "x"), [(i, 3 - i) for i in range(4)])

    def gather(self, block):
        ring = jnp.stack([block] + [self.turn(block, k) for k in (3, 2, 1)])
        ring = jnp.concatenate([ring, ring])
        own = lax.dynamic_slice_in_dim(ring, lax.rem(4 - self.z, 4), 4).reshape(
            4 * block.shape[0], -1
        )
        near = [own] + [self.plane(j, own) for j in (1, 2, 3)]
        return near + [lax.ppermute(b, "core", self.swap) for b in near]

    def scatter(self, keep, send, split, join):
        got = lax.ppermute(send, "core", self.swap)
        both = [keep[j].astype(F32) + got[j].astype(F32) for j in range(4)]
        more = [self.plane(j, both[j].astype(BF16)) for j in (1, 2, 3)]
        mine = both[0] + sum(m.astype(F32) for m in more)
        parts = split(mine)
        parts = lax.dynamic_slice_in_dim(jnp.concatenate([parts, parts]), self.z, 4)
        more = [self.turn(parts[k].astype(BF16), k) for k in (1, 2, 3)]
        return join(parts[0] + sum(m.astype(F32) for m in more))


class Flat:
    axes = ("dp", "fsdp")

    def __init__(self, sizes):
        self.flat = self.core = jnp.int32(0)
        self.index = lax.axis_index(self.axes)
        self.count = sizes

    def gather(self, block):
        full = lax.all_gather(block, self.axes, axis=0, tiled=True).reshape(8, 96, -1)
        return [full[b] for b in (0, 2, 4, 6, 1, 3, 5, 7)]

    def scatter(self, keep, send, split, join):
        blocks = jnp.stack([keep, send], 1).reshape((8,) + keep.shape[1:]).astype(F32)
        parts = jnp.stack([split(b, self.count // 8) for b in blocks])
        parts = parts.reshape((self.count,) + parts.shape[2:])
        mine = lax.psum_scatter(parts, self.axes, scatter_dimension=0, tiled=False)
        return join(mine)


def cut(fields, extra, block, ways=4):
    out, at = [], 0
    for groups, rows in fields:
        part = block[at : at + groups * rows].reshape(groups, ways, rows // ways, D)
        out.append(part.transpose(1, 0, 2, 3).reshape(ways, -1, D))
        at += groups * rows
    tail = block[at : at + extra]
    out.append(jnp.broadcast_to(tail[None], (ways,) + tail.shape))
    return jnp.concatenate(out, 1)


def layer(
    make,
    tokens,
    modality,
    token_mask,
    cotangent,
    mask_vector,
    ln_one_gain,
    ln_one_shift,
    w_qkv,
    w_out,
    ln_two_gain,
    ln_two_shift,
    w_up,
    w_down,
):
    net = make()
    part = w_qkv.shape[0]
    seqs = tokens.shape[0] // LEN
    rows = seqs * SEQ
    columns = jnp.stack([ln_one_gain, ln_one_shift, ln_two_gain, ln_two_shift], 1)
    packed = jnp.concatenate([w_qkv, w_out, jnp.pad(columns, ((0, 0), (0, 124)))], 1)
    pieces = net.gather(packed)
    up_text, down_text = gather_expert(w_up[1], w_down[1], net.axes)
    up_image, down_image = gather_expert(w_up[0], w_down[0], net.axes)

    masked = lay(token_mask, seqs)
    place = jnp.where(masked == 1, jnp.cumsum(masked, 0) - 1, -1).reshape(1, rows)
    blocks = jnp.maximum((jnp.sum(token_mask) + BLK - 1) // BLK, 1)
    near = [jnp.bitwise_xor(net.flat, j) * 2 for j in range(4)]
    where_ref = jnp.stack(
        [n + net.core for n in near]
        + [n + 1 - net.core for n in near]
        + [net.core, net.flat, blocks]
        + [modality[s * LEN] for s in range(seqs)]
    ).astype(jnp.int32)
    masked = masked.astype(F32)
    tokens = lay(tokens, seqs)
    cotangent = lay(cotangent, seqs)
    vector = mask_vector.astype(F32).reshape(1, D)
    n_columns = packed.shape[1]

    qkv, context, hidden, normed_one, normed_two, params = call(
        attention_kernel,
        seqs,
        (where_ref, tokens, masked, vector, *pieces),
        [by_step((SEQ, D)), by_step((SEQ, 1)), whole((1, D))] + [ANY] * 8,
        [
            ((rows, 3 * D), BF16),
            ((rows, D), BF16),
            ((rows, D), F32),
            ((rows, D), BF16),
            ((rows, D), BF16),
            ((8, D), F32),
        ],
        [
            by_step((SEQ, 3 * D)),
            by_step((SEQ, D)),
            by_step((SEQ, D)),
            by_step((SEQ, D)),
            by_step((SEQ, D)),
            pl.BlockSpec((8, D), lambda i, *_: (0, 0)),
        ],
        [pltpu.VMEM((D, n_columns), BF16), pltpu.SemaphoreType.DMA((8,))],
        rows * D * D * 8 + rows * SEQ * D * 8,
        "attention",
    )

    by_chunk = [
        pl.BlockSpec((1, D, D), lambda i, *_: (i, 0, 0)),
        pl.BlockSpec((D, D), lambda i, *_: (i, 0)),
    ]
    keep, send, grad_context, sums = call(
        feed_back_kernel,
        4,
        (where_ref, place, hidden, cotangent, context, params, up_text, down_text, *pieces),
        [whole((1, rows)), whole((rows, D)), whole((rows, D)), whole((rows, D)), whole((8, D))]
        + by_chunk
        + [ANY] * 8,
        [
            ((4, ROWS_ONE, D), BF16),
            ((4, ROWS_ONE, D), BF16),
            ((rows, D), BF16),
            ((8, D), F32),
        ],
        [ANY, ANY, whole((rows, D)), whole((8, D))],
        [pltpu.VMEM((rows, D), BF16)] * 5
        + [pltpu.VMEM((rows, D), F32)] * 2
        + [pltpu.VMEM((D, D), F32)] * 2
        + [
            pltpu.VMEM((D, D), BF16),
            pltpu.VMEM((2, 4, ROWS_ONE, D), BF16),
            pltpu.SemaphoreType.DMA((8,)),
            pltpu.SemaphoreType.DMA((2,)),
        ],
        BLK * D * FF * 12,
        "feed_back",
    )
    split_one = functools.partial(cut, [(4, 96), (1, 384), (1, 96)], 16)
    grads = net.scatter(keep, send, split_one, lambda v: v)
    grad_w_up = grads[: 4 * part].reshape(4, part, D).transpose(1, 0, 2).reshape(part, FF)
    grad_w_down = grads[4 * part : 8 * part]
    grad_w_out = grads[8 * part : 9 * part]
    extra_one = grads[9 * part :]

    keep, send, grad_tokens = call(
        attention_back_kernel,
        seqs,
        (where_ref, qkv, grad_context, normed_one, tokens, masked, vector, params, *pieces),
        [
            by_step((SEQ, 3 * D)),
            by_step((SEQ, D)),
            by_step((SEQ, D)),
            by_step((SEQ, D)),
            by_step((SEQ, 1)),
            whole((1, D)),
            whole((8, D)),
        ]
        + [ANY] * 8,
        [((4, ROWS_TWO, D), BF16), ((4, ROWS_TWO, D), BF16), ((rows, D), F32)],
        [ANY, ANY, by_step((SEQ, D))],
        [
            pltpu.VMEM((D, 3 * D), BF16),
            pltpu.VMEM((3, D, D), F32),
            pltpu.VMEM((8, D), F32),
            pltpu.VMEM((SEQ, 3 * D), BF16),
            pltpu.VMEM((2, 4, ROWS_TWO, D), BF16),
            pltpu.SemaphoreType.DMA((8,)),
            pltpu.SemaphoreType.DMA((2,)),
        ],
        rows * D * D * 12 + rows * SEQ * D * 20,
        "attention_back",
    )
    split_two = functools.partial(cut, [(3, 96)], 16)
    grads = net.scatter(keep, send, split_two, lambda v: v)
    grad_w_qkv = grads[: 3 * part].reshape(3, part, D).transpose(1, 0, 2).reshape(part, 3 * D)
    extra_two = grads[3 * part :]

    normed_two, hidden, _ = lax.optimization_barrier((normed_two, hidden, grad_tokens))
    after = hidden
    for text, up, down in ((True, up_text, down_text), (False, up_image, down_image)):
        (after,) = call(
            functools.partial(feed_kernel, text),
            4,
            (where_ref, normed_two, after, up, down),
            [whole((rows, D)), whole((rows, D))] + by_chunk,
            [((rows, D), F32 if text else BF16)],
            [whole((rows, D))],
            [pltpu.VMEM((rows, D), F32)]
            + ([pltpu.VMEM((seqs * TAIL, D), BF16)] if text else []),
            rows * D * FF * 2,
            "feed_text" if text else "feed_image",
        )
    output = unlay(after, seqs)

    def own(vector):
        return lax.dynamic_slice_in_dim(vector, net.index * part, part)

    return (
        output,
        unlay(grad_tokens, seqs),
        extra_one[2] + extra_two[2],
        own(extra_two[0]),
        own(extra_two[1]),
        grad_w_qkv,
        grad_w_out,
        own(extra_one[0]),
        own(extra_one[1]),
        grad_w_up,
        grad_w_down,
    )


def solution(mesh):
    if (mesh.shape["dp"], mesh.shape["fsdp"]) == (8, 4):
        mesh = Mesh(mesh.devices.reshape(2, 2, 2, 4), Cube.axes)
        make = Cube
    else:
        make = functools.partial(Flat, mesh.size)
    axes = Cube.axes if make is Cube else Flat.axes
    row, flat = P(axes, None), P(axes)
    middle = P(None, axes, None)
    in_specs = (row, flat, flat, row, P(), flat, flat, row, row, flat, flat, middle, middle)
    out_specs = (row, row, P(), flat, flat, row, row, flat, flat, row, row)
    return jax.shard_map(
        functools.partial(layer, make),
        mesh=mesh,
        in_specs=in_specs,
        out_specs=out_specs,
        check_vma=False,
    )
```

```python
import functools
import math

import jax
import jax.numpy as jnp
from jax import lax
from jax.experimental import pallas as pl
from jax.experimental.pallas import tpu as pltpu
from jax.sharding import Mesh, PartitionSpec as P

H = 12
HD = 64
LEN = 237
PATCHES = 197
HEAD = 208
TAIL = 48
SEQ = HEAD + TAIL
D = H * HD
FF = 4 * D
BLK = 256
EPS = 1e-05
F32 = jnp.float32
BF16 = jnp.bfloat16
MIB = 1 << 20
ROWS_FEED = 768
ROWS_OUT = 112
ROWS_QKV = 304


def dot(a, b):
    return jnp.dot(a, b, preferred_element_type=F32)


def dot_nt(a, b):
    return lax.dot_general(a, b, (((1,), (1,)), ((), ())), preferred_element_type=F32)


def dot_tn(a, b):
    return lax.dot_general(a, b, (((0,), (0,)), ((), ())), preferred_element_type=F32)


def mean(rows):
    return jnp.mean(rows, -1, keepdims=True)


def normalize(rows):
    centred = rows - mean(rows)
    inverse = lax.rsqrt(mean(centred * centred) + EPS)
    return centred * inverse, inverse


def normalize_back(grad, unit, inverse, gain):
    scaled = grad * gain
    return inverse * (scaled - mean(scaled) - unit * mean(scaled * unit))


def total(rows):
    return jnp.sum(rows, 0, keepdims=True)


def halves(pair):
    lane = lax.broadcasted_iota(jnp.int32, pair.shape, 1)
    zero = jnp.zeros_like(pair)
    return jnp.concatenate(
        [jnp.where(lane < HD, pair, zero), jnp.where(lane < HD, zero, pair)], 0
    )


def softmax_pair(queries, keys_cat):
    scores = dot_nt(queries, keys_cat)
    out = []
    for head in range(2):
        own = scores[:, head * SEQ : (head + 1) * SEQ]
        key = lax.broadcasted_iota(jnp.int32, own.shape, 1)
        valid = (key < PATCHES) | ((key >= HEAD) & (key < HEAD + LEN - PATCHES))
        own = jnp.where(valid, own, -1e30)
        peak = jnp.max(own, -1, keepdims=True)
        powers = jnp.exp(own - peak)
        out.append(powers / jnp.sum(powers, -1, keepdims=True))
    return jnp.concatenate(out, 1)


def spans(where_ref, pieces, rows):
    for side in range(2):
        for j in range(5):
            block = where_ref[4 * side + min(j, 3)]
            size = rows if j < 3 else rows // 2
            yield pieces[5 * side + j], block, (size if j == 4 else 0), size


def started(copies, sems, start=True):
    copies = [
        pltpu.make_async_copy(source, target, sems.at[j])
        for j, (source, target) in enumerate(copies)
    ]
    if start:
        for copy in copies:
            copy.start()
    return copies


def load_pieces(where_ref, pieces, target, sems, columns, start=True):
    return started(
        [
            (
                piece.at[:, pl.ds(columns[0], columns[1])],
                target.at[pl.ds(pl.multiple_of(block * 96 + first, 16), size), :],
            )
            for piece, block, first, size in spans(where_ref, pieces, 96)
        ],
        sems,
        start,
    )


def load_expert(where_ref, pieces, up, down, sems):
    copies = []
    for piece, block, first, size in spans(where_ref, pieces, 768):
        if first == 0:
            for chunk in range(4):
                copies.append(
                    (
                        piece.at[pl.ds(chunk * 96, 96), :],
                        up.at[chunk, pl.ds(pl.multiple_of(block * 96, 96), 96), :],
                    )
                )
        if first + size == 768:
            copies.append(
                (
                    piece.at[pl.ds(384 - first, 384), :],
                    down.at[pl.ds(pl.multiple_of(block * 384, 384), 384), :],
                )
            )
    return started(copies, sems)


def wait_all(copies):
    for copy in copies:
        copy.wait()


def attention_kernel(where_ref, tokens, masked, vector, *rest):
    pieces, rest = rest[:10], rest[10:]
    qkv, softs, context, hidden, normed_one, normed_two, params, weights, sems = rest

    @pl.when(pl.program_id(0) == 0)
    def _():
        wait_all(load_pieces(where_ref, pieces, weights, sems, (0, weights.shape[1])))
        columns = weights[:, 4 * D : 4 * D + 128].astype(F32)
        params[...] = jnp.transpose(columns)[:8]

    start = jnp.where(masked[...] == 1.0, vector[...], tokens[...].astype(F32))
    unit, _ = normalize(start)
    first = (unit * params[0:1] + params[1:2]).astype(BF16)
    normed_one[...] = first
    for third in range(3):
        at = pl.ds(third * D, D)
        qkv[:, at] = dot(first, weights[:, at]).astype(BF16)
    for pair in range(H // 2):
        queries = qkv[:, pl.ds(pair * 128, 128)] * BF16(1.0 / math.sqrt(HD))
        keys = halves(qkv[:, pl.ds(D + pair * 128, 128)])
        values = halves(qkv[:, pl.ds(2 * D + pair * 128, 128)])
        soft = softmax_pair(queries, keys)
        softs[0, pair] = soft
        attention = soft.astype(BF16)
        context[:, pl.ds(pair * 128, 128)] = dot(attention, values).astype(BF16)
    after = start + dot(context[...], weights[:, pl.ds(3 * D, D)])
    hidden[...] = after
    unit, _ = normalize(after)
    normed_two[...] = (unit * params[2:3] + params[3:4]).astype(BF16)


def chosen(place, block):
    row = lax.broadcasted_iota(jnp.int32, (BLK, place.shape[1]), 0) + block * BLK
    return jnp.where(row == place[...], 1.0, 0.0).astype(BF16)


def rows_of(block):
    return pl.ds(pl.multiple_of(block * BLK, BLK), BLK)


def feed_back_kernel(where_ref, place, hidden, cotangent, context, params, *rest):
    pieces, rest = rest[:10], rest[10:]
    keep, send, send_far, *kept = rest[:7]
    (high, low, rows_two, *rows_kept) = rest[7:14]
    rows_hidden, rows_cot, rows_context, grad_two = rows_kept
    (sum_up, sum_down, w_up, w_down, stage, sems, out_sems, kept_sems) = rest[14:]
    step = pl.program_id(0)
    blocks = where_ref[10]
    core = where_ref[8]

    def keeping(block):
        return [
            pltpu.make_async_copy(a.at[rows_of(block), :], b.at[rows_of(block), :], kept_sems.at[j])
            for j, (a, b) in enumerate(zip(rows_kept, kept, strict=True))
        ]

    @pl.when(step == 0)
    def _():
        copies = load_expert(where_ref, pieces, w_up, w_down, sems)
        high[...] = hidden[...].astype(BF16)
        low[...] = (hidden[...] - high[...].astype(F32)).astype(BF16)

        def gather(block, _):
            pick, at = chosen(place, block), rows_of(block)
            rows = dot(pick, high[...]) + dot(pick, low[...])
            rows_hidden[at, :] = rows
            rows_cot[at, :] = dot(pick, cotangent[...]).astype(BF16)
            rows_context[at, :] = dot(pick, context[...]).astype(BF16)
            unit, _ = normalize(rows)
            rows_two[at, :] = (unit * params[2:3] + params[3:4]).astype(BF16)
            grad_two[at, :] = jnp.zeros((BLK, D), F32)
            return 0

        lax.fori_loop(0, blocks, gather, 0)
        wait_all(copies)

    up = w_up.at[step]
    down = w_down.at[pl.ds(pl.multiple_of(step * D, D), D), :]

    def expert(block, _):
        at = rows_of(block)
        rows, grads = rows_two[at, :], rows_cot[at, :]
        pre = dot(rows, up[...])
        chance = 0.5 * (1.0 + lax.erf(pre * math.sqrt(0.5)))
        activated = (pre * chance).astype(BF16)
        slope = chance + pre * (jnp.exp(-0.5 * pre * pre) * (1.0 / math.sqrt(2.0 * math.pi)))
        grad_pre = (dot_nt(grads, down[...]) * slope).astype(BF16)
        grad_two[at, :] += dot_nt(grad_pre, up[...])
        add_down = dot_tn(activated, grads)
        add_up = dot_tn(rows, grad_pre)

        @pl.when(block == 0)
        def _():
            sum_down[...] = add_down
            sum_up[...] = add_up

        @pl.when(block > 0)
        def _():
            sum_down[...] += add_down
            sum_up[...] += add_up

        return 0

    lax.fori_loop(0, blocks, expert, 0)

    def leaving(at_step):
        rows = pl.ds(pl.multiple_of(at_step * 96, 96), 96)
        columns = pl.ds(384, 384)
        mine = jnp.bitwise_xor(at_step, where_ref[9])
        near = jnp.minimum(mine, 2)
        sem = out_sems.at[at_step]
        return [
            (None, stage.at[0, :, rows, :], keep.at[:, rows, :], sem.at[0]),
            (None, stage.at[0, mine, columns, :], keep.at[mine, columns, :], sem.at[1]),
            (None, stage.at[1, pl.ds(0, 3), rows, :], send.at[:, rows, :], sem.at[2]),
            (None, stage.at[1, 3, rows, :], send_far.at[rows, :], sem.at[3]),
            (mine < 3, stage.at[1, near, columns, :], send.at[near, columns, :], sem.at[4]),
            (mine == 3, stage.at[1, 3, columns, :], send_far.at[columns, :], sem.at[4]),
        ]

    def each(copies, act):
        for when, source, target, sem in copies:
            copy = pltpu.make_async_copy(source, target, sem)
            if when is None:
                act(copy)
            else:
                pl.when(when)(functools.partial(act, copy))

    up_at = pl.ds(pl.multiple_of(step * 96, 96), 96)
    mine = jnp.bitwise_xor(step, where_ref[9])
    for side in range(2):
        for j in range(4):
            source = pl.ds(pl.multiple_of(where_ref[4 * side + j] * 96, 96), 96)
            stage[side, j, up_at, :] = sum_up[source, :].astype(BF16)
        half = core if side == 0 else 1 - core
        source = pl.ds(pl.multiple_of(half * 384, 384), 384)
        stage[side, mine, pl.ds(384, 384), :] = sum_down[source, :].astype(BF16)
    each(leaving(step), lambda copy: copy.start())

    @pl.when(step == pl.num_programs(0) - 1)
    def _():
        def start(block, _):
            for copy in keeping(block):
                copy.start()
            return 0

        def wait(block, _):
            for copy in keeping(block):
                copy.wait()
            return 0

        def both(block, _):
            start(block, 0)
            return wait(block, 0)

        lax.fori_loop(0, blocks, both, 0)
        for at_step in range(4):
            each(leaving(at_step), lambda copy: copy.wait())


def hidden_back_kernel(where_ref, place, params, *rest):
    kept, pieces, rest = rest[:4], rest[4:14], rest[14:]
    keep, send, grad_context = rest[:3]
    rows_hidden, rows_cot, rows_context, grad_two, w_out, sum_out, sums, sems, kept_sems = rest[3:]
    blocks = where_ref[10]
    copies = load_pieces(where_ref, pieces, w_out, sems, (3 * D, D))
    grad_context[...] = jnp.zeros_like(grad_context)
    sums[...] = jnp.zeros_like(sums)
    sum_out[...] = jnp.zeros_like(sum_out)
    wait_all(copies)

    def back(block, _):
        got = started(
            [
                (a.at[rows_of(block), :], b)
                for a, b in zip(
                    kept, (rows_hidden, rows_cot, rows_context, grad_two), strict=True
                )
            ],
            kept_sems,
        )
        pick = chosen(place, block)
        wait_all(got)
        unit, inverse = normalize(rows_hidden[...])
        grad = grad_two[...]
        grad_hidden = rows_cot[...].astype(F32) + normalize_back(
            grad, unit, inverse, params[2:3]
        )
        sums[0:1] += total(grad * unit)
        sums[1:2] += total(grad)
        sums[2:3] += total(grad_hidden)
        grad_attn = grad_hidden.astype(BF16)
        sum_out[...] += dot_tn(rows_context[...], grad_attn)
        rows = dot_nt(grad_attn, w_out[...]).astype(BF16)
        grad_context[...] += dot_tn(pick, rows).astype(BF16)
        return 0

    lax.fori_loop(0, blocks, back, 0)
    extra = jnp.concatenate([sums[...], jnp.zeros_like(sums[...])], 0).astype(BF16)
    for side, out in enumerate((keep, send)):
        for j in range(4):
            source = pl.ds(pl.multiple_of(where_ref[4 * side + j] * 96, 96), 96)
            out[j, pl.ds(0, 96), :] = sum_out[source, :].astype(BF16)
            out[j, pl.ds(96, 16), :] = extra


def put_rows(target, rows, seq):
    target[seq * LEN : seq * LEN + PATCHES] = rows[:PATCHES]
    target[seq * LEN + PATCHES : (seq + 1) * LEN] = rows[HEAD : HEAD + LEN - PATCHES]


def attention_back_kernel(
    where_ref, qkv, softs, grad_context, normed_one, tokens, masked, vector, params, *rest
):
    pieces = rest[:10]
    keep, send, grad_tokens = rest[10:13]
    weights, sums, grad_qkv, stage, sems, out_sems = rest[13:]
    step = pl.program_id(0)
    here = pl.ds(pl.multiple_of(step * SEQ, SEQ), SEQ)

    def copies():
        return load_pieces(where_ref, pieces, weights, sems, (0, 3 * D), False)

    @pl.when(step == 0)
    def _():
        for copy in copies():
            copy.start()
        sums[...] = jnp.zeros_like(sums)

    inv_root = 1.0 / math.sqrt(HD)
    top = lax.broadcasted_iota(jnp.int32, (128, SEQ), 0) < HD
    for pair in range(H // 2):
        queries = qkv[:, pl.ds(pair * 128, 128)]
        keys = halves(qkv[:, pl.ds(D + pair * 128, 128)])
        values = halves(qkv[:, pl.ds(2 * D + pair * 128, 128)])
        grads = grad_context[:, pl.ds(pair * 128, 128)]
        grad_soft = dot_nt(grads, values)
        parts = []
        for head in range(2):
            span = slice(head * SEQ, (head + 1) * SEQ)
            own, grad = softs[0, pair, :, span], grad_soft[:, span]
            parts.append(own * (grad - jnp.sum(own * grad, -1, keepdims=True)))
        grad_scores = jnp.concatenate(parts, 1).astype(BF16)
        grad_qkv[here, pl.ds(pair * 128, 128)] = (dot(grad_scores, keys) * inv_root).astype(BF16)
        by_key = dot_tn(queries, grad_scores) * inv_root
        by_key = jnp.where(top, by_key[:, :SEQ], by_key[:, SEQ:])
        grad_qkv[here, pl.ds(D + pair * 128, 128)] = jnp.transpose(by_key).astype(BF16)
        by_value = dot_tn(grads, softs[0, pair].astype(BF16))
        by_value = jnp.where(top, by_value[:, :SEQ], by_value[:, SEQ:])
        grad_qkv[here, pl.ds(2 * D + pair * 128, 128)] = jnp.transpose(by_value).astype(BF16)

    @pl.when(step == 0)
    def _():
        wait_all(copies())

    grad_one = dot_nt(grad_qkv[here, :], weights[...])
    start = jnp.where(masked[...] == 1.0, vector[...], tokens[...].astype(F32))
    unit, inverse = normalize(start)
    grad_start = normalize_back(grad_one, unit, inverse, params[0:1])
    sums[0:1] += total(grad_one * unit)
    sums[1:2] += total(grad_one)
    sums[2:3] += total(jnp.where(masked[...] == 1.0, grad_start, 0.0))
    kept = jnp.where(masked[...] == 1.0, 0.0, grad_start)
    for seq in range(normed_one.shape[0] // SEQ):
        pl.when(step == seq)(functools.partial(put_rows, grad_tokens, kept, seq))

    @pl.when(step == pl.num_programs(0) - 1)
    def _():
        extra = jnp.concatenate([sums[...], jnp.zeros_like(sums[...])], 0).astype(BF16)
        for third in range(3):
            for part in range(3):
                at = pl.ds(third * D + part * SEQ, SEQ)
                add = dot_tn(normed_one[...], grad_qkv[:, at]).astype(BF16)
                for block in range(8):
                    stage[block, pl.ds(third * 96, 96), pl.ds(part * SEQ, SEQ)] = add[
                        block * 96 : (block + 1) * 96
                    ]
        out_copies = []
        for side, out in enumerate((keep, send)):
            for j in range(4):
                block = where_ref[4 * side + j]
                stage[block, pl.ds(3 * 96, 16), :] = extra
                out_copies.append((stage.at[block], out.at[j]))
        wait_all(started(out_copies, out_sems))


def gelu(pre):
    return (pre * (0.5 * (1.0 + lax.erf(pre * math.sqrt(0.5))))).astype(BF16)


def feed_kernel(text, where_ref, rows_in, before, *rest):
    pieces, (out, sums, w_up, w_down, sems, *tails) = rest[:10], rest[10:]
    tails = flat = tails[0]
    step = pl.program_id(0)
    seqs = rows_in.shape[0] // SEQ

    @pl.when(step == 0)
    def _():
        copies = load_expert(where_ref, pieces, w_up, w_down, sems)
        sums[...] = before[...]
        if text:
            for seq in range(seqs):
                tails[pl.ds(seq * TAIL, TAIL), :] = rows_in[pl.ds(seq * SEQ + HEAD, TAIL), :]
        wait_all(copies)

    up = w_up.at[step]
    down = w_down.at[pl.ds(pl.multiple_of(step * D, D), D), :]
    for seq in range(seqs):
        head = pl.ds(seq * SEQ, HEAD)

        @pl.when(where_ref[11 + seq] == int(text))
        def _():
            activated = gelu(dot(rows_in[head, :], up[...]))
            sums[head, :] += dot(activated, down[...])

    if text:
        more = dot(gelu(dot(tails[...], up[...])), down[...])
        for seq in range(seqs):
            sums[pl.ds(seq * SEQ + HEAD, TAIL), :] += more[seq * TAIL : (seq + 1) * TAIL]

    @pl.when(step == pl.num_programs(0) - 1)
    def _():
        if text:
            out[...] = sums[...]
        else:
            for seq in range(seqs):
                put_rows(flat, sums[pl.ds(seq * SEQ, SEQ), :], seq)
            out[...] = flat[...].astype(BF16)


def whole(shape):
    return pl.BlockSpec(shape, lambda *_: (0,) * len(shape), pipeline_mode=pl.Buffered(1))


def by_step(shape):
    return pl.BlockSpec(shape, lambda i, *_: (i,) + (0,) * (len(shape) - 1))


ANY = pl.BlockSpec(memory_space=pl.ANY)


def call(kernel, steps, ins, in_specs, outs, out_specs, scratch, name):
    run = pl.pallas_call(
        kernel,
        out_shape=tuple(jax.ShapeDtypeStruct(s, d) for s, d in outs),
        grid_spec=pltpu.PrefetchScalarGridSpec(
            num_scalar_prefetch=1,
            grid=(steps,),
            in_specs=in_specs,
            out_specs=out_specs,
            scratch_shapes=scratch,
        ),
        compiler_params=pltpu.CompilerParams(vmem_limit_bytes=60 * MIB),
        cost_estimate=pl.CostEstimate(flops=1, bytes_accessed=1, transcendentals=0),
        name=name,
    )
    return run(*ins)


def lay(rows, seqs):
    rows = rows.reshape(seqs, LEN, -1)
    return jnp.concatenate(
        [
            jnp.pad(rows[:, :PATCHES], ((0, 0), (0, HEAD - PATCHES), (0, 0))),
            jnp.pad(rows[:, PATCHES:], ((0, 0), (0, TAIL - LEN + PATCHES), (0, 0))),
        ],
        1,
    ).reshape(seqs * SEQ, -1)


def tie(*trees):
    return lax.optimization_barrier(trees)


def in_order(rows, part, blocks=0, axis=0):
    rows = jnp.moveaxis(rows, axis, blocks)
    shape, columns = rows.shape[:blocks], rows.shape[-1]
    count, size = rows.shape[blocks], rows.shape[blocks + 1]
    if size == part:
        return rows.reshape(*shape, count * part, columns)
    up = rows[..., : 4 * part, :].reshape(*shape, count, 4, part, columns)
    up = jnp.swapaxes(up, blocks, blocks + 1).reshape(*shape, 4 * count * part, columns)
    down = rows[..., 4 * part :, :].reshape(*shape, count * (size - 4 * part), columns)
    return jnp.concatenate([up, down], -2)


class Cube:
    axes = ("y", "x", "core", "z")
    swap = [(0, 1), (1, 0)]

    def __init__(self):
        y, x, core, z = (lax.axis_index(a) for a in self.axes)
        self.z, self.core, self.flat = z, core, y * 2 + x
        self.index = ((y * 2 + x) * 2 + core) * 4 + z

    def turn(self, block, k):
        return lax.ppermute(block, "z", [(i, (i + k) % 4) for i in range(4)])

    def turns(self, block):
        return [block] + [self.turn(block, k) for k in (1, 2, 3)]

    def ring(self, ring, part):
        out = []
        for place in range(4):
            k = lax.rem(self.z + 4 - place, 4)
            out.append(
                jnp.where(
                    k == 0,
                    ring[0],
                    jnp.where(k == 1, ring[1], jnp.where(k == 2, ring[2], ring[3])),
                )
            )
        return in_order(jnp.stack(out), part)

    def swapped(self, block, axis):
        return lax.ppermute(block, axis, self.swap)

    def sides(self, own):
        return own, self.swapped(own, "x"), self.swapped(own, "y")

    def halves(self, near):
        half = near[0].shape[0] // 2
        return near[1][:half], near[2][half:]

    def to_corners(self, near, halves):
        return (*near, self.swapped(halves[0], "y"), self.swapped(halves[1], "x"))

    def corner(self, near):
        return self.to_corners(near, self.halves(near))

    def cores(self, near):
        return [*near] + [self.swapped(b, "core") for b in near]

    def plane(self, j, block):
        if j == 1:
            return self.swapped(block, "x")
        if j == 2:
            return self.swapped(block, "y")
        return lax.ppermute(block, ("y", "x"), [(i, 3 - i) for i in range(4)])

    def to_core(self, block):
        return self.swapped(block, "core")

    def far_sums(self, keep, got):
        return (keep[3].astype(F32) + got.astype(F32)).astype(BF16)

    def to_corner(self, both):
        half = both.shape[0] // 2
        return self.swapped(both[:half], "x"), self.swapped(both[half:], "y")

    def side_sums(self, keep, got, corner, *out):
        half = corner[0].shape[0]
        by_x = jnp.pad(corner[0], ((0, half), (0, 0))).astype(F32)
        by_y = jnp.pad(corner[1], ((half, 0), (0, 0))).astype(F32)
        to_x = keep[1].astype(F32) + got[1].astype(F32) + by_y
        to_y = keep[2].astype(F32) + got[2].astype(F32) + by_x
        sums = self.plane_sums(*out)
        to_x = jnp.concatenate([to_x.astype(BF16), sums[2]])
        to_y = jnp.concatenate([to_y.astype(BF16), sums[3]])
        return [keep, got, to_x, to_y, *out, sums[4]]

    def to_sides(self, sums):
        return [
            *sums[:2],
            self.swapped(sums[2], "x"),
            self.swapped(sums[3], "y"),
            *sums[4:6],
            self.plane(3, sums[6]),
        ]

    def side_groups(self, sums):
        keep, got, by_x, by_y, keep_out, got_out, by_plane = sums
        rows = keep.shape[1]
        return (
            [keep, got, by_x[:rows], by_y[:rows]],
            [keep_out, got_out, by_x[rows:], by_y[rows:], by_plane],
        )

    def plane_sums(self, keep, got):
        both = [keep[j].astype(F32) + got[j].astype(F32) for j in (1, 2, 3)]
        return [keep, got] + [b.astype(BF16) for b in both]

    def to_plane(self, sums):
        return sums[:2] + [self.plane(j, sums[j + 1]) for j in (1, 2, 3)]

    def ring_sums(self, groups, split):
        mine = [sum(m.astype(F32) for m in (g[0][0], g[1][0], *g[2:])) for g in groups]
        parts = split(jnp.concatenate(mine) if len(mine) > 1 else mine[0])
        parts = lax.dynamic_slice_in_dim(jnp.concatenate([parts, parts]), self.z, 4)
        return [parts[0]] + [parts[k].astype(BF16) for k in (1, 2, 3)]

    def to_ring(self, parts, which):
        return [self.turn(p, k) if k in which else p for k, p in enumerate(parts)]

    def add_ring(self, ring):
        return ring[0] + sum(m.astype(F32) for m in ring[1:])


class Flat:
    axes = ("dp", "fsdp")

    def __init__(self, count):
        self.flat = self.core = jnp.int32(0)
        self.index = lax.axis_index(self.axes)
        self.count = count

    def turns(self, block):
        return lax.all_gather(block, self.axes, axis=0)

    def ring(self, full, part):
        return in_order(full.reshape((8, -1) + full.shape[1:]), part, 1, 1)

    def sides(self, own):
        return own

    def halves(self, near):
        return ()

    def to_corners(self, near, halves):
        return near

    def corner(self, near):
        return near

    def cores(self, near):
        half = near.shape[1] // 2
        out = []
        for side in range(2):
            out += [near[side], near[2 + side], near[4 + side]]
            out += [near[6 + side, :half], near[6 + side, half:]]
        return out

    def to_core(self, block):
        return block

    def far_sums(self, keep, got):
        return got

    def to_corner(self, both):
        return both

    def side_sums(self, keep, got, corner, *out):
        got = jnp.concatenate([got, corner[None]])
        return self.plane_sums(keep, got) + self.plane_sums(*out)

    def to_sides(self, sums):
        return sums

    def side_groups(self, sums):
        return [sums[:1], sums[1:]]

    def plane_sums(self, keep, got):
        return [jnp.stack([keep, got], 1).reshape((8,) + keep.shape[1:])]

    def to_plane(self, sums):
        return sums

    def ring_sums(self, groups, split):
        blocks = jnp.concatenate([g[0] for g in groups], 1).astype(F32)
        parts = jnp.stack([split(b, self.count // 8) for b in blocks])
        return [parts.reshape((self.count,) + parts.shape[2:])]

    def to_ring(self, parts, which):
        if 3 not in which:
            return parts
        return [lax.psum_scatter(parts[0], self.axes, scatter_dimension=0, tiled=False)]

    def add_ring(self, ring):
        return ring[0]


def pack_expert(up, down):
    part = up.shape[0]
    up = up.reshape(part, 4, D).transpose(1, 0, 2).reshape(4 * part, D)
    return jnp.concatenate([up, down], 0)


def cut(fields, extra, block, ways=4):
    out, at = [], 0
    for groups, rows in fields:
        part = block[at : at + groups * rows].reshape(groups, ways, rows // ways, D)
        out.append(part.transpose(1, 0, 2, 3).reshape(ways, -1, D))
        at += groups * rows
    tail = block[at : at + extra]
    out.append(jnp.broadcast_to(tail[None], (ways,) + tail.shape))
    return jnp.concatenate(out, 1)


def layer(
    make,
    tokens,
    modality,
    token_mask,
    cotangent,
    mask_vector,
    ln_one_gain,
    ln_one_shift,
    w_qkv,
    w_out,
    ln_two_gain,
    ln_two_shift,
    w_up,
    w_down,
):
    net = make()
    part = w_qkv.shape[0]
    seqs = tokens.shape[0] // LEN
    rows = seqs * SEQ
    columns = jnp.stack([ln_one_gain, ln_one_shift, ln_two_gain, ln_two_shift], 1)
    packed = jnp.concatenate([w_qkv, w_out, jnp.pad(columns, ((0, 0), (0, 124)))], 1)
    n_columns = packed.shape[1]
    ring = net.turns(packed)

    seq_masks = token_mask.reshape(seqs, LEN)
    masked = jnp.concatenate(
        [
            jnp.pad(seq_masks[:, :PATCHES], ((0, 0), (0, HEAD - PATCHES))),
            jnp.pad(seq_masks[:, PATCHES:], ((0, 0), (0, TAIL - LEN + PATCHES))),
        ],
        1,
    ).reshape(1, rows)
    order = jnp.cumsum(masked, 1)
    place = jnp.where(masked == 1, order - 1, -1)
    blocks = jnp.maximum((order[0, rows - 1] + BLK - 1) // BLK, 1)
    near = jnp.arange(8, dtype=jnp.int32)
    near = jnp.bitwise_xor(net.flat, near & 3) * 2 + jnp.bitwise_xor(net.core, near >> 2)
    where_ref = jnp.concatenate(
        [
            near,
            jnp.stack([net.core, net.flat, blocks]).astype(jnp.int32),
            modality.reshape(seqs, LEN)[:, 0],
        ]
    )
    tokens = lay(tokens, seqs)
    ring, where_ref, tokens = tie(ring, where_ref, tokens)

    own = net.ring(ring, part)
    near = net.sides(own)
    text, _ = tie(pack_expert(w_up[1], w_down[1]), own)
    ring_text = net.turns(text)
    masked = masked.astype(F32).reshape(rows, 1)
    cotangent = lay(cotangent, seqs)
    vector = mask_vector.astype(F32).reshape(1, D)
    near, masked, place, cotangent, vector = tie(near, masked, place, cotangent, vector)
    pieces = net.cores(net.corner(near))
    own_text = net.ring(ring_text, part)
    pieces, own_text, image = tie(pieces, own_text, pack_expert(w_up[0], w_down[0]))
    near_text = net.sides(own_text)
    image = net.turns(image)

    qkv, softs, context, hidden, normed_one, normed_two, params = call(
        attention_kernel,
        seqs,
        (where_ref, tokens, masked, vector, *pieces),
        [by_step((SEQ, D)), by_step((SEQ, 1)), whole((1, D))] + [ANY] * 10,
        [
            ((rows, 3 * D), BF16),
            ((seqs, H // 2, SEQ, 2 * SEQ), F32),
            ((rows, D), BF16),
            ((rows, D), F32),
            ((rows, D), BF16),
            ((rows, D), BF16),
            ((8, D), F32),
        ],
        [
            by_step((SEQ, 3 * D)),
            by_step((1, H // 2, SEQ, 2 * SEQ)),
            by_step((SEQ, D)),
            by_step((SEQ, D)),
            by_step((SEQ, D)),
            by_step((SEQ, D)),
            pl.BlockSpec((8, D), lambda i, *_: (0, 0)),
        ],
        [pltpu.VMEM((D, n_columns), BF16), pltpu.SemaphoreType.DMA((10,))],
        "attention",
    )

    near_text, image, (qkv, softs, context, hidden, normed_one, normed_two, params) = tie(
        near_text, image, (qkv, softs, context, hidden, normed_one, normed_two, params)
    )
    pieces_text = net.cores(net.corner(near_text))
    image, pieces_text = tie(net.ring(image, part), pieces_text)
    near_image = net.sides(image)

    feed_block = (ROWS_FEED, D)
    keep, send, send_far, *kept = call(
        feed_back_kernel,
        4,
        (where_ref, place, hidden, cotangent, context, params, *pieces_text),
        [whole((1, rows)), whole((rows, D)), whole((rows, D)), whole((rows, D)), whole((8, D))]
        + [ANY] * 10,
        [((4, *feed_block), BF16), ((3, *feed_block), BF16), (feed_block, BF16)]
        + [((rows, D), F32), ((rows, D), BF16), ((rows, D), BF16), ((rows, D), F32)],
        [ANY] * 7,
        [pltpu.VMEM((rows, D), BF16)] * 3
        + [
            pltpu.VMEM((rows, D), F32),
            pltpu.VMEM((rows, D), BF16),
            pltpu.VMEM((rows, D), BF16),
            pltpu.VMEM((rows, D), F32),
        ]
        + [pltpu.VMEM((D, D), F32)] * 2
        + [
            pltpu.VMEM((4, D, D), BF16),
            pltpu.VMEM((FF, D), BF16),
            pltpu.VMEM((2, 4, *feed_block), BF16),
            pltpu.SemaphoreType.DMA((40,)),
            pltpu.SemaphoreType.DMA((4, 5)),
            pltpu.SemaphoreType.DMA((4,)),
        ],
        "feed_back",
    )
    near_image, keep, send, send_far, kept = tie(near_image, keep, send, send_far, kept)
    far = net.far_sums(keep, net.to_core(send_far))
    kept, far, send = tie(kept, far, send)
    got = net.to_core(send)
    corner = net.to_corner(far)
    keep_out, send_out, grad_context = call(
        hidden_back_kernel,
        1,
        (where_ref, place, params, *kept, *pieces),
        [whole((1, rows)), whole((8, D))] + [ANY] * 14,
        [((4, ROWS_OUT, D), BF16)] * 2 + [((rows, D), BF16)],
        [whole((4, ROWS_OUT, D))] * 2 + [whole((rows, D))],
        [
            pltpu.VMEM((BLK, D), F32),
            pltpu.VMEM((BLK, D), BF16),
            pltpu.VMEM((BLK, D), BF16),
            pltpu.VMEM((BLK, D), F32),
            pltpu.VMEM((D, D), BF16),
            pltpu.VMEM((D, D), F32),
            pltpu.VMEM((8, D), F32),
            pltpu.SemaphoreType.DMA((10,)),
            pltpu.SemaphoreType.DMA((4,)),
        ],
        "hidden_back",
    )
    corner, got, keep_out, send_out, grad_context = tie(
        corner, got, keep_out, send_out, grad_context
    )
    got_out = net.to_core(send_out)
    sums_feed = net.side_sums(keep, got, corner, keep_out, got_out)
    halves_image = net.halves(near_image)
    sums_feed, grad_context, halves_image = tie(sums_feed, grad_context, halves_image)
    sums_feed = net.to_sides(sums_feed)
    near_image = net.to_corners(near_image, halves_image)

    keep, send, grad_tokens = call(
        attention_back_kernel,
        seqs,
        (where_ref, qkv, softs, grad_context, normed_one, tokens, masked, vector, params, *pieces),
        [
            by_step((SEQ, 3 * D)),
            by_step((1, H // 2, SEQ, 2 * SEQ)),
            by_step((SEQ, D)),
            whole((rows, D)),
            by_step((SEQ, D)),
            by_step((SEQ, 1)),
            whole((1, D)),
            whole((8, D)),
        ]
        + [ANY] * 10,
        [((4, ROWS_QKV, D), BF16), ((4, ROWS_QKV, D), BF16), ((seqs * LEN, D), F32)],
        [ANY, ANY, whole((seqs * LEN, D))],
        [
            pltpu.VMEM((D, 3 * D), BF16),
            pltpu.VMEM((8, D), F32),
            pltpu.VMEM((rows, 3 * D), BF16),
            pltpu.VMEM((8, ROWS_QKV, D), BF16),
            pltpu.SemaphoreType.DMA((10,)),
            pltpu.SemaphoreType.DMA((8,)),
        ],
        "attention_back",
    )
    keep, send, grad_tokens, sums_feed, near_image = tie(
        keep, send, grad_tokens, sums_feed, near_image
    )
    got = net.to_core(send)
    near_image, got = tie(near_image, got)
    pieces_image = net.cores(near_image)
    sums_qkv = net.plane_sums(keep, got)
    ring_one = net.ring_sums(
        net.side_groups(sums_feed), functools.partial(cut, [(4, 96), (1, 384), (1, 96)], 16)
    )
    sums_qkv, ring_one, normed_two, after, pieces_image = tie(
        sums_qkv, ring_one, normed_two, hidden, pieces_image
    )
    sums_qkv = net.to_plane(sums_qkv)
    ring_one = net.to_ring(ring_one, (1, 2))
    for text in (True, False):
        weights = pieces_text if text else pieces_image
        (after,) = call(
            functools.partial(feed_kernel, text),
            4,
            (where_ref, normed_two, after, *weights),
            [whole((rows, D)), whole((rows, D))] + [ANY] * len(weights),
            [((rows, D), F32) if text else ((seqs * LEN, D), BF16)],
            [whole((rows if text else seqs * LEN, D))],
            [
                pltpu.VMEM((rows, D), F32),
                pltpu.VMEM((4, D, D), BF16),
                pltpu.VMEM((FF, D), BF16),
                pltpu.SemaphoreType.DMA((40,)),
                pltpu.VMEM((seqs * TAIL, D), BF16) if text else pltpu.VMEM((seqs * LEN, D), F32),
            ],
            "feed_text" if text else "feed_image",
        )
        if text:
            sums_qkv, ring_one, after = tie(sums_qkv, ring_one, after)
            ring_two = net.ring_sums([sums_qkv], functools.partial(cut, [(3, 96)], 16))
            ring_two, after = tie(ring_two, after)
            ring_two = net.to_ring(ring_two, (1, 2, 3))
            ring_one = net.to_ring(ring_one, (3,))

    ring_two, after = tie(ring_two, after)
    grads = net.add_ring(ring_one)
    grad_w_up = grads[: 4 * part].reshape(4, part, D).transpose(1, 0, 2).reshape(part, FF)
    grad_w_down = grads[4 * part : 8 * part]
    grad_w_out = grads[8 * part : 9 * part]
    extra_one = grads[9 * part :]
    grads = net.add_ring(ring_two)
    grad_w_qkv = grads[: 3 * part].reshape(3, part, D).transpose(1, 0, 2).reshape(part, 3 * D)
    extra_two = grads[3 * part :]

    def own(vector):
        return lax.dynamic_slice_in_dim(vector, net.index * part, part)

    return (
        after,
        grad_tokens,
        extra_one[2] + extra_two[2],
        own(extra_two[0]),
        own(extra_two[1]),
        grad_w_qkv,
        grad_w_out,
        own(extra_one[0]),
        own(extra_one[1]),
        grad_w_up,
        grad_w_down,
    )


def solution(mesh):
    if (mesh.shape["dp"], mesh.shape["fsdp"]) == (8, 4):
        mesh = Mesh(mesh.devices.reshape(2, 2, 2, 4), Cube.axes)
        make = Cube
    else:
        make = functools.partial(Flat, mesh.size)
    axes = Cube.axes if make is Cube else Flat.axes
    row, flat = P(axes, None), P(axes)
    middle = P(None, axes, None)
    in_specs = (row, flat, flat, row, P(), flat, flat, row, row, flat, flat, middle, middle)
    out_specs = (row, row, P(), flat, flat, row, row, flat, flat, row, row)
    return jax.shard_map(
        functools.partial(layer, make),
        mesh=mesh,
        in_specs=in_specs,
        out_specs=out_specs,
        check_vma=False,
    )
```

```python
import functools
import math

import jax
import jax.numpy as jnp
from jax import lax
from jax.experimental import pallas as pl
from jax.experimental.pallas import tpu as pltpu
from jax.sharding import Mesh, PartitionSpec as P

H = 12
HD = 64
LEN = 237
PATCHES = 197
HEAD = 208
TAIL = 48
SEQ = HEAD + TAIL
D = H * HD
FF = 4 * D
BLK = 256
EPS = 1e-05
F32 = jnp.float32
BF16 = jnp.bfloat16
MIB = 1 << 20
ROWS_ONE = 880
ROWS_QKV = 304


def dot(a, b):
    return jnp.dot(a, b, preferred_element_type=F32)


def dot_nt(a, b):
    return lax.dot_general(a, b, (((1,), (1,)), ((), ())), preferred_element_type=F32)


def dot_tn(a, b):
    return lax.dot_general(a, b, (((0,), (0,)), ((), ())), preferred_element_type=F32)


def mean(rows):
    return jnp.mean(rows, -1, keepdims=True)


def normalize(rows):
    centred = rows - mean(rows)
    inverse = lax.rsqrt(mean(centred * centred) + EPS)
    return centred * inverse, inverse


def normalize_back(grad, unit, inverse, gain):
    scaled = grad * gain
    return inverse * (scaled - mean(scaled) - unit * mean(scaled * unit))


def total(rows):
    return jnp.sum(rows, 0, keepdims=True)


def halves(pair):
    lane = lax.broadcasted_iota(jnp.int32, pair.shape, 1)
    zero = jnp.zeros_like(pair)
    return jnp.concatenate(
        [jnp.where(lane < HD, pair, zero), jnp.where(lane < HD, zero, pair)], 0
    )


def key_bias():
    key = lax.broadcasted_iota(jnp.int32, (1, SEQ), 1)
    valid = (key < PATCHES) | ((key >= HEAD) & (key < HEAD + LEN - PATCHES))
    return jnp.where(valid, 0.0, -1e30)


def softmax_pair(queries, keys_cat, bias):
    scores = dot_nt(queries, keys_cat)
    out = []
    for head in range(2):
        own = scores[:, head * SEQ : (head + 1) * SEQ] + bias
        powers = jnp.exp(own - jnp.max(own, -1, keepdims=True))
        out.append(powers * (1.0 / jnp.sum(powers, -1, keepdims=True)))
    return jnp.concatenate(out, 1)


def spans(where_ref, pieces, rows):
    for side in range(2):
        for j in range(5):
            block = where_ref[4 * side + min(j, 3)]
            size = rows if j < 3 else rows // 2
            yield pieces[5 * side + j], block, (size if j == 4 else 0), size


def started(copies, sems, start=True):
    copies = [
        pltpu.make_async_copy(source, target, sems.at[j])
        for j, (source, target) in enumerate(copies)
    ]
    if start:
        for copy in copies:
            copy.start()
    return copies


def load_pieces(where_ref, pieces, target, sems, columns, start=True):
    return started(
        [
            (
                piece.at[:, pl.ds(columns[0], columns[1])],
                target.at[pl.ds(pl.multiple_of(block * 96 + first, 16), size), :],
            )
            for piece, block, first, size in spans(where_ref, pieces, 96)
        ],
        sems,
        start,
    )


def load_expert(where_ref, pieces, up, down, sems):
    copies = []
    for piece, block, first, size in spans(where_ref, pieces, 768):
        if first == 0:
            for chunk in range(4):
                copies.append(
                    (
                        piece.at[pl.ds(chunk * 96, 96), :],
                        up.at[chunk, pl.ds(pl.multiple_of(block * 96, 96), 96), :],
                    )
                )
        if first + size == 768:
            copies.append(
                (
                    piece.at[pl.ds(384 - first, 384), :],
                    down.at[pl.ds(pl.multiple_of(block * 384, 384), 384), :],
                )
            )
    return started(copies, sems)


def wait_all(copies):
    for copy in copies:
        copy.wait()


def attention_kernel(where_ref, tokens, masked, vector, *rest):
    pieces, rest = rest[:10], rest[10:]
    qkv, softs, context, hidden, normed_one, normed_two, params, weights, sems = rest

    @pl.when(pl.program_id(0) == 0)
    def _():
        wait_all(load_pieces(where_ref, pieces, weights, sems, (0, weights.shape[1])))
        columns = weights[:, 4 * D : 4 * D + 128].astype(F32)
        params[...] = jnp.transpose(columns)[:8]

    start = jnp.where(masked[...] == 1.0, vector[...], tokens[...].astype(F32))
    unit, _ = normalize(start)
    first = (unit * params[0:1] + params[1:2]).astype(BF16)
    normed_one[...] = first
    for third in range(3):
        at = pl.ds(third * D, D)
        qkv[:, at] = dot(first, weights[:, at]).astype(BF16)
    bias = key_bias()
    for pair in range(H // 2):
        queries = qkv[:, pl.ds(pair * 128, 128)] * BF16(1.0 / math.sqrt(HD))
        keys = halves(qkv[:, pl.ds(D + pair * 128, 128)])
        values = halves(qkv[:, pl.ds(2 * D + pair * 128, 128)])
        soft = softmax_pair(queries, keys, bias)
        softs[0, pair] = soft
        attention = soft.astype(BF16)
        context[:, pl.ds(pair * 128, 128)] = dot(attention, values).astype(BF16)
    after = start + dot(context[...], weights[:, pl.ds(3 * D, D)])
    hidden[...] = after
    unit, _ = normalize(after)
    normed_two[...] = (unit * params[2:3] + params[3:4]).astype(BF16)


def chosen(place, block):
    row = lax.broadcasted_iota(jnp.int32, (BLK, place.shape[1]), 0) + block * BLK
    return jnp.where(row == place[...], 1.0, 0.0).astype(BF16)


def rows_of(block):
    return pl.ds(pl.multiple_of(block * BLK, BLK), BLK)


def feed_back_kernel(where_ref, place, hidden, cotangent, context, params, *rest):
    pieces, attention_pieces, rest = rest[:10], rest[10:20], rest[20:]
    keep, send, send_far, grad_context = rest[:4]
    (high, low, rows_two, rows_hidden, rows_cot, rows_context, grad_two) = rest[4:11]
    (sum_up, sum_down, sums, w_up, w_down, w_out, stage) = rest[11:18]
    sems, attention_sems, out_sems = rest[18:]
    step = pl.program_id(0)
    blocks = where_ref[10]
    core = where_ref[8]

    def out_copies():
        return load_pieces(where_ref, attention_pieces, w_out, attention_sems, (3 * D, D), False)

    @pl.when(step == 0)
    def _():
        copies = load_expert(where_ref, pieces, w_up, w_down, sems)
        for copy in out_copies():
            copy.start()
        high[...] = hidden[...].astype(BF16)
        low[...] = (hidden[...] - high[...].astype(F32)).astype(BF16)

        def gather(block, _):
            pick, at = chosen(place, block), rows_of(block)
            rows = dot(pick, high[...]) + dot(pick, low[...])
            rows_hidden[at, :] = rows
            rows_cot[at, :] = dot(pick, cotangent[...]).astype(BF16)
            rows_context[at, :] = dot(pick, context[...]).astype(BF16)
            unit, _ = normalize(rows)
            rows_two[at, :] = (unit * params[2:3] + params[3:4]).astype(BF16)
            grad_two[at, :] = jnp.zeros((BLK, D), F32)
            return 0

        lax.fori_loop(0, blocks, gather, 0)
        wait_all(copies)

    up = w_up.at[step]
    down = w_down.at[pl.ds(pl.multiple_of(step * D, D), D), :]

    def expert(block, _):
        at = rows_of(block)
        rows, grads = rows_two[at, :], rows_cot[at, :]
        pre = dot(rows, up[...])
        chance = 0.5 * (1.0 + lax.erf(pre * math.sqrt(0.5)))
        activated = (pre * chance).astype(BF16)
        slope = chance + pre * (jnp.exp(-0.5 * pre * pre) * (1.0 / math.sqrt(2.0 * math.pi)))
        grad_pre = (dot_nt(grads, down[...]) * slope).astype(BF16)
        grad_two[at, :] += dot_nt(grad_pre, up[...])
        add_down = dot_tn(activated, grads)
        add_up = dot_tn(rows, grad_pre)

        @pl.when(block == 0)
        def _():
            sum_down[...] = add_down
            sum_up[...] = add_up

        @pl.when(block > 0)
        def _():
            sum_down[...] += add_down
            sum_up[...] += add_up

        return 0

    lax.fori_loop(0, blocks, expert, 0)

    def leaving(at_step):
        rows = pl.ds(pl.multiple_of(at_step * 96, 96), 96)
        columns = pl.ds(384, 384)
        mine = jnp.bitwise_xor(at_step, where_ref[9])
        near = jnp.minimum(mine, 2)
        sem = out_sems.at[at_step]
        return [
            (None, stage.at[0, :, rows, :], keep.at[:, rows, :], sem.at[0]),
            (None, stage.at[0, mine, columns, :], keep.at[mine, columns, :], sem.at[1]),
            (None, stage.at[1, pl.ds(0, 3), rows, :], send.at[:, rows, :], sem.at[2]),
            (None, stage.at[1, 3, rows, :], send_far.at[rows, :], sem.at[3]),
            (mine < 3, stage.at[1, near, columns, :], send.at[near, columns, :], sem.at[4]),
            (mine == 3, stage.at[1, 3, columns, :], send_far.at[columns, :], sem.at[4]),
        ]

    def each(copies, act):
        for when, source, target, sem in copies:
            copy = pltpu.make_async_copy(source, target, sem)
            if when is None:
                act(copy)
            else:
                pl.when(when)(functools.partial(act, copy))

    up_at = pl.ds(pl.multiple_of(step * 96, 96), 96)
    mine = jnp.bitwise_xor(step, where_ref[9])
    for side in range(2):
        for j in range(4):
            source = pl.ds(pl.multiple_of(where_ref[4 * side + j] * 96, 96), 96)
            stage[side, j, up_at, :] = sum_up[source, :].astype(BF16)
        half = core if side == 0 else 1 - core
        source = pl.ds(pl.multiple_of(half * 384, 384), 384)
        stage[side, mine, pl.ds(384, 384), :] = sum_down[source, :].astype(BF16)
    each(leaving(step), lambda copy: copy.start())

    @pl.when(step == pl.num_programs(0) - 1)
    def _():
        wait_all(out_copies())
        sums[...] = jnp.zeros_like(sums)

        def back(block, _):
            pick, at = chosen(place, block), rows_of(block)
            unit, inverse = normalize(rows_hidden[at, :])
            grad = grad_two[at, :]
            grad_hidden = rows_cot[at, :].astype(F32) + normalize_back(
                grad, unit, inverse, params[2:3]
            )
            sums[0:1] += total(grad * unit)
            sums[1:2] += total(grad)
            sums[2:3] += total(grad_hidden)
            grad_attn = grad_hidden.astype(BF16)
            add_out = dot_tn(rows_context[at, :], grad_attn)
            rows = dot_nt(grad_attn, w_out[...]).astype(BF16)
            rows = dot_tn(pick, rows).astype(BF16)

            @pl.when(block == 0)
            def _():
                sum_up[...] = add_out
                grad_context[...] = rows

            @pl.when(block > 0)
            def _():
                sum_up[...] += add_out
                grad_context[...] += rows

            return 0

        lax.fori_loop(0, blocks, back, 0)
        extra = jnp.concatenate([sums[...], jnp.zeros_like(sums[...])], 0).astype(BF16)
        for side in range(2):
            for j in range(4):
                source = pl.ds(pl.multiple_of(where_ref[4 * side + j] * 96, 96), 96)
                stage[side, j, pl.ds(768, 96), :] = sum_up[source, :].astype(BF16)
                stage[side, j, pl.ds(864, 16), :] = extra
        rows = pl.ds(768, 112)
        sem = out_sems.at[4]
        last = [
            (None, stage.at[0, :, rows, :], keep.at[:, rows, :], sem.at[0]),
            (None, stage.at[1, pl.ds(0, 3), rows, :], send.at[:, rows, :], sem.at[1]),
            (None, stage.at[1, 3, rows, :], send_far.at[rows, :], sem.at[2]),
        ]
        each(last, lambda copy: copy.start())
        each(last, lambda copy: copy.wait())
        for at_step in range(4):
            each(leaving(at_step), lambda copy: copy.wait())


def put_rows(target, rows, seq):
    target[seq * LEN : seq * LEN + PATCHES] = rows[:PATCHES]
    target[seq * LEN + PATCHES : (seq + 1) * LEN] = rows[HEAD : HEAD + LEN - PATCHES]


def attention_back_kernel(
    where_ref, qkv, softs, grad_context, normed_one, tokens, masked, vector, params, *rest
):
    pieces = rest[:10]
    keep, send, grad_tokens = rest[10:13]
    weights, sums, grad_qkv, stage, sems, out_sems = rest[13:]
    step = pl.program_id(0)
    here = pl.ds(pl.multiple_of(step * SEQ, SEQ), SEQ)

    def copies():
        return load_pieces(where_ref, pieces, weights, sems, (0, 3 * D), False)

    @pl.when(step == 0)
    def _():
        for copy in copies():
            copy.start()
        sums[...] = jnp.zeros_like(sums)

    inv_root = 1.0 / math.sqrt(HD)
    top = lax.broadcasted_iota(jnp.int32, (128, SEQ), 0) < HD
    for pair in range(H // 2):
        queries = qkv[:, pl.ds(pair * 128, 128)]
        keys = halves(qkv[:, pl.ds(D + pair * 128, 128)])
        values = halves(qkv[:, pl.ds(2 * D + pair * 128, 128)])
        grads = grad_context[:, pl.ds(pair * 128, 128)]
        grad_soft = dot_nt(grads, values)
        parts = []
        for head in range(2):
            span = slice(head * SEQ, (head + 1) * SEQ)
            own, grad = softs[0, pair, :, span], grad_soft[:, span]
            parts.append(own * (grad - jnp.sum(own * grad, -1, keepdims=True)))
        grad_scores = jnp.concatenate(parts, 1).astype(BF16)
        grad_qkv[here, pl.ds(pair * 128, 128)] = (dot(grad_scores, keys) * inv_root).astype(BF16)
        by_key = dot_tn(queries, grad_scores) * inv_root
        by_key = jnp.where(top, by_key[:, :SEQ], by_key[:, SEQ:])
        grad_qkv[here, pl.ds(D + pair * 128, 128)] = jnp.transpose(by_key).astype(BF16)
        by_value = dot_tn(grads, softs[0, pair].astype(BF16))
        by_value = jnp.where(top, by_value[:, :SEQ], by_value[:, SEQ:])
        grad_qkv[here, pl.ds(2 * D + pair * 128, 128)] = jnp.transpose(by_value).astype(BF16)

    @pl.when(step == 0)
    def _():
        wait_all(copies())

    grad_one = dot_nt(grad_qkv[here, :], weights[...])
    start = jnp.where(masked[...] == 1.0, vector[...], tokens[...].astype(F32))
    unit, inverse = normalize(start)
    grad_start = normalize_back(grad_one, unit, inverse, params[0:1])
    sums[0:1] += total(grad_one * unit)
    sums[1:2] += total(grad_one)
    sums[2:3] += total(jnp.where(masked[...] == 1.0, grad_start, 0.0))
    kept = jnp.where(masked[...] == 1.0, 0.0, grad_start)
    for seq in range(normed_one.shape[0] // SEQ):
        pl.when(step == seq)(functools.partial(put_rows, grad_tokens, kept, seq))

    @pl.when(step == pl.num_programs(0) - 1)
    def _():
        extra = jnp.concatenate([sums[...], jnp.zeros_like(sums[...])], 0).astype(BF16)
        for third in range(3):
            for part in range(3):
                at = pl.ds(third * D + part * SEQ, SEQ)
                add = dot_tn(normed_one[...], grad_qkv[:, at]).astype(BF16)
                for block in range(8):
                    stage[block, pl.ds(third * 96, 96), pl.ds(part * SEQ, SEQ)] = add[
                        block * 96 : (block + 1) * 96
                    ]
        out_copies = []
        for side, out in enumerate((keep, send)):
            for j in range(4):
                block = where_ref[4 * side + j]
                stage[block, pl.ds(3 * 96, 16), :] = extra
                out_copies.append((stage.at[block], out.at[j]))
        wait_all(started(out_copies, out_sems))


def gelu(pre):
    return (pre * (0.5 * (1.0 + lax.erf(pre * math.sqrt(0.5))))).astype(BF16)


def feed_kernel(text, where_ref, rows_in, before, *rest):
    pieces, (out, sums, w_up, w_down, sems, *tails) = rest[:10], rest[10:]
    tails = flat = tails[0]
    step = pl.program_id(0)
    seqs = rows_in.shape[0] // SEQ

    @pl.when(step == 0)
    def _():
        copies = load_expert(where_ref, pieces, w_up, w_down, sems)
        sums[...] = before[...]
        if text:
            for seq in range(seqs):
                tails[pl.ds(seq * TAIL, TAIL), :] = rows_in[pl.ds(seq * SEQ + HEAD, TAIL), :]
        wait_all(copies)

    up = w_up.at[step]
    down = w_down.at[pl.ds(pl.multiple_of(step * D, D), D), :]
    for seq in range(seqs):
        head = pl.ds(seq * SEQ, HEAD)

        @pl.when(where_ref[11 + seq] == int(text))
        def _():
            activated = gelu(dot(rows_in[head, :], up[...]))
            sums[head, :] += dot(activated, down[...])

    if text:
        more = dot(gelu(dot(tails[...], up[...])), down[...])
        for seq in range(seqs):
            sums[pl.ds(seq * SEQ + HEAD, TAIL), :] += more[seq * TAIL : (seq + 1) * TAIL]

    @pl.when(step == pl.num_programs(0) - 1)
    def _():
        if text:
            out[...] = sums[...]
        else:
            for seq in range(seqs):
                put_rows(flat, sums[pl.ds(seq * SEQ, SEQ), :], seq)
            out[...] = flat[...].astype(BF16)


def whole(shape):
    return pl.BlockSpec(shape, lambda *_: (0,) * len(shape), pipeline_mode=pl.Buffered(1))


def by_step(shape):
    return pl.BlockSpec(shape, lambda i, *_: (i,) + (0,) * (len(shape) - 1))


ANY = pl.BlockSpec(memory_space=pl.ANY)


def call(kernel, steps, ins, in_specs, outs, out_specs, scratch, name):
    run = pl.pallas_call(
        kernel,
        out_shape=tuple(jax.ShapeDtypeStruct(s, d) for s, d in outs),
        grid_spec=pltpu.PrefetchScalarGridSpec(
            num_scalar_prefetch=1,
            grid=(steps,),
            in_specs=in_specs,
            out_specs=out_specs,
            scratch_shapes=scratch,
        ),
        compiler_params=pltpu.CompilerParams(vmem_limit_bytes=60 * MIB),
        cost_estimate=pl.CostEstimate(flops=1, bytes_accessed=1, transcendentals=0),
        name=name,
    )
    return run(*ins)


def lay(rows, seqs):
    rows = rows.reshape(seqs, LEN, -1)
    return jnp.concatenate(
        [
            jnp.pad(rows[:, :PATCHES], ((0, 0), (0, HEAD - PATCHES), (0, 0))),
            jnp.pad(rows[:, PATCHES:], ((0, 0), (0, TAIL - LEN + PATCHES), (0, 0))),
        ],
        1,
    ).reshape(seqs * SEQ, -1)


def tie(*trees):
    return lax.optimization_barrier(trees)


def in_order(rows, part, blocks=0, axis=0):
    rows = jnp.moveaxis(rows, axis, blocks)
    shape, columns = rows.shape[:blocks], rows.shape[-1]
    count, size = rows.shape[blocks], rows.shape[blocks + 1]
    if size == part:
        return rows.reshape(*shape, count * part, columns)
    up = rows[..., : 4 * part, :].reshape(*shape, count, 4, part, columns)
    up = jnp.swapaxes(up, blocks, blocks + 1).reshape(*shape, 4 * count * part, columns)
    down = rows[..., 4 * part :, :].reshape(*shape, count * (size - 4 * part), columns)
    return jnp.concatenate([up, down], -2)


class Cube:
    axes = ("y", "x", "core", "z")
    swap = [(0, 1), (1, 0)]

    def __init__(self):
        y, x, core, z = (lax.axis_index(a) for a in self.axes)
        self.z, self.core, self.flat = z, core, y * 2 + x
        self.index = ((y * 2 + x) * 2 + core) * 4 + z

    def turn(self, block, k):
        return lax.ppermute(block, "z", [(i, (i + k) % 4) for i in range(4)])

    def turns(self, block):
        return [block] + [self.turn(block, k) for k in (1, 2, 3)]

    def ring(self, ring, part):
        out = []
        for place in range(4):
            k = lax.rem(self.z + 4 - place, 4)
            out.append(
                jnp.where(
                    k == 0,
                    ring[0],
                    jnp.where(k == 1, ring[1], jnp.where(k == 2, ring[2], ring[3])),
                )
            )
        return in_order(jnp.stack(out), part)

    def swapped(self, block, axis):
        return lax.ppermute(block, axis, self.swap)

    def sides(self, own):
        return own, self.swapped(own, "x"), self.swapped(own, "y")

    def halves(self, near):
        half = near[0].shape[0] // 2
        return near[1][:half], near[2][half:]

    def to_corners(self, near, halves):
        return (*near, self.swapped(halves[0], "y"), self.swapped(halves[1], "x"))

    def corner(self, near):
        return self.to_corners(near, self.halves(near))

    def cores(self, near):
        return [*near] + [self.swapped(b, "core") for b in near]

    def plane(self, j, block):
        if j == 1:
            return self.swapped(block, "x")
        if j == 2:
            return self.swapped(block, "y")
        return lax.ppermute(block, ("y", "x"), [(i, 3 - i) for i in range(4)])

    def to_core(self, block):
        return self.swapped(block, "core")

    def far_sums(self, keep, got):
        return (keep[3].astype(F32) + got.astype(F32)).astype(BF16)

    def to_corner(self, both):
        half = both.shape[0] // 2
        return self.swapped(both[:half], "x"), self.swapped(both[half:], "y")

    def side_sums(self, keep, got, corner):
        half = corner[0].shape[0]
        by_x = jnp.pad(corner[0], ((0, half), (0, 0))).astype(F32)
        by_y = jnp.pad(corner[1], ((half, 0), (0, 0))).astype(F32)
        to_x = keep[1].astype(F32) + got[1].astype(F32) + by_y
        to_y = keep[2].astype(F32) + got[2].astype(F32) + by_x
        return [keep, got, to_x.astype(BF16), to_y.astype(BF16)]

    def to_sides(self, sums):
        return [*sums[:2], self.swapped(sums[2], "x"), self.swapped(sums[3], "y")]

    def plane_sums(self, keep, got):
        both = [keep[j].astype(F32) + got[j].astype(F32) for j in (1, 2, 3)]
        return [keep, got] + [b.astype(BF16) for b in both]

    def to_plane(self, sums):
        return sums[:2] + [self.plane(j, sums[j + 1]) for j in (1, 2, 3)]

    def last(self, near):
        return near[3:]

    def cores_of(self, near, last):
        return self.cores([*near[:3], *last])

    def far_cores(self, near):
        return [self.swapped(b, "core") for b in near]

    def rest_cores(self, near, far):
        return [*near, *far] + self.far_cores(near[len(far) :])

    def ring_sums(self, group, fields):
        keep, got, *more = group
        mine = sum(m.astype(F32) for m in (keep[0], got[0], *more))
        rounded = lax.optimization_barrier(mine.astype(BF16))
        return [cut(mine, fields, self.z)] + [
            cut(rounded, fields, lax.rem(self.z + k, 4)) for k in (1, 2, 3)
        ]

    def to_ring(self, parts, which):
        return [self.turn(p, k) if k in which else p for k, p in enumerate(parts)]

    def add_ring(self, ring):
        return ring[0] + sum(m.astype(F32) for m in ring[1:])


class Flat:
    axes = ("dp", "fsdp")

    def __init__(self, count):
        self.flat = self.core = jnp.int32(0)
        self.index = lax.axis_index(self.axes)
        self.count = count

    def turns(self, block):
        return lax.all_gather(block, self.axes, axis=0)

    def ring(self, full, part):
        return in_order(full.reshape((8, -1) + full.shape[1:]), part, 1, 1)

    def sides(self, own):
        return own

    def halves(self, near):
        return ()

    def to_corners(self, near, halves):
        return near

    def corner(self, near):
        return near

    def cores(self, near):
        half = near.shape[1] // 2
        out = []
        for side in range(2):
            out += [near[side], near[2 + side], near[4 + side]]
            out += [near[6 + side, :half], near[6 + side, half:]]
        return out

    def to_core(self, block):
        return block

    def far_sums(self, keep, got):
        return got

    def to_corner(self, both):
        return both

    def side_sums(self, keep, got, corner):
        return self.plane_sums(keep, jnp.concatenate([got, corner[None]]))

    def to_sides(self, sums):
        return sums

    def plane_sums(self, keep, got):
        return [jnp.stack([keep, got], 1).reshape((8,) + keep.shape[1:])]

    def to_plane(self, sums):
        return sums

    def last(self, near):
        return ()

    def cores_of(self, near, last):
        return self.cores(near)

    def far_cores(self, near):
        return ()

    def rest_cores(self, near, far):
        return self.cores(near)

    def ring_sums(self, group, fields):
        ways = self.count // 8
        parts = [[cut(block, fields, w, ways) for w in range(ways)] for block in group[0]]
        return jnp.stack([p for block in parts for p in block]).astype(F32)

    def to_ring(self, parts, which):
        if 3 not in which:
            return parts
        return lax.psum_scatter(parts, self.axes, scatter_dimension=0, tiled=False)

    def add_ring(self, ring):
        return ring


def pack_expert(up, down):
    part = up.shape[0]
    up = up.reshape(part, 4, D).transpose(1, 0, 2).reshape(4 * part, D)
    return jnp.concatenate([up, down], 0)


def cut(rows, fields, place, ways=4):
    out, at = [], 0
    for groups, size in fields:
        part = rows[at : at + max(groups, 1) * size]
        at += max(groups, 1) * size
        if groups:
            part = part.reshape(groups, ways, size // ways, D)
            part = lax.dynamic_index_in_dim(part, place, 1, keepdims=False).reshape(-1, D)
        out.append(part)
    return jnp.concatenate(out)


def layer(
    make,
    tokens,
    modality,
    token_mask,
    cotangent,
    mask_vector,
    ln_one_gain,
    ln_one_shift,
    w_qkv,
    w_out,
    ln_two_gain,
    ln_two_shift,
    w_up,
    w_down,
):
    net = make()
    part = w_qkv.shape[0]
    seqs = tokens.shape[0] // LEN
    rows = seqs * SEQ
    columns = jnp.stack([ln_one_gain, ln_one_shift, ln_two_gain, ln_two_shift], 1)
    packed = jnp.concatenate([w_qkv, w_out, jnp.pad(columns, ((0, 0), (0, 124)))], 1)
    n_columns = packed.shape[1]
    ring = net.turns(packed)

    seq_masks = token_mask.reshape(seqs, LEN)
    masked = jnp.concatenate(
        [
            jnp.pad(seq_masks[:, :PATCHES], ((0, 0), (0, HEAD - PATCHES))),
            jnp.pad(seq_masks[:, PATCHES:], ((0, 0), (0, TAIL - LEN + PATCHES))),
        ],
        1,
    ).reshape(1, rows)
    order = jnp.cumsum(masked, 1)
    place = jnp.where(masked == 1, order - 1, -1)
    blocks = jnp.maximum((order[0, rows - 1] + BLK - 1) // BLK, 1)
    near = jnp.arange(8, dtype=jnp.int32)
    near = jnp.bitwise_xor(net.flat, near & 3) * 2 + jnp.bitwise_xor(net.core, near >> 2)
    where_ref = jnp.concatenate(
        [
            near,
            jnp.stack([net.core, net.flat, blocks]).astype(jnp.int32),
            modality.reshape(seqs, LEN)[:, 0],
        ]
    )
    tokens = lay(tokens, seqs)
    ring, where_ref, tokens = tie(ring, where_ref, tokens)

    own = net.ring(ring, part)
    near = net.sides(own)
    text, _ = tie(pack_expert(w_up[1], w_down[1]), own)
    ring_text = net.turns(text)
    masked = masked.astype(F32).reshape(rows, 1)
    cotangent = lay(cotangent, seqs)
    vector = mask_vector.astype(F32).reshape(1, D)
    near, masked, place, cotangent, vector = tie(near, masked, place, cotangent, vector)
    pieces = net.cores(net.corner(near))
    own_text = net.ring(ring_text, part)
    pieces, own_text, image = tie(pieces, own_text, pack_expert(w_up[0], w_down[0]))
    near_text = net.sides(own_text)
    image = net.turns(image)

    def feed(text, before, weights):
        return call(
            functools.partial(feed_kernel, text),
            4,
            (where_ref, normed_two, before, *weights),
            [whole((rows, D)), whole((rows, D))] + [ANY] * 10,
            [((rows, D), F32) if text else ((seqs * LEN, D), BF16)],
            [whole((rows if text else seqs * LEN, D))],
            [
                pltpu.VMEM((rows, D), F32),
                pltpu.VMEM((4, D, D), BF16),
                pltpu.VMEM((FF, D), BF16),
                pltpu.SemaphoreType.DMA((40,)),
                pltpu.VMEM((seqs * TAIL, D), BF16) if text else pltpu.VMEM((seqs * LEN, D), F32),
            ],
            "feed_text" if text else "feed_image",
        )[0]

    qkv, softs, context, hidden, normed_one, normed_two, params = call(
        attention_kernel,
        seqs,
        (where_ref, tokens, masked, vector, *pieces),
        [by_step((SEQ, D)), by_step((SEQ, 1)), whole((1, D))] + [ANY] * 10,
        [
            ((rows, 3 * D), BF16),
            ((seqs, H // 2, SEQ, 2 * SEQ), F32),
            ((rows, D), BF16),
            ((rows, D), F32),
            ((rows, D), BF16),
            ((rows, D), BF16),
            ((8, D), F32),
        ],
        [
            by_step((SEQ, 3 * D)),
            by_step((1, H // 2, SEQ, 2 * SEQ)),
            by_step((SEQ, D)),
            by_step((SEQ, D)),
            by_step((SEQ, D)),
            by_step((SEQ, D)),
            pl.BlockSpec((8, D), lambda i, *_: (0, 0)),
        ],
        [pltpu.VMEM((D, n_columns), BF16), pltpu.SemaphoreType.DMA((10,))],
        "attention",
    )

    near_text, image, (qkv, softs, context, hidden, normed_one, normed_two, params) = tie(
        near_text, image, (qkv, softs, context, hidden, normed_one, normed_two, params)
    )
    near_text = net.corner(near_text)
    last, image = tie(net.last(near_text), net.ring(image, part))
    pieces_text = net.cores_of(near_text, last)
    image, pieces_text = tie(image, pieces_text)
    near_image = net.sides(image)

    block = (ROWS_ONE, D)
    keep, send, send_far, grad_context = call(
        feed_back_kernel,
        4,
        (where_ref, place, hidden, cotangent, context, params, *pieces_text, *pieces),
        [whole((1, rows)), whole((rows, D)), whole((rows, D)), whole((rows, D)), whole((8, D))]
        + [ANY] * 20,
        [((4, *block), BF16), ((3, *block), BF16), (block, BF16), ((rows, D), BF16)],
        [ANY] * 3 + [whole((rows, D))],
        [pltpu.VMEM((rows, D), BF16)] * 3
        + [
            pltpu.VMEM((rows, D), F32),
            pltpu.VMEM((rows, D), BF16),
            pltpu.VMEM((rows, D), BF16),
            pltpu.VMEM((rows, D), F32),
        ]
        + [pltpu.VMEM((D, D), F32)] * 2
        + [
            pltpu.VMEM((8, D), F32),
            pltpu.VMEM((4, D, D), BF16),
            pltpu.VMEM((FF, D), BF16),
            pltpu.VMEM((D, D), BF16),
            pltpu.VMEM((2, 4, *block), BF16),
            pltpu.SemaphoreType.DMA((40,)),
            pltpu.SemaphoreType.DMA((10,)),
            pltpu.SemaphoreType.DMA((5, 5)),
        ],
        "feed_back",
    )
    near_image, keep, send, send_far, grad_context = tie(
        near_image, keep, send, send_far, grad_context
    )
    far = net.far_sums(keep, net.to_core(send_far))
    halves_image = net.halves(near_image)
    far, send, hidden, halves_image = tie(far, send, hidden, halves_image)
    got = net.to_core(send)
    corner = net.to_corner(far)
    near_image = net.to_corners(near_image, halves_image)
    after = feed(True, hidden, pieces_text)
    corner, got, near_image, after = tie(corner, got, near_image, after)
    sums_feed = net.side_sums(keep, got, corner)
    sums_feed, grad_context = tie(sums_feed, grad_context)
    sums_feed = net.to_sides(sums_feed)
    far_image = net.far_cores(near_image[:3])

    keep, send, grad_tokens = call(
        attention_back_kernel,
        seqs,
        (where_ref, qkv, softs, grad_context, normed_one, tokens, masked, vector, params, *pieces),
        [
            by_step((SEQ, 3 * D)),
            by_step((1, H // 2, SEQ, 2 * SEQ)),
            by_step((SEQ, D)),
            whole((rows, D)),
            by_step((SEQ, D)),
            by_step((SEQ, 1)),
            whole((1, D)),
            whole((8, D)),
        ]
        + [ANY] * 10,
        [((4, ROWS_QKV, D), BF16), ((4, ROWS_QKV, D), BF16), ((seqs * LEN, D), F32)],
        [ANY, ANY, whole((seqs * LEN, D))],
        [
            pltpu.VMEM((D, 3 * D), BF16),
            pltpu.VMEM((8, D), F32),
            pltpu.VMEM((rows, 3 * D), BF16),
            pltpu.VMEM((8, ROWS_QKV, D), BF16),
            pltpu.SemaphoreType.DMA((10,)),
            pltpu.SemaphoreType.DMA((8,)),
        ],
        "attention_back",
    )
    keep, send, grad_tokens, sums_feed, far_image = tie(
        keep, send, grad_tokens, sums_feed, far_image
    )
    got = net.to_core(send)
    pieces_image = net.rest_cores(near_image, far_image)
    sums_qkv = net.plane_sums(keep, got)
    ring_one = net.ring_sums(sums_feed, [(4, 96), (1, 384), (1, 96), (0, 16)])
    sums_qkv, ring_one, after, pieces_image = tie(sums_qkv, ring_one, after, pieces_image)
    sums_qkv = net.to_plane(sums_qkv)
    ring_one = net.to_ring(ring_one, (1, 2))
    output = feed(False, after, pieces_image)
    sums_qkv, ring_one, output = tie(sums_qkv, ring_one, output)
    ring_two = net.ring_sums(sums_qkv, [(3, 96), (0, 16)])
    ring_one = net.to_ring(ring_one, (3,))
    ring_two = net.to_ring(ring_two, (1, 2, 3))

    grads = net.add_ring(ring_one)
    grad_w_up = grads[: 4 * part].reshape(4, part, D).transpose(1, 0, 2).reshape(part, FF)
    grad_w_down = grads[4 * part : 8 * part]
    grad_w_out = grads[8 * part : 9 * part]
    extra_one = grads[9 * part :]
    grads = net.add_ring(ring_two)
    grad_w_qkv = grads[: 3 * part].reshape(3, part, D).transpose(1, 0, 2).reshape(part, 3 * D)
    extra_two = grads[3 * part :]

    def own(vector):
        return lax.dynamic_slice_in_dim(vector, net.index * part, part)

    return (
        output,
        grad_tokens,
        extra_one[2] + extra_two[2],
        own(extra_two[0]),
        own(extra_two[1]),
        grad_w_qkv,
        grad_w_out,
        own(extra_one[0]),
        own(extra_one[1]),
        grad_w_up,
        grad_w_down,
    )


def solution(mesh):
    if (mesh.shape["dp"], mesh.shape["fsdp"]) == (8, 4):
        mesh = Mesh(mesh.devices.reshape(2, 2, 2, 4), Cube.axes)
        make = Cube
    else:
        make = functools.partial(Flat, mesh.size)
    axes = Cube.axes if make is Cube else Flat.axes
    row, flat = P(axes, None), P(axes)
    middle = P(None, axes, None)
    in_specs = (row, flat, flat, row, P(), flat, flat, row, row, flat, flat, middle, middle)
    out_specs = (row, row, P(), flat, flat, row, row, flat, flat, row, row)
    return jax.shard_map(
        functools.partial(layer, make),
        mesh=mesh,
        in_specs=in_specs,
        out_specs=out_specs,
        check_vma=False,
    )
```

```python
import functools
import math

import jax
import jax.numpy as jnp
from jax import lax
from jax.experimental import pallas as pl
from jax.experimental.pallas import tpu as pltpu
from jax.sharding import Mesh, PartitionSpec as P

H = 12
HD = 64
LEN = 237
PATCHES = 197
HEAD = 208
TAIL = 48
SEQ = HEAD + TAIL
D = H * HD
FF = 4 * D
BLK = 256
EPS = 1e-05
F32 = jnp.float32
BF16 = jnp.bfloat16
MIB = 1 << 20
ROWS_ONE = 864
ROWS_QKV = 304


def dot(a, b):
    return jnp.dot(a, b, preferred_element_type=F32)


def dot_nt(a, b):
    return lax.dot_general(a, b, (((1,), (1,)), ((), ())), preferred_element_type=F32)


def dot_tn(a, b):
    return lax.dot_general(a, b, (((0,), (0,)), ((), ())), preferred_element_type=F32)


def mean(rows):
    return jnp.mean(rows, -1, keepdims=True)


def normalize(rows):
    centred = rows - mean(rows)
    inverse = lax.rsqrt(mean(centred * centred) + EPS)
    return centred * inverse, inverse


def normalize_back(grad, unit, inverse, gain):
    scaled = grad * gain
    return inverse * (scaled - mean(scaled) - unit * mean(scaled * unit))


def total(rows):
    return jnp.sum(rows, 0, keepdims=True)


def halves(pair):
    lane = lax.broadcasted_iota(jnp.int32, pair.shape, 1)
    zero = jnp.zeros_like(pair)
    return jnp.concatenate(
        [jnp.where(lane < HD, pair, zero), jnp.where(lane < HD, zero, pair)], 0
    )


def key_bias():
    key = lax.broadcasted_iota(jnp.int32, (1, SEQ), 1)
    valid = (key < PATCHES) | ((key >= HEAD) & (key < HEAD + LEN - PATCHES))
    return jnp.where(valid, 0.0, -1e30)


def softmax_pair(queries, keys_cat, bias):
    scores = dot_nt(queries, keys_cat)
    out = []
    for head in range(2):
        own = scores[:, head * SEQ : (head + 1) * SEQ] + bias
        powers = jnp.exp(own - jnp.max(own, -1, keepdims=True))
        out.append(powers * (1.0 / jnp.sum(powers, -1, keepdims=True)))
    return jnp.concatenate(out, 1)


def spans(where_ref, pieces, rows):
    for side in range(2):
        for j in range(5):
            block = where_ref[4 * side + min(j, 3)]
            size = rows if j < 3 else rows // 2
            yield pieces[5 * side + j], block, (size if j == 4 else 0), size


def started(copies, sems, start=True):
    copies = [
        pltpu.make_async_copy(source, target, sems.at[j])
        for j, (source, target) in enumerate(copies)
    ]
    if start:
        for copy in copies:
            copy.start()
    return copies


def load_pieces(where_ref, pieces, target, sems, columns, start=True):
    return started(
        [
            (
                piece.at[:, pl.ds(columns[0], columns[1])],
                target.at[pl.ds(pl.multiple_of(block * 96 + first, 16), size), :],
            )
            for piece, block, first, size in spans(where_ref, pieces, 96)
        ],
        sems,
        start,
    )


def load_expert(where_ref, pieces, up, down, sems):
    copies = []
    for piece, block, first, size in spans(where_ref, pieces, 768):
        if first == 0:
            for chunk in range(4):
                copies.append(
                    (
                        piece.at[pl.ds(chunk * 96, 96), :],
                        up.at[chunk, pl.ds(pl.multiple_of(block * 96, 96), 96), :],
                    )
                )
        if first + size == 768:
            copies.append(
                (
                    piece.at[pl.ds(384 - first, 384), :],
                    down.at[pl.ds(pl.multiple_of(block * 384, 384), 384), :],
                )
            )
    return started(copies, sems)


def wait_all(copies):
    for copy in copies:
        copy.wait()


def attention_kernel(where_ref, tokens, masked, vector, *rest):
    pieces, rest = rest[:10], rest[10:]
    qkv, softs, context, hidden, normed_one, normed_two, params, weights, sems = rest

    @pl.when(pl.program_id(0) == 0)
    def _():
        wait_all(load_pieces(where_ref, pieces, weights, sems, (0, weights.shape[1])))
        columns = weights[:, 4 * D : 4 * D + 128].astype(F32)
        params[...] = jnp.transpose(columns)[:8]

    start = jnp.where(masked[...] == 1.0, vector[...], tokens[...].astype(F32))
    unit, _ = normalize(start)
    first = (unit * params[0:1] + params[1:2]).astype(BF16)
    normed_one[...] = first
    for third in range(3):
        at = pl.ds(third * D, D)
        qkv[:, at] = dot(first, weights[:, at]).astype(BF16)
    bias = key_bias()
    for pair in range(H // 2):
        queries = qkv[:, pl.ds(pair * 128, 128)] * BF16(1.0 / math.sqrt(HD))
        keys = halves(qkv[:, pl.ds(D + pair * 128, 128)])
        values = halves(qkv[:, pl.ds(2 * D + pair * 128, 128)])
        soft = softmax_pair(queries, keys, bias)
        softs[0, pair] = soft
        attention = soft.astype(BF16)
        context[:, pl.ds(pair * 128, 128)] = dot(attention, values).astype(BF16)
    after = start + dot(context[...], weights[:, pl.ds(3 * D, D)])
    hidden[...] = after
    unit, _ = normalize(after)
    normed_two[...] = (unit * params[2:3] + params[3:4]).astype(BF16)


def chosen(place, block):
    row = lax.broadcasted_iota(jnp.int32, (BLK, place.shape[1]), 0) + block * BLK
    return jnp.where(row == place[...], 1.0, 0.0).astype(BF16)


def rows_of(block):
    return pl.ds(pl.multiple_of(block * BLK, BLK), BLK)


def feed_back_kernel(where_ref, place, hidden, cotangent, context, params, *rest):
    pieces, attention_pieces, rest = rest[:10], rest[10:20], rest[20:]
    keep, send, send_far, grad_context, sums = rest[:5]
    (high, low, rows_two, rows_hidden, rows_cot, rows_context, grad_two) = rest[5:12]
    (sum_up, sum_down, w_up, w_down, w_out, stage) = rest[12:18]
    sems, attention_sems, out_sems = rest[18:]
    step = pl.program_id(0)
    blocks = where_ref[10]
    core = where_ref[8]

    def out_copies():
        return load_pieces(where_ref, attention_pieces, w_out, attention_sems, (3 * D, D), False)

    @pl.when(step == 0)
    def _():
        copies = load_expert(where_ref, pieces, w_up, w_down, sems)
        for copy in out_copies():
            copy.start()
        high[...] = hidden[...].astype(BF16)
        low[...] = (hidden[...] - high[...].astype(F32)).astype(BF16)

        def gather(block, _):
            pick, at = chosen(place, block), rows_of(block)
            rows = dot(pick, high[...]) + dot(pick, low[...])
            rows_hidden[at, :] = rows
            rows_cot[at, :] = dot(pick, cotangent[...]).astype(BF16)
            rows_context[at, :] = dot(pick, context[...]).astype(BF16)
            unit, _ = normalize(rows)
            rows_two[at, :] = (unit * params[2:3] + params[3:4]).astype(BF16)
            grad_two[at, :] = jnp.zeros((BLK, D), F32)
            return 0

        lax.fori_loop(0, blocks, gather, 0)
        wait_all(copies)

    up = w_up.at[step]
    down = w_down.at[pl.ds(pl.multiple_of(step * D, D), D), :]

    def expert(block, _):
        at = rows_of(block)
        rows, grads = rows_two[at, :], rows_cot[at, :]
        pre = dot(rows, up[...])
        chance = 0.5 * (1.0 + lax.erf(pre * math.sqrt(0.5)))
        activated = (pre * chance).astype(BF16)
        slope = chance + pre * (jnp.exp(-0.5 * pre * pre) * (1.0 / math.sqrt(2.0 * math.pi)))
        grad_pre = (dot_nt(grads, down[...]) * slope).astype(BF16)
        grad_two[at, :] += dot_nt(grad_pre, up[...])
        add_down = dot_tn(activated, grads)
        add_up = dot_tn(rows, grad_pre)

        @pl.when(block == 0)
        def _():
            sum_down[...] = add_down
            sum_up[...] = add_up

        @pl.when(block > 0)
        def _():
            sum_down[...] += add_down
            sum_up[...] += add_up

        return 0

    lax.fori_loop(0, blocks, expert, 0)

    def leaving(at_step):
        rows = pl.ds(pl.multiple_of(at_step * 96, 96), 96)
        columns = pl.ds(384, 384)
        mine = jnp.bitwise_xor(at_step, where_ref[9])
        near = jnp.minimum(mine, 2)
        sem = out_sems.at[at_step]
        return [
            (None, stage.at[0, :, rows, :], keep.at[:, rows, :], sem.at[0]),
            (None, stage.at[0, mine, columns, :], keep.at[mine, columns, :], sem.at[1]),
            (None, stage.at[1, pl.ds(0, 3), rows, :], send.at[:, rows, :], sem.at[2]),
            (None, stage.at[1, 3, rows, :], send_far.at[rows, :], sem.at[3]),
            (mine < 3, stage.at[1, near, columns, :], send.at[near, columns, :], sem.at[4]),
            (mine == 3, stage.at[1, 3, columns, :], send_far.at[columns, :], sem.at[4]),
        ]

    def each(copies, act):
        for when, source, target, sem in copies:
            copy = pltpu.make_async_copy(source, target, sem)
            if when is None:
                act(copy)
            else:
                pl.when(when)(functools.partial(act, copy))

    up_at = pl.ds(pl.multiple_of(step * 96, 96), 96)
    mine = jnp.bitwise_xor(step, where_ref[9])
    for side in range(2):
        for j in range(4):
            source = pl.ds(pl.multiple_of(where_ref[4 * side + j] * 96, 96), 96)
            stage[side, j, up_at, :] = sum_up[source, :].astype(BF16)
        half = core if side == 0 else 1 - core
        source = pl.ds(pl.multiple_of(half * 384, 384), 384)
        stage[side, mine, pl.ds(384, 384), :] = sum_down[source, :].astype(BF16)
    each(leaving(step), lambda copy: copy.start())

    @pl.when(step == pl.num_programs(0) - 1)
    def _():
        wait_all(out_copies())
        sums[...] = jnp.zeros_like(sums)

        def back(block, _):
            pick, at = chosen(place, block), rows_of(block)
            unit, inverse = normalize(rows_hidden[at, :])
            grad = grad_two[at, :]
            grad_hidden = rows_cot[at, :].astype(F32) + normalize_back(
                grad, unit, inverse, params[2:3]
            )
            sums[0:1] += total(grad * unit)
            sums[1:2] += total(grad)
            sums[2:3] += total(grad_hidden)
            grad_attn = grad_hidden.astype(BF16)
            add_out = dot_tn(rows_context[at, :], grad_attn)
            rows = dot_nt(grad_attn, w_out[...]).astype(BF16)
            rows = dot_tn(pick, rows).astype(BF16)

            @pl.when(block == 0)
            def _():
                sum_up[...] = add_out
                grad_context[...] = rows

            @pl.when(block > 0)
            def _():
                sum_up[...] += add_out
                grad_context[...] += rows

            return 0

        lax.fori_loop(0, blocks, back, 0)
        for side in range(2):
            for j in range(4):
                source = pl.ds(pl.multiple_of(where_ref[4 * side + j] * 96, 96), 96)
                stage[side, j, pl.ds(768, 96), :] = sum_up[source, :].astype(BF16)
        rows = pl.ds(768, 96)
        sem = out_sems.at[4]
        last = [
            (None, stage.at[0, :, rows, :], keep.at[:, rows, :], sem.at[0]),
            (None, stage.at[1, pl.ds(0, 3), rows, :], send.at[:, rows, :], sem.at[1]),
            (None, stage.at[1, 3, rows, :], send_far.at[rows, :], sem.at[2]),
        ]
        each(last, lambda copy: copy.start())
        each(last, lambda copy: copy.wait())
        for at_step in range(4):
            each(leaving(at_step), lambda copy: copy.wait())


def put_rows(target, rows, seq):
    target[seq * LEN : seq * LEN + PATCHES] = rows[:PATCHES]
    target[seq * LEN + PATCHES : (seq + 1) * LEN] = rows[HEAD : HEAD + LEN - PATCHES]


def attention_back_kernel(
    where_ref, qkv, softs, grad_context, normed_one, tokens, masked, vector, params, before, *rest
):
    pieces = rest[:10]
    keep, send, grad_tokens = rest[10:13]
    weights, sums, grad_qkv, stage, sems, out_sems = rest[13:]
    step = pl.program_id(0)
    here = pl.ds(pl.multiple_of(step * SEQ, SEQ), SEQ)

    def copies():
        return load_pieces(where_ref, pieces, weights, sems, (0, 3 * D), False)

    @pl.when(step == 0)
    def _():
        for copy in copies():
            copy.start()
        sums[...] = before[...]

    inv_root = 1.0 / math.sqrt(HD)
    top = lax.broadcasted_iota(jnp.int32, (128, SEQ), 0) < HD
    for pair in range(H // 2):
        queries = qkv[:, pl.ds(pair * 128, 128)]
        keys = halves(qkv[:, pl.ds(D + pair * 128, 128)])
        values = halves(qkv[:, pl.ds(2 * D + pair * 128, 128)])
        grads = grad_context[:, pl.ds(pair * 128, 128)]
        grad_soft = dot_nt(grads, values)
        parts = []
        for head in range(2):
            span = slice(head * SEQ, (head + 1) * SEQ)
            own, grad = softs[0, pair, :, span], grad_soft[:, span]
            parts.append(own * (grad - jnp.sum(own * grad, -1, keepdims=True)))
        grad_scores = jnp.concatenate(parts, 1).astype(BF16)
        grad_qkv[here, pl.ds(pair * 128, 128)] = (dot(grad_scores, keys) * inv_root).astype(BF16)
        by_key = dot_tn(queries, grad_scores) * inv_root
        by_key = jnp.where(top, by_key[:, :SEQ], by_key[:, SEQ:])
        grad_qkv[here, pl.ds(D + pair * 128, 128)] = jnp.transpose(by_key).astype(BF16)
        by_value = dot_tn(grads, softs[0, pair].astype(BF16))
        by_value = jnp.where(top, by_value[:, :SEQ], by_value[:, SEQ:])
        grad_qkv[here, pl.ds(2 * D + pair * 128, 128)] = jnp.transpose(by_value).astype(BF16)

    @pl.when(step == 0)
    def _():
        wait_all(copies())

    grad_one = dot_nt(grad_qkv[here, :], weights[...])
    start = jnp.where(masked[...] == 1.0, vector[...], tokens[...].astype(F32))
    unit, inverse = normalize(start)
    grad_start = normalize_back(grad_one, unit, inverse, params[0:1])
    sums[3:4] += total(grad_one * unit)
    sums[4:5] += total(grad_one)
    sums[2:3] += total(jnp.where(masked[...] == 1.0, grad_start, 0.0))
    kept = jnp.where(masked[...] == 1.0, 0.0, grad_start)
    for seq in range(normed_one.shape[0] // SEQ):
        pl.when(step == seq)(functools.partial(put_rows, grad_tokens, kept, seq))

    @pl.when(step == pl.num_programs(0) - 1)
    def _():
        extra = jnp.concatenate([sums[...], jnp.zeros_like(sums[...])], 0).astype(BF16)
        for third in range(3):
            for part in range(3):
                at = pl.ds(third * D + part * SEQ, SEQ)
                add = dot_tn(normed_one[...], grad_qkv[:, at]).astype(BF16)
                for block in range(8):
                    stage[block, pl.ds(third * 96, 96), pl.ds(part * SEQ, SEQ)] = add[
                        block * 96 : (block + 1) * 96
                    ]
        out_copies = []
        for side, out in enumerate((keep, send)):
            for j in range(4):
                block = where_ref[4 * side + j]
                stage[block, pl.ds(3 * 96, 16), :] = extra
                out_copies.append((stage.at[block], out.at[j]))
        wait_all(started(out_copies, out_sems))


def gelu(pre):
    return (pre * (0.5 * (1.0 + lax.erf(pre * math.sqrt(0.5))))).astype(BF16)


def feed_kernel(text, where_ref, rows_in, before, *rest):
    pieces, (out, sums, w_up, w_down, sems, *tails) = rest[:10], rest[10:]
    tails = flat = tails[0]
    step = pl.program_id(0)
    seqs = rows_in.shape[0] // SEQ

    @pl.when(step == 0)
    def _():
        copies = load_expert(where_ref, pieces, w_up, w_down, sems)
        sums[...] = before[...]
        if text:
            for seq in range(seqs):
                tails[pl.ds(seq * TAIL, TAIL), :] = rows_in[pl.ds(seq * SEQ + HEAD, TAIL), :]
        wait_all(copies)

    up = w_up.at[step]
    down = w_down.at[pl.ds(pl.multiple_of(step * D, D), D), :]
    for seq in range(seqs):
        head = pl.ds(seq * SEQ, HEAD)

        @pl.when(where_ref[11 + seq] == int(text))
        def _():
            activated = gelu(dot(rows_in[head, :], up[...]))
            sums[head, :] += dot(activated, down[...])

    if text:
        more = dot(gelu(dot(tails[...], up[...])), down[...])
        for seq in range(seqs):
            sums[pl.ds(seq * SEQ + HEAD, TAIL), :] += more[seq * TAIL : (seq + 1) * TAIL]

    @pl.when(step == pl.num_programs(0) - 1)
    def _():
        if text:
            out[...] = sums[...]
        else:
            for seq in range(seqs):
                put_rows(flat, sums[pl.ds(seq * SEQ, SEQ), :], seq)
            out[...] = flat[...].astype(BF16)


def whole(shape):
    return pl.BlockSpec(shape, lambda *_: (0,) * len(shape), pipeline_mode=pl.Buffered(1))


def by_step(shape):
    return pl.BlockSpec(shape, lambda i, *_: (i,) + (0,) * (len(shape) - 1))


ANY = pl.BlockSpec(memory_space=pl.ANY)


def call(kernel, steps, ins, in_specs, outs, out_specs, scratch, name):
    run = pl.pallas_call(
        kernel,
        out_shape=tuple(jax.ShapeDtypeStruct(s, d) for s, d in outs),
        grid_spec=pltpu.PrefetchScalarGridSpec(
            num_scalar_prefetch=1,
            grid=(steps,),
            in_specs=in_specs,
            out_specs=out_specs,
            scratch_shapes=scratch,
        ),
        compiler_params=pltpu.CompilerParams(vmem_limit_bytes=60 * MIB),
        cost_estimate=pl.CostEstimate(flops=1, bytes_accessed=1, transcendentals=0),
        name=name,
    )
    return run(*ins)


def lay(rows, seqs):
    rows = rows.reshape(seqs, LEN, -1)
    return jnp.concatenate(
        [
            jnp.pad(rows[:, :PATCHES], ((0, 0), (0, HEAD - PATCHES), (0, 0))),
            jnp.pad(rows[:, PATCHES:], ((0, 0), (0, TAIL - LEN + PATCHES), (0, 0))),
        ],
        1,
    ).reshape(seqs * SEQ, -1)


def tie(*trees):
    return lax.optimization_barrier(trees)


def in_order(rows, part, blocks=0, axis=0):
    rows = jnp.moveaxis(rows, axis, blocks)
    shape, columns = rows.shape[:blocks], rows.shape[-1]
    count, size = rows.shape[blocks], rows.shape[blocks + 1]
    if size == part:
        return rows.reshape(*shape, count * part, columns)
    up = rows[..., : 4 * part, :].reshape(*shape, count, 4, part, columns)
    up = jnp.swapaxes(up, blocks, blocks + 1).reshape(*shape, 4 * count * part, columns)
    down = rows[..., 4 * part :, :].reshape(*shape, count * (size - 4 * part), columns)
    return jnp.concatenate([up, down], -2)


class Cube:
    axes = ("y", "x", "core", "z")
    swap = [(0, 1), (1, 0)]

    def __init__(self):
        y, x, core, z = (lax.axis_index(a) for a in self.axes)
        self.z, self.core, self.flat = z, core, y * 2 + x
        self.index = ((y * 2 + x) * 2 + core) * 4 + z

    def turn(self, block, k):
        return lax.ppermute(block, "z", [(i, (i + k) % 4) for i in range(4)])

    def turns(self, block):
        return [block] + [self.turn(block, k) for k in (1, 2, 3)]

    def ring(self, ring, part):
        out = []
        for place in range(4):
            k = lax.rem(self.z + 4 - place, 4)
            out.append(
                jnp.where(
                    k == 0,
                    ring[0],
                    jnp.where(k == 1, ring[1], jnp.where(k == 2, ring[2], ring[3])),
                )
            )
        return in_order(jnp.stack(out), part)

    def swapped(self, block, axis):
        return lax.ppermute(block, axis, self.swap)

    def sides(self, own):
        return own, self.swapped(own, "x"), self.swapped(own, "y")

    def halves(self, near):
        half = near[0].shape[0] // 2
        return near[1][:half], near[2][half:]

    def to_corners(self, near, halves):
        return (*near, self.swapped(halves[0], "y"), self.swapped(halves[1], "x"))

    def corner(self, near):
        return self.to_corners(near, self.halves(near))

    def cores(self, near):
        return [*near] + [self.swapped(b, "core") for b in near]

    def plane(self, j, block):
        if j == 1:
            return self.swapped(block, "x")
        if j == 2:
            return self.swapped(block, "y")
        return lax.ppermute(block, ("y", "x"), [(i, 3 - i) for i in range(4)])

    def to_core(self, block):
        return self.swapped(block, "core")

    def far_sums(self, keep, got):
        half = got.shape[0] // 2
        return [
            (keep[3, at].astype(F32) + got[at].astype(F32)).astype(BF16)
            for at in (slice(half), slice(half, None))
        ]

    def to_corner(self, both):
        return self.swapped(both[0], "x"), self.swapped(both[1], "y")

    def side_sums(self, keep, got, corner):
        half = corner[0].shape[0]
        by_x = jnp.pad(corner[0], ((0, half), (0, 0))).astype(F32)
        by_y = jnp.pad(corner[1], ((half, 0), (0, 0))).astype(F32)
        to_x = keep[1].astype(F32) + got[1].astype(F32) + by_y
        to_y = keep[2].astype(F32) + got[2].astype(F32) + by_x
        return [keep, got, to_x.astype(BF16), to_y.astype(BF16)]

    def to_sides(self, sums):
        return [*sums[:2], self.swapped(sums[2], "x"), self.swapped(sums[3], "y")]

    def plane_sums(self, keep, got, rows):
        both = [keep[j, :rows].astype(F32) + got[j, :rows].astype(F32) for j in (1, 2, 3)]
        return [keep, got] + [b.astype(BF16) for b in both]

    def to_plane(self, sums):
        return sums[:2] + [self.plane(j, sums[j + 1]) for j in (1, 2, 3)]

    def last(self, near):
        return near[3:]

    def cores_of(self, near, last):
        return self.cores([*near[:3], *last])

    def far_cores(self, near):
        return [self.swapped(b, "core") for b in near]

    def rest_cores(self, near, far):
        return [*near, *far] + self.far_cores(near[len(far) :])

    def ring_sums(self, group, fields):
        keep, got, *more = group
        rows = more[0].shape[0]
        mine = sum(m.astype(F32) for m in (keep[0, :rows], got[0, :rows], *more))
        rounded = lax.optimization_barrier(mine.astype(BF16))
        return [cut(mine, fields, self.z)] + [
            cut(rounded, fields, lax.rem(self.z + k, 4)) for k in (1, 2, 3)
        ]

    def to_ring(self, parts, which):
        return [self.turn(p, k) if k in which else p for k, p in enumerate(parts)]

    def add_ring(self, ring):
        return ring[0] + sum(m.astype(F32) for m in ring[1:])


class Flat:
    axes = ("dp", "fsdp")

    def __init__(self, count):
        self.flat = self.core = jnp.int32(0)
        self.index = lax.axis_index(self.axes)
        self.count = count

    def turns(self, block):
        return lax.all_gather(block, self.axes, axis=0)

    def ring(self, full, part):
        return in_order(full.reshape((8, -1) + full.shape[1:]), part, 1, 1)

    def sides(self, own):
        return own

    def halves(self, near):
        return ()

    def to_corners(self, near, halves):
        return near

    def corner(self, near):
        return near

    def cores(self, near):
        half = near.shape[1] // 2
        out = []
        for side in range(2):
            out += [near[side], near[2 + side], near[4 + side]]
            out += [near[6 + side, :half], near[6 + side, half:]]
        return out

    def to_core(self, block):
        return block

    def far_sums(self, keep, got):
        return got

    def to_corner(self, both):
        return both

    def side_sums(self, keep, got, corner):
        return self.plane_sums(keep, jnp.concatenate([got, corner[None]]), None)

    def to_sides(self, sums):
        return sums

    def plane_sums(self, keep, got, rows):
        return [jnp.stack([keep, got], 1).reshape((8,) + keep.shape[1:])]

    def to_plane(self, sums):
        return sums

    def last(self, near):
        return ()

    def cores_of(self, near, last):
        return self.cores(near)

    def far_cores(self, near):
        return ()

    def rest_cores(self, near, far):
        return self.cores(near)

    def ring_sums(self, group, fields):
        ways = self.count // 8
        parts = [[cut(block, fields, w, ways) for w in range(ways)] for block in group[0]]
        return jnp.stack([p for block in parts for p in block]).astype(F32)

    def to_ring(self, parts, which):
        if 3 not in which:
            return parts
        return lax.psum_scatter(parts, self.axes, scatter_dimension=0, tiled=False)

    def add_ring(self, ring):
        return ring


def pack_expert(up, down):
    part = up.shape[0]
    up = up.reshape(part, 4, D).transpose(1, 0, 2).reshape(4 * part, D)
    return jnp.concatenate([up, down], 0)


def cut(rows, fields, place, ways=4):
    out, at = [], 0
    for groups, size in fields:
        part = rows[at : at + max(groups, 1) * size]
        at += max(groups, 1) * size
        if groups:
            part = part.reshape(groups, ways, size // ways, D)
            part = lax.dynamic_index_in_dim(part, place, 1, keepdims=False).reshape(-1, D)
        out.append(part)
    return jnp.concatenate(out)


def layer(
    make,
    tokens,
    modality,
    token_mask,
    cotangent,
    mask_vector,
    ln_one_gain,
    ln_one_shift,
    w_qkv,
    w_out,
    ln_two_gain,
    ln_two_shift,
    w_up,
    w_down,
):
    net = make()
    part = w_qkv.shape[0]
    seqs = tokens.shape[0] // LEN
    rows = seqs * SEQ
    columns = jnp.stack([ln_one_gain, ln_one_shift, ln_two_gain, ln_two_shift], 1)
    packed = jnp.concatenate([w_qkv, w_out, jnp.pad(columns, ((0, 0), (0, 124)))], 1)
    n_columns = packed.shape[1]
    ring = net.turns(packed)

    seq_masks = token_mask.reshape(seqs, LEN)
    masked = jnp.concatenate(
        [
            jnp.pad(seq_masks[:, :PATCHES], ((0, 0), (0, HEAD - PATCHES))),
            jnp.pad(seq_masks[:, PATCHES:], ((0, 0), (0, TAIL - LEN + PATCHES))),
        ],
        1,
    ).reshape(1, rows)
    order = jnp.cumsum(masked, 1)
    place = jnp.where(masked == 1, order - 1, -1)
    blocks = jnp.maximum((order[0, rows - 1] + BLK - 1) // BLK, 1)
    near = jnp.arange(8, dtype=jnp.int32)
    near = jnp.bitwise_xor(net.flat, near & 3) * 2 + jnp.bitwise_xor(net.core, near >> 2)
    where_ref = jnp.concatenate(
        [
            near,
            jnp.stack([net.core, net.flat, blocks]).astype(jnp.int32),
            modality.reshape(seqs, LEN)[:, 0],
        ]
    )
    tokens = lay(tokens, seqs)
    ring, where_ref, tokens = tie(ring, where_ref, tokens)

    own = net.ring(ring, part)
    near = net.sides(own)
    text, _ = tie(pack_expert(w_up[1], w_down[1]), own)
    ring_text = net.turns(text)
    masked = masked.astype(F32).reshape(rows, 1)
    cotangent = lay(cotangent, seqs)
    vector = mask_vector.astype(F32).reshape(1, D)
    near, masked, place, cotangent, vector = tie(near, masked, place, cotangent, vector)
    pieces = net.cores(net.corner(near))
    own_text = net.ring(ring_text, part)
    pieces, own_text, image = tie(pieces, own_text, pack_expert(w_up[0], w_down[0]))
    near_text = net.sides(own_text)
    image = net.turns(image)

    def feed(text, before, weights):
        return call(
            functools.partial(feed_kernel, text),
            4,
            (where_ref, normed_two, before, *weights),
            [whole((rows, D)), whole((rows, D))] + [ANY] * 10,
            [((rows, D), F32) if text else ((seqs * LEN, D), BF16)],
            [whole((rows if text else seqs * LEN, D))],
            [
                pltpu.VMEM((rows, D), F32),
                pltpu.VMEM((4, D, D), BF16),
                pltpu.VMEM((FF, D), BF16),
                pltpu.SemaphoreType.DMA((40,)),
                pltpu.VMEM((seqs * TAIL, D), BF16) if text else pltpu.VMEM((seqs * LEN, D), F32),
            ],
            "feed_text" if text else "feed_image",
        )[0]

    qkv, softs, context, hidden, normed_one, normed_two, params = call(
        attention_kernel,
        seqs,
        (where_ref, tokens, masked, vector, *pieces),
        [by_step((SEQ, D)), by_step((SEQ, 1)), whole((1, D))] + [ANY] * 10,
        [
            ((rows, 3 * D), BF16),
            ((seqs, H // 2, SEQ, 2 * SEQ), F32),
            ((rows, D), BF16),
            ((rows, D), F32),
            ((rows, D), BF16),
            ((rows, D), BF16),
            ((8, D), F32),
        ],
        [
            by_step((SEQ, 3 * D)),
            by_step((1, H // 2, SEQ, 2 * SEQ)),
            by_step((SEQ, D)),
            by_step((SEQ, D)),
            by_step((SEQ, D)),
            by_step((SEQ, D)),
            pl.BlockSpec((8, D), lambda i, *_: (0, 0)),
        ],
        [pltpu.VMEM((D, n_columns), BF16), pltpu.SemaphoreType.DMA((10,))],
        "attention",
    )

    near_text, image, (qkv, softs, context, hidden, normed_one, normed_two, params) = tie(
        near_text, image, (qkv, softs, context, hidden, normed_one, normed_two, params)
    )
    near_text = net.corner(near_text)
    last, image = tie(net.last(near_text), net.ring(image, part))
    pieces_text = net.cores_of(near_text, last)
    image, pieces_text = tie(image, pieces_text)
    near_image = net.sides(image)

    block = (ROWS_ONE, D)
    keep, send, send_far, grad_context, sums = call(
        feed_back_kernel,
        4,
        (where_ref, place, hidden, cotangent, context, params, *pieces_text, *pieces),
        [whole((1, rows)), whole((rows, D)), whole((rows, D)), whole((rows, D)), whole((8, D))]
        + [ANY] * 20,
        [((4, *block), BF16), ((3, *block), BF16), (block, BF16), ((rows, D), BF16), ((8, D), F32)],
        [ANY] * 3 + [whole((rows, D)), whole((8, D))],
        [pltpu.VMEM((rows, D), BF16)] * 3
        + [
            pltpu.VMEM((rows, D), F32),
            pltpu.VMEM((rows, D), BF16),
            pltpu.VMEM((rows, D), BF16),
            pltpu.VMEM((rows, D), F32),
        ]
        + [pltpu.VMEM((D, D), F32)] * 2
        + [
            pltpu.VMEM((4, D, D), BF16),
            pltpu.VMEM((FF, D), BF16),
            pltpu.VMEM((D, D), BF16),
            pltpu.VMEM((2, 4, *block), BF16),
            pltpu.SemaphoreType.DMA((40,)),
            pltpu.SemaphoreType.DMA((10,)),
            pltpu.SemaphoreType.DMA((5, 5)),
        ],
        "feed_back",
    )
    near_image, keep, send, send_far, grad_context, sums = tie(
        near_image, keep, send, send_far, grad_context, sums
    )
    far = net.far_sums(keep, net.to_core(send_far))
    halves_image = net.halves(near_image)
    far, send, hidden, halves_image = tie(far, send, hidden, halves_image)
    got = net.to_core(send)
    corner = net.to_corner(far)
    near_image = net.to_corners(near_image, halves_image)
    after = feed(True, hidden, pieces_text)
    corner, got, near_image, after = tie(corner, got, near_image, after)
    sums_feed = net.side_sums(keep, got, corner)
    sums_feed, grad_context = tie(sums_feed, grad_context)
    sums_feed = net.to_sides(sums_feed)
    far_image = net.far_cores(near_image[:3])

    keep, send, grad_tokens = call(
        attention_back_kernel,
        seqs,
        (where_ref, qkv, softs, grad_context, normed_one, tokens, masked, vector, params, sums)
        + tuple(pieces),
        [
            by_step((SEQ, 3 * D)),
            by_step((1, H // 2, SEQ, 2 * SEQ)),
            by_step((SEQ, D)),
            whole((rows, D)),
            by_step((SEQ, D)),
            by_step((SEQ, 1)),
            whole((1, D)),
            whole((8, D)),
            whole((8, D)),
        ]
        + [ANY] * 10,
        [((4, ROWS_QKV, D), BF16), ((4, ROWS_QKV, D), BF16), ((seqs * LEN, D), F32)],
        [ANY, ANY, whole((seqs * LEN, D))],
        [
            pltpu.VMEM((D, 3 * D), BF16),
            pltpu.VMEM((8, D), F32),
            pltpu.VMEM((rows, 3 * D), BF16),
            pltpu.VMEM((8, ROWS_QKV, D), BF16),
            pltpu.SemaphoreType.DMA((10,)),
            pltpu.SemaphoreType.DMA((8,)),
        ],
        "attention_back",
    )
    keep, send, grad_tokens, sums_feed, far_image = tie(
        keep, send, grad_tokens, sums_feed, far_image
    )
    got = net.to_core(send)
    pieces_image = net.rest_cores(near_image, far_image)
    sums_qkv = net.plane_sums(keep, got, 296)
    ring_one = net.ring_sums(sums_feed, [(4, 96), (1, 384), (1, 96)])
    sums_qkv, ring_one, after, pieces_image = tie(sums_qkv, ring_one, after, pieces_image)
    sums_qkv = net.to_plane(sums_qkv)
    ring_one = net.to_ring(ring_one, (1, 2))
    output = feed(False, after, pieces_image)
    sums_qkv, ring_one, output = tie(sums_qkv, ring_one, output)
    ring_two = net.ring_sums(sums_qkv, [(3, 96), (0, 8)])
    ring_one = net.to_ring(ring_one, (3,))
    ring_two = net.to_ring(ring_two, (1, 2, 3))

    grads = net.add_ring(ring_one)
    grad_w_up = grads[: 4 * part].reshape(4, part, D).transpose(1, 0, 2).reshape(part, FF)
    grad_w_down = grads[4 * part : 8 * part]
    grad_w_out = grads[8 * part : 9 * part]
    grads = net.add_ring(ring_two)
    grad_w_qkv = grads[: 3 * part].reshape(3, part, D).transpose(1, 0, 2).reshape(part, 3 * D)
    extra = grads[3 * part :]

    def own(vector):
        return lax.dynamic_slice_in_dim(vector, net.index * part, part)

    return (
        output,
        grad_tokens,
        extra[2],
        own(extra[3]),
        own(extra[4]),
        grad_w_qkv,
        grad_w_out,
        own(extra[0]),
        own(extra[1]),
        grad_w_up,
        grad_w_down,
    )


def solution(mesh):
    if (mesh.shape["dp"], mesh.shape["fsdp"]) == (8, 4):
        mesh = Mesh(mesh.devices.reshape(2, 2, 2, 4), Cube.axes)
        make = Cube
    else:
        make = functools.partial(Flat, mesh.size)
    axes = Cube.axes if make is Cube else Flat.axes
    row, flat = P(axes, None), P(axes)
    middle = P(None, axes, None)
    in_specs = (row, flat, flat, row, P(), flat, flat, row, row, flat, flat, middle, middle)
    out_specs = (row, row, P(), flat, flat, row, row, flat, flat, row, row)
    return jax.shard_map(
        functools.partial(layer, make),
        mesh=mesh,
        in_specs=in_specs,
        out_specs=out_specs,
        check_vma=False,
    )
```

```python
import functools
import math

import jax
import jax.numpy as jnp
from jax import lax
from jax.experimental import pallas as pl
from jax.experimental.pallas import tpu as pltpu
from jax.sharding import Mesh, PartitionSpec as P

H = 12
HD = 64
LEN = 237
PATCHES = 197
HEAD = 208
TAIL = 48
SEQ = HEAD + TAIL
D = H * HD
FF = 4 * D
BLK = 256
EPS = 1e-05
F32 = jnp.float32
BF16 = jnp.bfloat16
MIB = 1 << 20
ROWS_ONE = 864
ROWS_QKV = 304


def dot(a, b):
    return jnp.dot(a, b, preferred_element_type=F32)


def dot_nt(a, b):
    return lax.dot_general(a, b, (((1,), (1,)), ((), ())), preferred_element_type=F32)


def dot_tn(a, b):
    return lax.dot_general(a, b, (((0,), (0,)), ((), ())), preferred_element_type=F32)


def mean(rows):
    return jnp.mean(rows, -1, keepdims=True)


def normalize(rows):
    centred = rows - mean(rows)
    inverse = lax.rsqrt(mean(centred * centred) + EPS)
    return centred * inverse, inverse


def normalize_back(grad, unit, inverse, gain):
    scaled = grad * gain
    return inverse * (scaled - mean(scaled) - unit * mean(scaled * unit))


def total(rows):
    return jnp.sum(rows, 0, keepdims=True)


def halves(pair):
    lane = lax.broadcasted_iota(jnp.int32, pair.shape, 1)
    zero = jnp.zeros_like(pair)
    return jnp.concatenate(
        [jnp.where(lane < HD, pair, zero), jnp.where(lane < HD, zero, pair)], 0
    )


def key_bias():
    key = lax.broadcasted_iota(jnp.int32, (1, SEQ), 1)
    valid = (key < PATCHES) | ((key >= HEAD) & (key < HEAD + LEN - PATCHES))
    return jnp.where(valid, 0.0, -1e30)


def softmax_pair(queries, keys_cat, bias):
    scores = dot_nt(queries, keys_cat)
    out = []
    for head in range(2):
        own = scores[:, head * SEQ : (head + 1) * SEQ] + bias
        powers = jnp.exp(own - jnp.max(own, -1, keepdims=True))
        out.append(powers * (1.0 / jnp.sum(powers, -1, keepdims=True)))
    return jnp.concatenate(out, 1)


def spans(where_ref, pieces, rows):
    if len(pieces) == 8:
        for j in range(8):
            yield pieces[j], where_ref[j], 0, rows
        return
    for side in range(2):
        for j in range(5):
            block = where_ref[4 * side + min(j, 3)]
            size = rows if j < 3 else rows // 2
            yield pieces[5 * side + j], block, (size if j == 4 else 0), size


def started(copies, sems, start=True):
    copies = [
        pltpu.make_async_copy(source, target, sems.at[j])
        for j, (source, target) in enumerate(copies)
    ]
    if start:
        for copy in copies:
            copy.start()
    return copies


def load_pieces(where_ref, pieces, target, sems, columns, start=True):
    return started(
        [
            (
                piece.at[:, pl.ds(columns[0], columns[1])],
                target.at[pl.ds(pl.multiple_of(block * 96 + first, 16), size), :],
            )
            for piece, block, first, size in spans(where_ref, pieces, 96)
        ],
        sems,
        start,
    )


def load_expert(where_ref, pieces, up, down, sems):
    copies = []
    for piece, block, first, size in spans(where_ref, pieces, 768):
        if first == 0:
            for chunk in range(4):
                copies.append(
                    (
                        piece.at[pl.ds(chunk * 96, 96), :],
                        up.at[chunk, pl.ds(pl.multiple_of(block * 96, 96), 96), :],
                    )
                )
        if first + size == 768:
            copies.append(
                (
                    piece.at[pl.ds(384 - first, 384), :],
                    down.at[pl.ds(pl.multiple_of(block * 384, 384), 384), :],
                )
            )
    return started(copies, sems)


def wait_all(copies):
    for copy in copies:
        copy.wait()


def attention_kernel(where_ref, tokens, masked, vector, *rest):
    pieces, rest = rest[:8], rest[8:]
    qkv, softs, context, normed_one, params, weights, sems = rest

    @pl.when(pl.program_id(0) == 0)
    def _():
        wait_all(load_pieces(where_ref, pieces, weights, sems, (0, weights.shape[1])))
        columns = weights[:, 4 * D : 4 * D + 128].astype(F32)
        params[...] = jnp.transpose(columns)[:8]

    start = jnp.where(masked[...] == 1.0, vector[...], tokens[...].astype(F32))
    unit, _ = normalize(start)
    first = (unit * params[0:1] + params[1:2]).astype(BF16)
    normed_one[...] = first
    for third in range(3):
        at = pl.ds(third * D, D)
        qkv[:, at] = dot(first, weights[:, at]).astype(BF16)
    bias = key_bias()
    for pair in range(H // 2):
        queries = qkv[:, pl.ds(pair * 128, 128)] * BF16(1.0 / math.sqrt(HD))
        keys = halves(qkv[:, pl.ds(D + pair * 128, 128)])
        values = halves(qkv[:, pl.ds(2 * D + pair * 128, 128)])
        soft = softmax_pair(queries, keys, bias)
        softs[0, pair] = soft
        attention = soft.astype(BF16)
        context[:, pl.ds(pair * 128, 128)] = dot(attention, values).astype(BF16)


def chosen(place, block):
    row = lax.broadcasted_iota(jnp.int32, (BLK, place.shape[1]), 0) + block * BLK
    return jnp.where(row == place[...], 1.0, 0.0).astype(BF16)


def rows_of(block):
    return pl.ds(pl.multiple_of(block * BLK, BLK), BLK)


def feed_back_kernel(where_ref, place, vector, cotangent, context, params, *rest):
    pieces, attention_pieces, rest = rest[:10], rest[10:18], rest[18:]
    keep, send, send_far, grad_context, sums = rest[:5]
    rows_two, rows_hidden, rows_cot, rows_context, grad_two = rest[5:10]
    (sum_up, sum_down, w_up, w_down, w_out, stage) = rest[10:16]
    sems, attention_sems, out_sems = rest[16:]
    step = pl.program_id(0)
    blocks = where_ref[10]
    core = where_ref[8]

    @pl.when(step == 0)
    def _():
        copies = load_pieces(where_ref, attention_pieces, w_out, attention_sems, (3 * D, D))
        more = load_expert(where_ref, pieces, w_up, w_down, sems)

        def gather(block, _):
            pick, at = chosen(place, block), rows_of(block)
            rows_cot[at, :] = dot(pick, cotangent[...]).astype(BF16)
            rows_context[at, :] = dot(pick, context[...]).astype(BF16)
            grad_two[at, :] = jnp.zeros((BLK, D), F32)
            return 0

        def norm(block, _):
            at = rows_of(block)
            rows = vector[...] + dot(rows_context[at, :], w_out[...])
            rows_hidden[at, :] = rows
            unit, _ = normalize(rows)
            rows_two[at, :] = (unit * params[2:3] + params[3:4]).astype(BF16)
            return 0

        lax.fori_loop(0, blocks, gather, 0)
        wait_all(copies)
        lax.fori_loop(0, blocks, norm, 0)
        wait_all(more)

    up = w_up.at[step]
    down = w_down.at[pl.ds(pl.multiple_of(step * D, D), D), :]

    def expert(block, _):
        at = rows_of(block)
        rows, grads = rows_two[at, :], rows_cot[at, :]
        pre = dot(rows, up[...])
        chance = 0.5 * (1.0 + lax.erf(pre * math.sqrt(0.5)))
        activated = (pre * chance).astype(BF16)
        slope = chance + pre * (jnp.exp(-0.5 * pre * pre) * (1.0 / math.sqrt(2.0 * math.pi)))
        grad_pre = (dot_nt(grads, down[...]) * slope).astype(BF16)
        grad_two[at, :] += dot_nt(grad_pre, up[...])
        add_down = dot_tn(activated, grads)
        add_up = dot_tn(rows, grad_pre)

        @pl.when(block == 0)
        def _():
            sum_down[...] = add_down
            sum_up[...] = add_up

        @pl.when(block > 0)
        def _():
            sum_down[...] += add_down
            sum_up[...] += add_up

        return 0

    lax.fori_loop(0, blocks, expert, 0)

    def leaving(at_step):
        rows = pl.ds(pl.multiple_of(at_step * 96, 96), 96)
        columns = pl.ds(384, 384)
        mine = jnp.bitwise_xor(at_step, where_ref[9])
        near = jnp.minimum(mine, 2)
        sem = out_sems.at[at_step]
        return [
            (None, stage.at[0, :, rows, :], keep.at[:, rows, :], sem.at[0]),
            (None, stage.at[0, mine, columns, :], keep.at[mine, columns, :], sem.at[1]),
            (None, stage.at[1, pl.ds(0, 3), rows, :], send.at[:, rows, :], sem.at[2]),
            (None, stage.at[1, 3, rows, :], send_far.at[rows, :], sem.at[3]),
            (mine < 3, stage.at[1, near, columns, :], send.at[near, columns, :], sem.at[4]),
            (mine == 3, stage.at[1, 3, columns, :], send_far.at[columns, :], sem.at[4]),
        ]

    def each(copies, act):
        for when, source, target, sem in copies:
            copy = pltpu.make_async_copy(source, target, sem)
            if when is None:
                act(copy)
            else:
                pl.when(when)(functools.partial(act, copy))

    up_at = pl.ds(pl.multiple_of(step * 96, 96), 96)
    mine = jnp.bitwise_xor(step, where_ref[9])
    for side in range(2):
        for j in range(4):
            source = pl.ds(pl.multiple_of(where_ref[4 * side + j] * 96, 96), 96)
            stage[side, j, up_at, :] = sum_up[source, :].astype(BF16)
        half = core if side == 0 else 1 - core
        source = pl.ds(pl.multiple_of(half * 384, 384), 384)
        stage[side, mine, pl.ds(384, 384), :] = sum_down[source, :].astype(BF16)
    each(leaving(step), lambda copy: copy.start())

    @pl.when(step == pl.num_programs(0) - 1)
    def _():
        sums[...] = jnp.zeros_like(sums)

        def back(block, _):
            pick, at = chosen(place, block), rows_of(block)
            unit, inverse = normalize(rows_hidden[at, :])
            grad = grad_two[at, :]
            grad_hidden = rows_cot[at, :].astype(F32) + normalize_back(
                grad, unit, inverse, params[2:3]
            )
            sums[0:1] += total(grad * unit)
            sums[1:2] += total(grad)
            sums[2:3] += total(grad_hidden)
            grad_attn = grad_hidden.astype(BF16)
            add_out = dot_tn(rows_context[at, :], grad_attn)
            rows = dot_nt(grad_attn, w_out[...]).astype(BF16)
            rows = dot_tn(pick, rows).astype(BF16)

            @pl.when(block == 0)
            def _():
                sum_up[...] = add_out
                grad_context[...] = rows

            @pl.when(block > 0)
            def _():
                sum_up[...] += add_out
                grad_context[...] += rows

            return 0

        lax.fori_loop(0, blocks, back, 0)
        for side in range(2):
            for j in range(4):
                source = pl.ds(pl.multiple_of(where_ref[4 * side + j] * 96, 96), 96)
                stage[side, j, pl.ds(768, 96), :] = sum_up[source, :].astype(BF16)
        rows = pl.ds(768, 96)
        sem = out_sems.at[4]
        last = [
            (None, stage.at[0, :, rows, :], keep.at[:, rows, :], sem.at[0]),
            (None, stage.at[1, pl.ds(0, 3), rows, :], send.at[:, rows, :], sem.at[1]),
            (None, stage.at[1, 3, rows, :], send_far.at[rows, :], sem.at[2]),
        ]
        each(last, lambda copy: copy.start())
        each(last, lambda copy: copy.wait())
        for at_step in range(4):
            each(leaving(at_step), lambda copy: copy.wait())


def put_rows(target, rows, seq):
    target[seq * LEN : seq * LEN + PATCHES] = rows[:PATCHES]
    target[seq * LEN + PATCHES : (seq + 1) * LEN] = rows[HEAD : HEAD + LEN - PATCHES]


def attention_back_kernel(
    where_ref, qkv, softs, grad_context, normed_one, tokens, masked, vector, params, before, *rest
):
    pieces = rest[:8]
    keep, send, grad_tokens = rest[8:11]
    weights, sums, grad_qkv, stage, sems, out_sems = rest[11:]
    step = pl.program_id(0)
    here = pl.ds(pl.multiple_of(step * SEQ, SEQ), SEQ)

    def copies():
        return load_pieces(where_ref, pieces, weights, sems, (0, 3 * D), False)

    @pl.when(step == 0)
    def _():
        for copy in copies():
            copy.start()
        sums[...] = before[...]

    inv_root = 1.0 / math.sqrt(HD)
    top = lax.broadcasted_iota(jnp.int32, (128, SEQ), 0) < HD
    for pair in range(H // 2):
        queries = qkv[:, pl.ds(pair * 128, 128)]
        keys = halves(qkv[:, pl.ds(D + pair * 128, 128)])
        values = halves(qkv[:, pl.ds(2 * D + pair * 128, 128)])
        grads = grad_context[:, pl.ds(pair * 128, 128)]
        grad_soft = dot_nt(grads, values)
        parts = []
        for head in range(2):
            span = slice(head * SEQ, (head + 1) * SEQ)
            own, grad = softs[0, pair, :, span], grad_soft[:, span]
            parts.append(own * (grad - jnp.sum(own * grad, -1, keepdims=True)))
        grad_scores = jnp.concatenate(parts, 1).astype(BF16)
        grad_qkv[here, pl.ds(pair * 128, 128)] = (dot(grad_scores, keys) * inv_root).astype(BF16)
        by_key = dot_tn(queries, grad_scores) * inv_root
        by_key = jnp.where(top, by_key[:, :SEQ], by_key[:, SEQ:])
        grad_qkv[here, pl.ds(D + pair * 128, 128)] = jnp.transpose(by_key).astype(BF16)
        by_value = dot_tn(grads, softs[0, pair].astype(BF16))
        by_value = jnp.where(top, by_value[:, :SEQ], by_value[:, SEQ:])
        grad_qkv[here, pl.ds(2 * D + pair * 128, 128)] = jnp.transpose(by_value).astype(BF16)

    @pl.when(step == 0)
    def _():
        wait_all(copies())

    grad_one = dot_nt(grad_qkv[here, :], weights[...])
    start = jnp.where(masked[...] == 1.0, vector[...], tokens[...].astype(F32))
    unit, inverse = normalize(start)
    grad_start = normalize_back(grad_one, unit, inverse, params[0:1])
    sums[3:4] += total(grad_one * unit)
    sums[4:5] += total(grad_one)
    sums[2:3] += total(jnp.where(masked[...] == 1.0, grad_start, 0.0))
    kept = jnp.where(masked[...] == 1.0, 0.0, grad_start)
    for seq in range(normed_one.shape[0] // SEQ):
        pl.when(step == seq)(functools.partial(put_rows, grad_tokens, kept, seq))

    @pl.when(step == pl.num_programs(0) - 1)
    def _():
        extra = jnp.concatenate([sums[...], jnp.zeros_like(sums[...])], 0).astype(BF16)
        for third in range(3):
            for part in range(3):
                at = pl.ds(third * D + part * SEQ, SEQ)
                add = dot_tn(normed_one[...], grad_qkv[:, at]).astype(BF16)
                for block in range(8):
                    stage[block, pl.ds(third * 96, 96), pl.ds(part * SEQ, SEQ)] = add[
                        block * 96 : (block + 1) * 96
                    ]
        out_copies = []
        for side, out in enumerate((keep, send)):
            for j in range(4):
                block = where_ref[4 * side + j]
                stage[block, pl.ds(3 * 96, 16), :] = extra
                out_copies.append((stage.at[block], out.at[j]))
        wait_all(started(out_copies, out_sems))


def gelu(pre):
    return (pre * (0.5 * (1.0 + lax.erf(pre * math.sqrt(0.5))))).astype(BF16)


def feed(text, where_ref, rows_in, sums, up, down, tails):
    seqs = rows_in.shape[0] // SEQ
    for seq in range(seqs):
        head = pl.ds(seq * SEQ, HEAD)

        @pl.when(where_ref[11 + seq] == int(text))
        def _():
            activated = gelu(dot(rows_in[head, :], up[...]))
            sums[head, :] += dot(activated, down[...])

    if text:
        more = dot(gelu(dot(tails[...], up[...])), down[...])
        for seq in range(seqs):
            sums[pl.ds(seq * SEQ + HEAD, TAIL), :] += more[seq * TAIL : (seq + 1) * TAIL]


def feed_text_kernel(where_ref, tokens, masked, vector, context, params, *rest):
    pieces, attention_pieces, rest = rest[:10], rest[10:18], rest[18:]
    out, normed_two, w_up, w_down, w_out, sems, attention_sems, tails = rest
    step = pl.program_id(0)

    @pl.when(step == 0)
    def _():
        copies = load_pieces(where_ref, attention_pieces, w_out, attention_sems, (3 * D, D))
        more = load_expert(where_ref, pieces, w_up, w_down, sems)
        wait_all(copies)
        for seq in range(tokens.shape[0] // SEQ):
            at = pl.ds(seq * SEQ, SEQ)
            start = jnp.where(masked[at, :] == 1.0, vector[...], tokens[at, :].astype(F32))
            hidden = start + dot(context[at, :], w_out[...])
            out[at, :] = hidden
            unit, _ = normalize(hidden)
            second = (unit * params[2:3] + params[3:4]).astype(BF16)
            normed_two[at, :] = second
            tails[pl.ds(seq * TAIL, TAIL), :] = second[HEAD:]
        wait_all(more)

    down = w_down.at[pl.ds(pl.multiple_of(step * D, D), D), :]
    feed(True, where_ref, normed_two, out, w_up.at[step], down, tails)


def feed_image_kernel(where_ref, rows_in, before, *rest):
    pieces, (out, sums, w_up, w_down, sems, flat) = rest[:10], rest[10:]
    step = pl.program_id(0)

    @pl.when(step == 0)
    def _():
        copies = load_expert(where_ref, pieces, w_up, w_down, sems)
        sums[...] = before[...]
        wait_all(copies)

    down = w_down.at[pl.ds(pl.multiple_of(step * D, D), D), :]
    feed(False, where_ref, rows_in, sums, w_up.at[step], down, None)

    @pl.when(step == pl.num_programs(0) - 1)
    def _():
        for seq in range(rows_in.shape[0] // SEQ):
            put_rows(flat, sums[pl.ds(seq * SEQ, SEQ), :], seq)
        out[...] = flat[...].astype(BF16)


def whole(shape):
    return pl.BlockSpec(shape, lambda *_: (0,) * len(shape), pipeline_mode=pl.Buffered(1))


def by_step(shape):
    return pl.BlockSpec(shape, lambda i, *_: (i,) + (0,) * (len(shape) - 1))


ANY = pl.BlockSpec(memory_space=pl.ANY)


def call(kernel, steps, ins, in_specs, outs, out_specs, scratch, name):
    run = pl.pallas_call(
        kernel,
        out_shape=tuple(jax.ShapeDtypeStruct(s, d) for s, d in outs),
        grid_spec=pltpu.PrefetchScalarGridSpec(
            num_scalar_prefetch=1,
            grid=(steps,),
            in_specs=in_specs,
            out_specs=out_specs,
            scratch_shapes=scratch,
        ),
        compiler_params=pltpu.CompilerParams(vmem_limit_bytes=60 * MIB),
        cost_estimate=pl.CostEstimate(flops=1, bytes_accessed=1, transcendentals=0),
        name=name,
    )
    return run(*ins)


def lay(rows, seqs):
    rows = rows.reshape(seqs, LEN, -1)
    return jnp.concatenate(
        [
            jnp.pad(rows[:, :PATCHES], ((0, 0), (0, HEAD - PATCHES), (0, 0))),
            jnp.pad(rows[:, PATCHES:], ((0, 0), (0, TAIL - LEN + PATCHES), (0, 0))),
        ],
        1,
    ).reshape(seqs * SEQ, -1)


def tie(*trees):
    return lax.optimization_barrier(trees)


def in_order(rows, part, blocks=0, axis=0):
    rows = jnp.moveaxis(rows, axis, blocks)
    shape, columns = rows.shape[:blocks], rows.shape[-1]
    count, size = rows.shape[blocks], rows.shape[blocks + 1]
    if size == part:
        return rows.reshape(*shape, count * part, columns)
    up = rows[..., : 4 * part, :].reshape(*shape, count, 4, part, columns)
    up = jnp.swapaxes(up, blocks, blocks + 1).reshape(*shape, 4 * count * part, columns)
    down = rows[..., 4 * part :, :].reshape(*shape, count * (size - 4 * part), columns)
    return jnp.concatenate([up, down], -2)


class Cube:
    axes = ("y", "x", "core", "z")
    swap = [(0, 1), (1, 0)]

    def __init__(self):
        y, x, core, z = (lax.axis_index(a) for a in self.axes)
        self.z, self.core, self.flat = z, core, y * 2 + x
        self.index = ((y * 2 + x) * 2 + core) * 4 + z

    def turn(self, block, k):
        return lax.ppermute(block, "z", [(i, (i + k) % 4) for i in range(4)])

    def turns(self, block):
        return [block] + [self.turn(block, k) for k in (1, 2, 3)]

    def ring(self, ring, part):
        out = []
        for place in range(4):
            k = lax.rem(self.z + 4 - place, 4)
            out.append(
                jnp.where(
                    k == 0,
                    ring[0],
                    jnp.where(k == 1, ring[1], jnp.where(k == 2, ring[2], ring[3])),
                )
            )
        return in_order(jnp.stack(out), part)

    def swapped(self, block, axis):
        return lax.ppermute(block, axis, self.swap)

    def sides(self, own):
        return own, self.swapped(own, "x"), self.swapped(own, "y")

    def halves(self, near):
        half = near[0].shape[0] // 2
        return near[1][:half], near[2][half:]

    def to_corners(self, near, halves):
        return (*near, self.swapped(halves[0], "y"), self.swapped(halves[1], "x"))

    def corner(self, near):
        return self.to_corners(near, self.halves(near))

    def cores(self, near):
        return [*near] + [self.swapped(b, "core") for b in near]

    def plane(self, j, block):
        if j == 1:
            return self.swapped(block, "x")
        if j == 2:
            return self.swapped(block, "y")
        return lax.ppermute(block, ("y", "x"), [(i, 3 - i) for i in range(4)])

    def to_core(self, block):
        return self.swapped(block, "core")

    def far_sums(self, keep, got):
        half = got.shape[0] // 2
        return [
            (keep[3, at].astype(F32) + got[at].astype(F32)).astype(BF16)
            for at in (slice(half), slice(half, None))
        ]

    def to_corner(self, both):
        return self.swapped(both[0], "x"), self.swapped(both[1], "y")

    def side_sums(self, keep, got, corner):
        half = corner[0].shape[0]
        by_x = jnp.pad(corner[0], ((0, half), (0, 0))).astype(F32)
        by_y = jnp.pad(corner[1], ((half, 0), (0, 0))).astype(F32)
        to_x = keep[1].astype(F32) + got[1].astype(F32) + by_y
        to_y = keep[2].astype(F32) + got[2].astype(F32) + by_x
        return [keep, got, to_x.astype(BF16), to_y.astype(BF16)]

    def to_sides(self, sums):
        return [*sums[:2], self.swapped(sums[2], "x"), self.swapped(sums[3], "y")]

    def plane_sums(self, keep, got, rows):
        both = [keep[j, :rows].astype(F32) + got[j, :rows].astype(F32) for j in (1, 2, 3)]
        return [keep, got] + [b.astype(BF16) for b in both]

    def to_plane(self, sums):
        return sums[:2] + [self.plane(j, sums[j + 1]) for j in (1, 2, 3)]

    def square(self, own):
        return [own] + [self.plane(j, own) for j in (1, 2, 3)]

    def square_cores(self, near):
        return [*near] + [self.swapped(b, "core") for b in near]

    def last(self, near):
        return near[3:]

    def cores_of(self, near, last):
        return self.cores([*near[:3], *last])

    def far_cores(self, near):
        return [self.swapped(b, "core") for b in near]

    def all_cores(self, near, far, last):
        return [*near, *far, *last]

    def ring_sums(self, group, fields):
        keep, got, *more = group
        rows = more[0].shape[0]
        mine = sum(m.astype(F32) for m in (keep[0, :rows], got[0, :rows], *more))
        rounded = lax.optimization_barrier(mine.astype(BF16))
        return [cut(mine, fields, self.z)] + [
            cut(rounded, fields, lax.rem(self.z + k, 4)) for k in (1, 2, 3)
        ]

    def to_ring(self, parts, which):
        return [self.turn(p, k) if k in which else p for k, p in enumerate(parts)]

    def add_ring(self, ring):
        return ring[0] + sum(m.astype(F32) for m in ring[1:])


class Flat:
    axes = ("dp", "fsdp")

    def __init__(self, count):
        self.flat = self.core = jnp.int32(0)
        self.index = lax.axis_index(self.axes)
        self.count = count

    def turns(self, block):
        return lax.all_gather(block, self.axes, axis=0)

    def ring(self, full, part):
        return in_order(full.reshape((8, -1) + full.shape[1:]), part, 1, 1)

    def sides(self, own):
        return own

    def halves(self, near):
        return ()

    def to_corners(self, near, halves):
        return near

    def corner(self, near):
        return near

    def cores(self, near):
        half = near.shape[1] // 2
        out = []
        for side in range(2):
            out += [near[side], near[2 + side], near[4 + side]]
            out += [near[6 + side, :half], near[6 + side, half:]]
        return out

    def to_core(self, block):
        return block

    def far_sums(self, keep, got):
        return got

    def to_corner(self, both):
        return both

    def side_sums(self, keep, got, corner):
        return self.plane_sums(keep, jnp.concatenate([got, corner[None]]), None)

    def to_sides(self, sums):
        return sums

    def plane_sums(self, keep, got, rows):
        return [jnp.stack([keep, got], 1).reshape((8,) + keep.shape[1:])]

    def to_plane(self, sums):
        return sums

    def square(self, own):
        return own

    def square_cores(self, near):
        return [near[b] for b in (0, 2, 4, 6, 1, 3, 5, 7)]

    def last(self, near):
        return ()

    def cores_of(self, near, last):
        return self.cores(near)

    def far_cores(self, near):
        return ()

    def all_cores(self, near, far, last):
        return self.cores(near)

    def ring_sums(self, group, fields):
        ways = self.count // 8
        parts = [[cut(block, fields, w, ways) for w in range(ways)] for block in group[0]]
        return jnp.stack([p for block in parts for p in block]).astype(F32)

    def to_ring(self, parts, which):
        if 3 not in which:
            return parts
        return lax.psum_scatter(parts, self.axes, scatter_dimension=0, tiled=False)

    def add_ring(self, ring):
        return ring


def pack_expert(up, down):
    part = up.shape[0]
    up = up.reshape(part, 4, D).transpose(1, 0, 2).reshape(4 * part, D)
    return jnp.concatenate([up, down], 0)


def cut(rows, fields, place, ways=4):
    out, at = [], 0
    for groups, size in fields:
        part = rows[at : at + max(groups, 1) * size]
        at += max(groups, 1) * size
        if groups:
            part = part.reshape(groups, ways, size // ways, D)
            part = lax.dynamic_index_in_dim(part, place, 1, keepdims=False).reshape(-1, D)
        out.append(part)
    return jnp.concatenate(out)


def layer(
    make,
    tokens,
    modality,
    token_mask,
    cotangent,
    mask_vector,
    ln_one_gain,
    ln_one_shift,
    w_qkv,
    w_out,
    ln_two_gain,
    ln_two_shift,
    w_up,
    w_down,
):
    net = make()
    part = w_qkv.shape[0]
    seqs = tokens.shape[0] // LEN
    rows = seqs * SEQ
    columns = jnp.stack([ln_one_gain, ln_one_shift, ln_two_gain, ln_two_shift], 1)
    packed = jnp.concatenate([w_qkv, w_out, jnp.pad(columns, ((0, 0), (0, 124)))], 1)
    n_columns = packed.shape[1]
    ring = net.turns(packed)

    seq_masks = token_mask.reshape(seqs, LEN)
    masked = jnp.concatenate(
        [
            jnp.pad(seq_masks[:, :PATCHES], ((0, 0), (0, HEAD - PATCHES))),
            jnp.pad(seq_masks[:, PATCHES:], ((0, 0), (0, TAIL - LEN + PATCHES))),
        ],
        1,
    ).reshape(1, rows)
    order = jnp.cumsum(masked, 1)
    place = jnp.where(masked == 1, order - 1, -1)
    blocks = jnp.maximum((order[0, rows - 1] + BLK - 1) // BLK, 1)
    near = jnp.arange(8, dtype=jnp.int32)
    near = jnp.bitwise_xor(net.flat, near & 3) * 2 + jnp.bitwise_xor(net.core, near >> 2)
    where_ref = jnp.concatenate(
        [
            near,
            jnp.stack([net.core, net.flat, blocks]).astype(jnp.int32),
            modality.reshape(seqs, LEN)[:, 0],
        ]
    )
    tokens = lay(tokens, seqs)
    ring, where_ref, tokens = tie(ring, where_ref, tokens)

    own = net.ring(ring, part)
    near = net.square(own)
    text, _ = tie(pack_expert(w_up[1], w_down[1]), own)
    ring_text = net.turns(text)
    masked = masked.astype(F32).reshape(rows, 1)
    cotangent = lay(cotangent, seqs)
    vector = mask_vector.astype(F32).reshape(1, D)
    near, masked, place, cotangent, vector = tie(near, masked, place, cotangent, vector)
    pieces = net.square_cores(near)
    own_text = net.ring(ring_text, part)
    pieces, own_text, image = tie(pieces, own_text, pack_expert(w_up[0], w_down[0]))
    near_text = net.sides(own_text)
    image = net.turns(image)

    qkv, softs, context, normed_one, params = call(
        attention_kernel,
        seqs,
        (where_ref, tokens, masked, vector, *pieces),
        [by_step((SEQ, D)), by_step((SEQ, 1)), whole((1, D))] + [ANY] * 8,
        [
            ((rows, 3 * D), BF16),
            ((seqs, H // 2, SEQ, 2 * SEQ), F32),
            ((rows, D), BF16),
            ((rows, D), BF16),
            ((8, D), F32),
        ],
        [
            by_step((SEQ, 3 * D)),
            by_step((1, H // 2, SEQ, 2 * SEQ)),
            by_step((SEQ, D)),
            by_step((SEQ, D)),
            pl.BlockSpec((8, D), lambda i, *_: (0, 0)),
        ],
        [pltpu.VMEM((D, n_columns), BF16), pltpu.SemaphoreType.DMA((10,))],
        "attention",
    )

    near_text, image, qkv, softs, context, normed_one, params = tie(
        near_text, image, qkv, softs, context, normed_one, params
    )
    near_text = net.corner(near_text)
    last, image = tie(net.last(near_text), net.ring(image, part))
    pieces_text = net.cores_of(near_text, last)
    image, pieces_text = tie(image, pieces_text)
    near_image = net.sides(image)

    block = (ROWS_ONE, D)
    keep, send, send_far, grad_context, sums = call(
        feed_back_kernel,
        4,
        (where_ref, place, vector, cotangent, context, params, *pieces_text, *pieces),
        [whole((1, rows)), whole((1, D)), whole((rows, D)), whole((rows, D)), whole((8, D))]
        + [ANY] * 18,
        [((4, *block), BF16), ((3, *block), BF16), (block, BF16), ((rows, D), BF16), ((8, D), F32)],
        [ANY] * 3 + [whole((rows, D)), whole((8, D))],
        [
            pltpu.VMEM((rows, D), BF16),
            pltpu.VMEM((rows, D), F32),
            pltpu.VMEM((rows, D), BF16),
            pltpu.VMEM((rows, D), BF16),
            pltpu.VMEM((rows, D), F32),
        ]
        + [pltpu.VMEM((D, D), F32)] * 2
        + [
            pltpu.VMEM((4, D, D), BF16),
            pltpu.VMEM((FF, D), BF16),
            pltpu.VMEM((D, D), BF16),
            pltpu.VMEM((2, 4, *block), BF16),
            pltpu.SemaphoreType.DMA((40,)),
            pltpu.SemaphoreType.DMA((10,)),
            pltpu.SemaphoreType.DMA((5, 5)),
        ],
        "feed_back",
    )
    near_image, keep, send, send_far, grad_context, sums = tie(
        near_image, keep, send, send_far, grad_context, sums
    )
    far = net.far_sums(keep, net.to_core(send_far))
    halves_image = net.halves(near_image)
    far, send, context, halves_image = tie(far, send, context, halves_image)
    got = net.to_core(send)
    corner = net.to_corner(far)
    near_image = net.to_corners(near_image, halves_image)
    experts = [pltpu.VMEM((4, D, D), BF16), pltpu.VMEM((FF, D), BF16)]
    after, normed_two = call(
        feed_text_kernel,
        4,
        (where_ref, tokens, masked, vector, context, params, *pieces_text, *pieces),
        [whole((rows, D)), whole((rows, 1)), whole((1, D)), whole((rows, D)), whole((8, D))]
        + [ANY] * 18,
        [((rows, D), F32), ((rows, D), BF16)],
        [whole((rows, D))] * 2,
        experts
        + [
            pltpu.VMEM((D, D), BF16),
            pltpu.SemaphoreType.DMA((40,)),
            pltpu.SemaphoreType.DMA((10,)),
            pltpu.VMEM((seqs * TAIL, D), BF16),
        ],
        "feed_text",
    )
    corner, got, near_image, after = tie(corner, got, near_image, after)
    sums_feed = net.side_sums(keep, got, corner)
    last_image = net.far_cores(net.last(near_image))
    sums_feed, grad_context, last_image = tie(sums_feed, grad_context, last_image)
    sums_feed = net.to_sides(sums_feed)
    far_image = net.far_cores(near_image[:3])

    keep, send, grad_tokens = call(
        attention_back_kernel,
        seqs,
        (where_ref, qkv, softs, grad_context, normed_one, tokens, masked, vector, params, sums)
        + tuple(pieces),
        [
            by_step((SEQ, 3 * D)),
            by_step((1, H // 2, SEQ, 2 * SEQ)),
            by_step((SEQ, D)),
            whole((rows, D)),
            by_step((SEQ, D)),
            by_step((SEQ, 1)),
            whole((1, D)),
            whole((8, D)),
            whole((8, D)),
        ]
        + [ANY] * 8,
        [((4, ROWS_QKV, D), BF16), ((4, ROWS_QKV, D), BF16), ((seqs * LEN, D), F32)],
        [ANY, ANY, whole((seqs * LEN, D))],
        [
            pltpu.VMEM((D, 3 * D), BF16),
            pltpu.VMEM((8, D), F32),
            pltpu.VMEM((rows, 3 * D), BF16),
            pltpu.VMEM((8, ROWS_QKV, D), BF16),
            pltpu.SemaphoreType.DMA((10,)),
            pltpu.SemaphoreType.DMA((8,)),
        ],
        "attention_back",
    )
    keep, send, grad_tokens, sums_feed, far_image = tie(
        keep, send, grad_tokens, sums_feed, far_image
    )
    got = net.to_core(send)
    pieces_image = net.all_cores(near_image, far_image, last_image)
    sums_qkv = net.plane_sums(keep, got, 296)
    ring_one = net.ring_sums(sums_feed, [(4, 96), (1, 384), (1, 96)])
    sums_qkv, ring_one, after, pieces_image = tie(sums_qkv, ring_one, after, pieces_image)
    sums_qkv = net.to_plane(sums_qkv)
    ring_one = net.to_ring(ring_one, (1, 2))
    (output,) = call(
        feed_image_kernel,
        4,
        (where_ref, normed_two, after, *pieces_image),
        [whole((rows, D)), whole((rows, D))] + [ANY] * 10,
        [((seqs * LEN, D), BF16)],
        [whole((seqs * LEN, D))],
        [pltpu.VMEM((rows, D), F32)]
        + experts
        + [pltpu.SemaphoreType.DMA((40,)), pltpu.VMEM((seqs * LEN, D), F32)],
        "feed_image",
    )
    sums_qkv, ring_one, output = tie(sums_qkv, ring_one, output)
    ring_two = net.ring_sums(sums_qkv, [(3, 96), (0, 8)])
    ring_one = net.to_ring(ring_one, (3,))
    ring_two = net.to_ring(ring_two, (1, 2, 3))

    grads = net.add_ring(ring_one)
    grad_w_up = grads[: 4 * part].reshape(4, part, D).transpose(1, 0, 2).reshape(part, FF)
    grad_w_down = grads[4 * part : 8 * part]
    grad_w_out = grads[8 * part : 9 * part]
    grads = net.add_ring(ring_two)
    grad_w_qkv = grads[: 3 * part].reshape(3, part, D).transpose(1, 0, 2).reshape(part, 3 * D)
    extra = grads[3 * part :]
    owned = lax.dynamic_slice_in_dim(extra, net.index * part, part, 1)

    return (
        output,
        grad_tokens,
        extra[2],
        owned[3],
        owned[4],
        grad_w_qkv,
        grad_w_out,
        owned[0],
        owned[1],
        grad_w_up,
        grad_w_down,
    )


def solution(mesh):
    if (mesh.shape["dp"], mesh.shape["fsdp"]) == (8, 4):
        mesh = Mesh(mesh.devices.reshape(2, 2, 2, 4), Cube.axes)
        make = Cube
    else:
        make = functools.partial(Flat, mesh.size)
    axes = Cube.axes if make is Cube else Flat.axes
    row, flat = P(axes, None), P(axes)
    middle = P(None, axes, None)
    in_specs = (row, flat, flat, row, P(), flat, flat, row, row, flat, flat, middle, middle)
    out_specs = (row, row, P(), flat, flat, row, row, flat, flat, row, row)
    return jax.shard_map(
        functools.partial(layer, make),
        mesh=mesh,
        in_specs=in_specs,
        out_specs=out_specs,
        check_vma=False,
    )
```

```python
import functools
import math

import jax
import jax.numpy as jnp
from jax import lax
from jax.experimental import pallas as pl
from jax.experimental.pallas import tpu as pltpu
from jax.sharding import Mesh, PartitionSpec as P

H = 12
HD = 64
LEN = 237
PATCHES = 197
HEAD = 208
TAIL = 48
SEQ = HEAD + TAIL
D = H * HD
FF = 4 * D
BLK = 256
EPS = 1e-05
F32 = jnp.float32
BF16 = jnp.bfloat16
MIB = 1 << 20
ROWS_ONE = 864
ROWS_QKV = 304


def dot(a, b):
    return jnp.dot(a, b, preferred_element_type=F32)


def dot_nt(a, b):
    return lax.dot_general(a, b, (((1,), (1,)), ((), ())), preferred_element_type=F32)


def dot_tn(a, b):
    return lax.dot_general(a, b, (((0,), (0,)), ((), ())), preferred_element_type=F32)


def mean(rows):
    return jnp.mean(rows, -1, keepdims=True)


def normalize(rows):
    centred = rows - mean(rows)
    inverse = lax.rsqrt(mean(centred * centred) + EPS)
    return centred * inverse, inverse


def normalize_back(grad, unit, inverse, gain):
    scaled = grad * gain
    return inverse * (scaled - mean(scaled) - unit * mean(scaled * unit))


def total(rows):
    return jnp.sum(rows, 0, keepdims=True)


def halves(pair):
    lane = lax.broadcasted_iota(jnp.int32, pair.shape, 1)
    zero = jnp.zeros_like(pair)
    return jnp.concatenate(
        [jnp.where(lane < HD, pair, zero), jnp.where(lane < HD, zero, pair)], 0
    )


def key_bias():
    key = lax.broadcasted_iota(jnp.int32, (1, SEQ), 1)
    valid = (key < PATCHES) | ((key >= HEAD) & (key < HEAD + LEN - PATCHES))
    return jnp.where(valid, 0.0, -1e30)


def softmax_pair(queries, keys_cat, bias):
    scores = dot_nt(queries, keys_cat)
    out = []
    for head in range(2):
        own = scores[:, head * SEQ : (head + 1) * SEQ] + bias
        powers = jnp.exp(own - jnp.max(own, -1, keepdims=True))
        out.append(powers * (1.0 / jnp.sum(powers, -1, keepdims=True)))
    return jnp.concatenate(out, 1)


def spans(where_ref, pieces, rows):
    if len(pieces) == 8:
        for j in range(8):
            yield pieces[j], where_ref[j], 0, rows
        return
    for side in range(2):
        for j in range(5):
            block = where_ref[4 * side + min(j, 3)]
            size = rows if j < 3 else rows // 2
            yield pieces[5 * side + j], block, (size if j == 4 else 0), size


def started(copies, sems, start=True):
    copies = [
        pltpu.make_async_copy(source, target, sems.at[j])
        for j, (source, target) in enumerate(copies)
    ]
    if start:
        for copy in copies:
            copy.start()
    return copies


def load_pieces(where_ref, pieces, target, sems, columns, start=True):
    return started(
        [
            (
                piece.at[:, pl.ds(columns[0], columns[1])],
                target.at[pl.ds(pl.multiple_of(block * 96 + first, 16), size), :],
            )
            for piece, block, first, size in spans(where_ref, pieces, 96)
        ],
        sems,
        start,
    )


def load_expert(where_ref, pieces, up, down, sems):
    copies = []
    for piece, block, first, size in spans(where_ref, pieces, 768):
        if first == 0:
            for chunk in range(4):
                copies.append(
                    (
                        piece.at[pl.ds(chunk * 96, 96), :],
                        up.at[chunk, pl.ds(pl.multiple_of(block * 96, 96), 96), :],
                    )
                )
        if first + size == 768:
            copies.append(
                (
                    piece.at[pl.ds(384 - first, 384), :],
                    down.at[pl.ds(pl.multiple_of(block * 384, 384), 384), :],
                )
            )
    return started(copies, sems)


def wait_all(copies):
    for copy in copies:
        copy.wait()


def column(masked, seq):
    return jnp.transpose(masked[seq])[:, :1]


def attention_kernel(where_ref, tokens, masked, vector, *rest):
    pieces, rest = rest[:8], rest[8:]
    qkv, softs, context, normed_one, params, weights, sems = rest

    @pl.when(pl.program_id(0) == 0)
    def _():
        wait_all(load_pieces(where_ref, pieces, weights, sems, (0, weights.shape[1])))
        columns = weights[:, 4 * D : 4 * D + 128].astype(F32)
        params[...] = jnp.transpose(columns)[:8]

    start = jnp.where(column(masked, 0) == 1.0, vector[...], tokens[...].astype(F32))
    unit, _ = normalize(start)
    first = (unit * params[0:1] + params[1:2]).astype(BF16)
    normed_one[...] = first
    for third in range(3):
        at = pl.ds(third * D, D)
        qkv[:, at] = dot(first, weights[:, at]).astype(BF16)
    bias = key_bias()
    for pair in range(H // 2):
        queries = qkv[:, pl.ds(pair * 128, 128)] * BF16(1.0 / math.sqrt(HD))
        keys = halves(qkv[:, pl.ds(D + pair * 128, 128)])
        values = halves(qkv[:, pl.ds(2 * D + pair * 128, 128)])
        soft = softmax_pair(queries, keys, bias)
        softs[0, pair] = soft
        attention = soft.astype(BF16)
        context[:, pl.ds(pair * 128, 128)] = dot(attention, values).astype(BF16)


def chosen(place, block):
    row = lax.broadcasted_iota(jnp.int32, (BLK, place.shape[1]), 0) + block * BLK
    return jnp.where(row == place[...], 1.0, 0.0).astype(BF16)


def rows_of(block):
    return pl.ds(pl.multiple_of(block * BLK, BLK), BLK)


def feed_back_kernel(where_ref, place, vector, cotangent, context, params, *rest):
    pieces, attention_pieces, rest = rest[:10], rest[10:18], rest[18:]
    keep, send, send_far, grad_context, sums = rest[:5]
    rows_two, rows_hidden, rows_cot, rows_context, grad_two = rest[5:10]
    (sum_up, sum_down, w_up, w_down, w_out, stage) = rest[10:16]
    sems, attention_sems, out_sems = rest[16:]
    step = pl.program_id(0)
    blocks = where_ref[10]
    core = where_ref[8]

    @pl.when(step == 0)
    def _():
        copies = load_pieces(where_ref, attention_pieces, w_out, attention_sems, (3 * D, D))
        more = load_expert(where_ref, pieces, w_up, w_down, sems)

        def gather(block, _):
            pick, at = chosen(place, block), rows_of(block)
            rows_cot[at, :] = dot(pick, cotangent[...]).astype(BF16)
            rows_context[at, :] = dot(pick, context[...]).astype(BF16)
            grad_two[at, :] = jnp.zeros((BLK, D), F32)
            return 0

        def norm(block, _):
            at = rows_of(block)
            rows = vector[...] + dot(rows_context[at, :], w_out[...])
            rows_hidden[at, :] = rows
            unit, _ = normalize(rows)
            rows_two[at, :] = (unit * params[2:3] + params[3:4]).astype(BF16)
            return 0

        lax.fori_loop(0, blocks, gather, 0)
        wait_all(copies)
        lax.fori_loop(0, blocks, norm, 0)
        wait_all(more)

    up = w_up.at[step]
    down = w_down.at[pl.ds(pl.multiple_of(step * D, D), D), :]

    def expert(block, _):
        at = rows_of(block)
        rows, grads = rows_two[at, :], rows_cot[at, :]
        pre = dot(rows, up[...])
        chance = 0.5 * (1.0 + lax.erf(pre * math.sqrt(0.5)))
        activated = (pre * chance).astype(BF16)
        slope = chance + pre * (jnp.exp(-0.5 * pre * pre) * (1.0 / math.sqrt(2.0 * math.pi)))
        grad_pre = (dot_nt(grads, down[...]) * slope).astype(BF16)
        grad_two[at, :] += dot_nt(grad_pre, up[...])
        add_down = dot_tn(activated, grads)
        add_up = dot_tn(rows, grad_pre)

        @pl.when(block == 0)
        def _():
            sum_down[...] = add_down
            sum_up[...] = add_up

        @pl.when(block > 0)
        def _():
            sum_down[...] += add_down
            sum_up[...] += add_up

        return 0

    lax.fori_loop(0, blocks, expert, 0)

    def leaving(at_step):
        rows = pl.ds(pl.multiple_of(at_step * 96, 96), 96)
        columns = pl.ds(384, 384)
        mine = jnp.bitwise_xor(at_step, where_ref[9])
        near = jnp.minimum(mine, 2)
        sem = out_sems.at[at_step]
        return [
            (None, stage.at[0, :, rows, :], keep.at[:, rows, :], sem.at[0]),
            (None, stage.at[0, mine, columns, :], keep.at[mine, columns, :], sem.at[1]),
            (None, stage.at[1, pl.ds(0, 3), rows, :], send.at[:, rows, :], sem.at[2]),
            (None, stage.at[1, 3, rows, :], send_far.at[rows, :], sem.at[3]),
            (mine < 3, stage.at[1, near, columns, :], send.at[near, columns, :], sem.at[4]),
            (mine == 3, stage.at[1, 3, columns, :], send_far.at[columns, :], sem.at[4]),
        ]

    def each(copies, act):
        for when, source, target, sem in copies:
            copy = pltpu.make_async_copy(source, target, sem)
            if when is None:
                act(copy)
            else:
                pl.when(when)(functools.partial(act, copy))

    up_at = pl.ds(pl.multiple_of(step * 96, 96), 96)
    mine = jnp.bitwise_xor(step, where_ref[9])
    for side in range(2):
        for j in range(4):
            source = pl.ds(pl.multiple_of(where_ref[4 * side + j] * 96, 96), 96)
            stage[side, j, up_at, :] = sum_up[source, :].astype(BF16)
        half = core if side == 0 else 1 - core
        source = pl.ds(pl.multiple_of(half * 384, 384), 384)
        stage[side, mine, pl.ds(384, 384), :] = sum_down[source, :].astype(BF16)
    each(leaving(step), lambda copy: copy.start())

    @pl.when(step == pl.num_programs(0) - 1)
    def _():
        sums[...] = jnp.zeros_like(sums)

        def back(block, _):
            pick, at = chosen(place, block), rows_of(block)
            unit, inverse = normalize(rows_hidden[at, :])
            grad = grad_two[at, :]
            grad_hidden = rows_cot[at, :].astype(F32) + normalize_back(
                grad, unit, inverse, params[2:3]
            )
            sums[0:1] += total(grad * unit)
            sums[1:2] += total(grad)
            sums[2:3] += total(grad_hidden)
            grad_attn = grad_hidden.astype(BF16)
            add_out = dot_tn(rows_context[at, :], grad_attn)
            rows = dot_nt(grad_attn, w_out[...]).astype(BF16)
            rows = dot_tn(pick, rows).astype(BF16)

            @pl.when(block == 0)
            def _():
                sum_up[...] = add_out
                grad_context[...] = rows

            @pl.when(block > 0)
            def _():
                sum_up[...] += add_out
                grad_context[...] += rows

            return 0

        lax.fori_loop(0, blocks, back, 0)
        for side in range(2):
            for j in range(4):
                source = pl.ds(pl.multiple_of(where_ref[4 * side + j] * 96, 96), 96)
                stage[side, j, pl.ds(768, 96), :] = sum_up[source, :].astype(BF16)
        rows = pl.ds(768, 96)
        sem = out_sems.at[4]
        last = [
            (None, stage.at[0, :, rows, :], keep.at[:, rows, :], sem.at[0]),
            (None, stage.at[1, pl.ds(0, 3), rows, :], send.at[:, rows, :], sem.at[1]),
            (None, stage.at[1, 3, rows, :], send_far.at[rows, :], sem.at[2]),
        ]
        each(last, lambda copy: copy.start())
        each(last, lambda copy: copy.wait())
        for at_step in range(4):
            each(leaving(at_step), lambda copy: copy.wait())


def put_rows(target, rows, seq):
    target[seq * LEN : seq * LEN + PATCHES] = rows[:PATCHES]
    target[seq * LEN + PATCHES : (seq + 1) * LEN] = rows[HEAD : HEAD + LEN - PATCHES]


def attention_back_kernel(
    where_ref, qkv, softs, grad_context, normed_one, tokens, masked, vector, params, before, *rest
):
    pieces = rest[:8]
    keep, send, grad_tokens = rest[8:11]
    weights, sums, grad_qkv, stage, sems, out_sems = rest[11:]
    step = pl.program_id(0)
    here = pl.ds(pl.multiple_of(step * SEQ, SEQ), SEQ)

    def copies():
        return load_pieces(where_ref, pieces, weights, sems, (0, 3 * D), False)

    @pl.when(step == 0)
    def _():
        for copy in copies():
            copy.start()
        sums[...] = before[...]

    inv_root = 1.0 / math.sqrt(HD)
    top = lax.broadcasted_iota(jnp.int32, (128, SEQ), 0) < HD
    for pair in range(H // 2):
        queries = qkv[:, pl.ds(pair * 128, 128)]
        keys = halves(qkv[:, pl.ds(D + pair * 128, 128)])
        values = halves(qkv[:, pl.ds(2 * D + pair * 128, 128)])
        grads = grad_context[:, pl.ds(pair * 128, 128)]
        grad_soft = dot_nt(grads, values)
        parts = []
        for head in range(2):
            span = slice(head * SEQ, (head + 1) * SEQ)
            own, grad = softs[0, pair, :, span], grad_soft[:, span]
            parts.append(own * (grad - jnp.sum(own * grad, -1, keepdims=True)))
        grad_scores = jnp.concatenate(parts, 1).astype(BF16)
        grad_qkv[here, pl.ds(pair * 128, 128)] = (dot(grad_scores, keys) * inv_root).astype(BF16)
        by_key = dot_tn(queries, grad_scores) * inv_root
        by_key = jnp.where(top, by_key[:, :SEQ], by_key[:, SEQ:])
        grad_qkv[here, pl.ds(D + pair * 128, 128)] = jnp.transpose(by_key).astype(BF16)
        by_value = dot_tn(grads, softs[0, pair].astype(BF16))
        by_value = jnp.where(top, by_value[:, :SEQ], by_value[:, SEQ:])
        grad_qkv[here, pl.ds(2 * D + pair * 128, 128)] = jnp.transpose(by_value).astype(BF16)

    @pl.when(step == 0)
    def _():
        wait_all(copies())

    grad_one = dot_nt(grad_qkv[here, :], weights[...])
    hidden_row = column(masked, 0) == 1.0
    start = jnp.where(hidden_row, vector[...], tokens[...].astype(F32))
    unit, inverse = normalize(start)
    grad_start = normalize_back(grad_one, unit, inverse, params[0:1])
    sums[3:4] += total(grad_one * unit)
    sums[4:5] += total(grad_one)
    sums[2:3] += total(jnp.where(hidden_row, grad_start, 0.0))
    kept = jnp.where(hidden_row, 0.0, grad_start)
    for seq in range(normed_one.shape[0] // SEQ):
        pl.when(step == seq)(functools.partial(put_rows, grad_tokens, kept, seq))

    @pl.when(step == pl.num_programs(0) - 1)
    def _():
        extra = jnp.concatenate([sums[...], jnp.zeros_like(sums[...])], 0).astype(BF16)
        for third in range(3):
            for part in range(3):
                at = pl.ds(third * D + part * SEQ, SEQ)
                add = dot_tn(normed_one[...], grad_qkv[:, at]).astype(BF16)
                for block in range(8):
                    stage[block, pl.ds(third * 96, 96), pl.ds(part * SEQ, SEQ)] = add[
                        block * 96 : (block + 1) * 96
                    ]
        out_copies = []
        for side, out in enumerate((keep, send)):
            for j in range(4):
                block = where_ref[4 * side + j]
                stage[block, pl.ds(3 * 96, 16), :] = extra
                out_copies.append((stage.at[block], out.at[j]))
        wait_all(started(out_copies, out_sems))


def gelu(pre):
    return (pre * (0.5 * (1.0 + lax.erf(pre * math.sqrt(0.5))))).astype(BF16)


def feed(text, where_ref, rows_in, sums, up, down, tails):
    seqs = rows_in.shape[0] // SEQ
    for seq in range(seqs):
        head = pl.ds(seq * SEQ, HEAD)

        @pl.when(where_ref[11 + seq] == int(text))
        def _():
            activated = gelu(dot(rows_in[head, :], up[...]))
            sums[head, :] += dot(activated, down[...])

    if text:
        more = dot(gelu(dot(tails[...], up[...])), down[...])
        for seq in range(seqs):
            sums[pl.ds(seq * SEQ + HEAD, TAIL), :] += more[seq * TAIL : (seq + 1) * TAIL]


def feed_text_kernel(where_ref, tokens, masked, vector, context, params, *rest):
    pieces, attention_pieces, rest = rest[:10], rest[10:18], rest[18:]
    out, normed_two, w_up, w_down, w_out, sems, attention_sems, tails = rest
    step = pl.program_id(0)

    @pl.when(step == 0)
    def _():
        copies = load_pieces(where_ref, attention_pieces, w_out, attention_sems, (3 * D, D))
        more = load_expert(where_ref, pieces, w_up, w_down, sems)
        wait_all(copies)
        for seq in range(tokens.shape[0] // SEQ):
            at = pl.ds(seq * SEQ, SEQ)
            start = jnp.where(column(masked, seq) == 1.0, vector[...], tokens[at, :].astype(F32))
            hidden = start + dot(context[at, :], w_out[...])
            out[at, :] = hidden
            unit, _ = normalize(hidden)
            second = (unit * params[2:3] + params[3:4]).astype(BF16)
            normed_two[at, :] = second
            tails[pl.ds(seq * TAIL, TAIL), :] = second[HEAD:]
        wait_all(more)

    down = w_down.at[pl.ds(pl.multiple_of(step * D, D), D), :]
    feed(True, where_ref, normed_two, out, w_up.at[step], down, tails)


def feed_image_kernel(where_ref, rows_in, before, *rest):
    pieces, (out, sums, w_up, w_down, sems, flat) = rest[:10], rest[10:]
    step = pl.program_id(0)

    @pl.when(step == 0)
    def _():
        copies = load_expert(where_ref, pieces, w_up, w_down, sems)
        sums[...] = before[...]
        wait_all(copies)

    down = w_down.at[pl.ds(pl.multiple_of(step * D, D), D), :]
    feed(False, where_ref, rows_in, sums, w_up.at[step], down, None)

    @pl.when(step == pl.num_programs(0) - 1)
    def _():
        for seq in range(rows_in.shape[0] // SEQ):
            put_rows(flat, sums[pl.ds(seq * SEQ, SEQ), :], seq)
        out[...] = flat[...].astype(BF16)


def whole(shape):
    return pl.BlockSpec(shape, lambda *_: (0,) * len(shape), pipeline_mode=pl.Buffered(1))


def by_step(shape):
    return pl.BlockSpec(shape, lambda i, *_: (i,) + (0,) * (len(shape) - 1))


ANY = pl.BlockSpec(memory_space=pl.ANY)


def call(kernel, steps, ins, in_specs, outs, out_specs, scratch, name):
    run = pl.pallas_call(
        kernel,
        out_shape=tuple(jax.ShapeDtypeStruct(s, d) for s, d in outs),
        grid_spec=pltpu.PrefetchScalarGridSpec(
            num_scalar_prefetch=1,
            grid=(steps,),
            in_specs=in_specs,
            out_specs=out_specs,
            scratch_shapes=scratch,
        ),
        compiler_params=pltpu.CompilerParams(vmem_limit_bytes=60 * MIB),
        cost_estimate=pl.CostEstimate(flops=1, bytes_accessed=1, transcendentals=0),
        name=name,
    )
    return run(*ins)


def lay(rows, seqs):
    rows = rows.reshape(seqs, LEN, -1)
    return jnp.concatenate(
        [
            jnp.pad(rows[:, :PATCHES], ((0, 0), (0, HEAD - PATCHES), (0, 0))),
            jnp.pad(rows[:, PATCHES:], ((0, 0), (0, TAIL - LEN + PATCHES), (0, 0))),
        ],
        1,
    ).reshape(seqs * SEQ, -1)


def tie(*trees):
    return lax.optimization_barrier(trees)


def in_order(rows, part, blocks=0, axis=0):
    rows = jnp.moveaxis(rows, axis, blocks)
    shape, columns = rows.shape[:blocks], rows.shape[-1]
    count, size = rows.shape[blocks], rows.shape[blocks + 1]
    if size == part:
        return rows.reshape(*shape, count * part, columns)
    up = rows[..., : 4 * part, :].reshape(*shape, count, 4, part, columns)
    up = jnp.swapaxes(up, blocks, blocks + 1).reshape(*shape, 4 * count * part, columns)
    down = rows[..., 4 * part :, :].reshape(*shape, count * (size - 4 * part), columns)
    return jnp.concatenate([up, down], -2)


class Cube:
    axes = ("y", "x", "core", "z")
    swap = [(0, 1), (1, 0)]

    def __init__(self):
        y, x, core, z = (lax.axis_index(a) for a in self.axes)
        self.z, self.core, self.flat = z, core, y * 2 + x
        self.index = ((y * 2 + x) * 2 + core) * 4 + z

    def turn(self, block, k):
        return lax.ppermute(block, "z", [(i, (i + k) % 4) for i in range(4)])

    def turns(self, block):
        return [block] + [self.turn(block, k) for k in (1, 2, 3)]

    def ring(self, ring, part):
        out = []
        for place in range(4):
            k = lax.rem(self.z + 4 - place, 4)
            out.append(
                jnp.where(
                    k == 0,
                    ring[0],
                    jnp.where(k == 1, ring[1], jnp.where(k == 2, ring[2], ring[3])),
                )
            )
        return in_order(jnp.stack(out), part)

    def swapped(self, block, axis):
        return lax.ppermute(block, axis, self.swap)

    def sides(self, own):
        return own, self.swapped(own, "x"), self.swapped(own, "y")

    def halves(self, near):
        half = near[0].shape[0] // 2
        return near[1][:half], near[2][half:]

    def to_corners(self, near, halves):
        return (*near, self.swapped(halves[0], "y"), self.swapped(halves[1], "x"))

    def corner(self, near):
        return self.to_corners(near, self.halves(near))

    def cores(self, near):
        return [*near] + [self.swapped(b, "core") for b in near]

    def plane(self, j, block):
        if j == 1:
            return self.swapped(block, "x")
        if j == 2:
            return self.swapped(block, "y")
        return lax.ppermute(block, ("y", "x"), [(i, 3 - i) for i in range(4)])

    def to_core(self, block):
        return self.swapped(block, "core")

    def far_sums(self, keep, got):
        half = got.shape[0] // 2
        return [
            (keep[3, at].astype(F32) + got[at].astype(F32)).astype(BF16)
            for at in (slice(half), slice(half, None))
        ]

    def to_corner(self, both):
        return self.swapped(both[0], "x"), self.swapped(both[1], "y")

    def side_sums(self, keep, got, corner):
        half = corner[0].shape[0]
        by_x = jnp.pad(corner[0], ((0, half), (0, 0))).astype(F32)
        by_y = jnp.pad(corner[1], ((half, 0), (0, 0))).astype(F32)
        to_x = keep[1].astype(F32) + got[1].astype(F32) + by_y
        to_y = keep[2].astype(F32) + got[2].astype(F32) + by_x
        return [keep, got, to_x.astype(BF16), to_y.astype(BF16)]

    def to_sides(self, sums):
        return [*sums[:2], self.swapped(sums[2], "x"), self.swapped(sums[3], "y")]

    def plane_sums(self, keep, got, rows):
        both = [keep[j, :rows].astype(F32) + got[j, :rows].astype(F32) for j in (1, 2, 3)]
        return [keep, got] + [b.astype(BF16) for b in both]

    def to_plane(self, sums):
        return sums[:2] + [self.plane(j, sums[j + 1]) for j in (1, 2, 3)]

    def square(self, own):
        return [own] + [self.plane(j, own) for j in (1, 2, 3)]

    def square_cores(self, near):
        return [*near] + [self.swapped(b, "core") for b in near]

    def last(self, near):
        return near[3:]

    def cores_of(self, near, last):
        return self.cores([*near[:3], *last])

    def far_cores(self, near):
        return [self.swapped(b, "core") for b in near]

    def all_cores(self, near, far, last):
        return [*near, *far, *last]

    def ring_sums(self, group, fields):
        keep, got, *more = group
        rows = more[0].shape[0]
        mine = sum(m.astype(F32) for m in (keep[0, :rows], got[0, :rows], *more))
        rounded = lax.optimization_barrier(mine.astype(BF16))
        return [cut(mine, fields, self.z)] + [
            cut(rounded, fields, lax.rem(self.z + k, 4)) for k in (1, 2, 3)
        ]

    def to_ring(self, parts, which):
        return [self.turn(p, k) if k in which else p for k, p in enumerate(parts)]

    def add_ring(self, ring):
        return ring[0] + sum(m.astype(F32) for m in ring[1:])


class Flat:
    axes = ("dp", "fsdp")

    def __init__(self, count):
        self.flat = self.core = jnp.int32(0)
        self.index = lax.axis_index(self.axes)
        self.count = count

    def turns(self, block):
        return lax.all_gather(block, self.axes, axis=0)

    def ring(self, full, part):
        return in_order(full.reshape((8, -1) + full.shape[1:]), part, 1, 1)

    def sides(self, own):
        return own

    def halves(self, near):
        return ()

    def to_corners(self, near, halves):
        return near

    def corner(self, near):
        return near

    def cores(self, near):
        half = near.shape[1] // 2
        out = []
        for side in range(2):
            out += [near[side], near[2 + side], near[4 + side]]
            out += [near[6 + side, :half], near[6 + side, half:]]
        return out

    def to_core(self, block):
        return block

    def far_sums(self, keep, got):
        return got

    def to_corner(self, both):
        return both

    def side_sums(self, keep, got, corner):
        return self.plane_sums(keep, jnp.concatenate([got, corner[None]]), None)

    def to_sides(self, sums):
        return sums

    def plane_sums(self, keep, got, rows):
        return [jnp.stack([keep, got], 1).reshape((8,) + keep.shape[1:])]

    def to_plane(self, sums):
        return sums

    def square(self, own):
        return own

    def square_cores(self, near):
        return [near[b] for b in (0, 2, 4, 6, 1, 3, 5, 7)]

    def last(self, near):
        return ()

    def cores_of(self, near, last):
        return self.cores(near)

    def far_cores(self, near):
        return ()

    def all_cores(self, near, far, last):
        return self.cores(near)

    def ring_sums(self, group, fields):
        ways = self.count // 8
        parts = [[cut(block, fields, w, ways) for w in range(ways)] for block in group[0]]
        return jnp.stack([p for block in parts for p in block]).astype(F32)

    def to_ring(self, parts, which):
        if 3 not in which:
            return parts
        return lax.psum_scatter(parts, self.axes, scatter_dimension=0, tiled=False)

    def add_ring(self, ring):
        return ring


def pack_expert(up, down):
    part = up.shape[0]
    up = up.reshape(part, 4, D).transpose(1, 0, 2).reshape(4 * part, D)
    return jnp.concatenate([up, down], 0)


def cut(rows, fields, place, ways=4):
    out, at = [], 0
    for groups, size in fields:
        part = rows[at : at + max(groups, 1) * size]
        at += max(groups, 1) * size
        if groups:
            part = part.reshape(groups, ways, size // ways, D)
            part = lax.dynamic_index_in_dim(part, place, 1, keepdims=False).reshape(-1, D)
        out.append(part)
    return jnp.concatenate(out)


def layer(
    make,
    tokens,
    modality,
    token_mask,
    cotangent,
    mask_vector,
    ln_one_gain,
    ln_one_shift,
    w_qkv,
    w_out,
    ln_two_gain,
    ln_two_shift,
    w_up,
    w_down,
):
    net = make()
    part = w_qkv.shape[0]
    seqs = tokens.shape[0] // LEN
    rows = seqs * SEQ
    columns = jnp.stack([ln_one_gain, ln_one_shift, ln_two_gain, ln_two_shift], 1)
    packed = jnp.concatenate([w_qkv, w_out, jnp.pad(columns, ((0, 0), (0, 124)))], 1)
    n_columns = packed.shape[1]
    ring = net.turns(packed)

    seq_masks = token_mask.reshape(seqs, LEN)
    masked = jnp.concatenate(
        [
            jnp.pad(seq_masks[:, :PATCHES], ((0, 0), (0, HEAD - PATCHES))),
            jnp.pad(seq_masks[:, PATCHES:], ((0, 0), (0, TAIL - LEN + PATCHES))),
        ],
        1,
    ).reshape(1, rows)
    order = jnp.cumsum(masked, 1)
    place = jnp.where(masked == 1, order - 1, -1)
    blocks = jnp.maximum((order[0, rows - 1] + BLK - 1) // BLK, 1)
    near = jnp.arange(8, dtype=jnp.int32)
    near = jnp.bitwise_xor(net.flat, near & 3) * 2 + jnp.bitwise_xor(net.core, near >> 2)
    where_ref = jnp.concatenate(
        [
            near,
            jnp.stack([net.core, net.flat, blocks]).astype(jnp.int32),
            modality.reshape(seqs, LEN)[:, 0],
        ]
    )
    masked = jnp.broadcast_to(masked.reshape(seqs, 1, SEQ), (seqs, 8, SEQ)).astype(F32)
    ring, where_ref = tie(ring, where_ref)

    own = net.ring(ring, part)
    near = net.square(own)
    text, _ = tie(pack_expert(w_up[1], w_down[1]), own)
    ring_text = net.turns(text)
    tokens, cotangent, _ = tie(tokens, cotangent, own)
    tokens = lay(tokens, seqs)
    cotangent = lay(cotangent, seqs)
    vector = mask_vector.astype(F32).reshape(1, D)
    near, place, tokens, cotangent, vector = tie(near, place, tokens, cotangent, vector)
    pieces = net.square_cores(near)
    own_text = net.ring(ring_text, part)
    pieces, own_text, image = tie(pieces, own_text, pack_expert(w_up[0], w_down[0]))
    near_text = net.sides(own_text)
    image = net.turns(image)

    qkv, softs, context, normed_one, params = call(
        attention_kernel,
        seqs,
        (where_ref, tokens, masked, vector, *pieces),
        [by_step((SEQ, D)), by_step((1, 8, SEQ)), whole((1, D))] + [ANY] * 8,
        [
            ((rows, 3 * D), BF16),
            ((seqs, H // 2, SEQ, 2 * SEQ), F32),
            ((rows, D), BF16),
            ((rows, D), BF16),
            ((8, D), F32),
        ],
        [
            by_step((SEQ, 3 * D)),
            by_step((1, H // 2, SEQ, 2 * SEQ)),
            by_step((SEQ, D)),
            by_step((SEQ, D)),
            pl.BlockSpec((8, D), lambda i, *_: (0, 0)),
        ],
        [pltpu.VMEM((D, n_columns), BF16), pltpu.SemaphoreType.DMA((10,))],
        "attention",
    )

    near_text, image, qkv, softs, context, normed_one, params = tie(
        near_text, image, qkv, softs, context, normed_one, params
    )
    near_text = net.corner(near_text)
    last, image = tie(net.last(near_text), net.ring(image, part))
    pieces_text = net.cores_of(near_text, last)
    near_image = net.sides(image)

    block = (ROWS_ONE, D)
    keep, send, send_far, grad_context, sums = call(
        feed_back_kernel,
        4,
        (where_ref, place, vector, cotangent, context, params, *pieces_text, *pieces),
        [whole((1, rows)), whole((1, D)), whole((rows, D)), whole((rows, D)), whole((8, D))]
        + [ANY] * 18,
        [((4, *block), BF16), ((3, *block), BF16), (block, BF16), ((rows, D), BF16), ((8, D), F32)],
        [ANY] * 3 + [whole((rows, D)), whole((8, D))],
        [
            pltpu.VMEM((rows, D), BF16),
            pltpu.VMEM((rows, D), F32),
            pltpu.VMEM((rows, D), BF16),
            pltpu.VMEM((rows, D), BF16),
            pltpu.VMEM((rows, D), F32),
        ]
        + [pltpu.VMEM((D, D), F32)] * 2
        + [
            pltpu.VMEM((4, D, D), BF16),
            pltpu.VMEM((FF, D), BF16),
            pltpu.VMEM((D, D), BF16),
            pltpu.VMEM((2, 4, *block), BF16),
            pltpu.SemaphoreType.DMA((40,)),
            pltpu.SemaphoreType.DMA((10,)),
            pltpu.SemaphoreType.DMA((5, 5)),
        ],
        "feed_back",
    )
    near_image, keep, send, send_far, grad_context, sums = tie(
        near_image, keep, send, send_far, grad_context, sums
    )
    far = net.far_sums(keep, net.to_core(send_far))
    halves_image = net.halves(near_image)
    far, send, context, halves_image = tie(far, send, context, halves_image)
    got = net.to_core(send)
    corner = net.to_corner(far)
    near_image = net.to_corners(near_image, halves_image)
    experts = [pltpu.VMEM((4, D, D), BF16), pltpu.VMEM((FF, D), BF16)]
    after, normed_two = call(
        feed_text_kernel,
        4,
        (where_ref, tokens, masked, vector, context, params, *pieces_text, *pieces),
        [whole((rows, D)), whole((seqs, 8, SEQ)), whole((1, D)), whole((rows, D)), whole((8, D))]
        + [ANY] * 18,
        [((rows, D), F32), ((rows, D), BF16)],
        [whole((rows, D))] * 2,
        experts
        + [
            pltpu.VMEM((D, D), BF16),
            pltpu.SemaphoreType.DMA((40,)),
            pltpu.SemaphoreType.DMA((10,)),
            pltpu.VMEM((seqs * TAIL, D), BF16),
        ],
        "feed_text",
    )
    corner, got, near_image, after = tie(corner, got, near_image, after)
    sums_feed = net.side_sums(keep, got, corner)
    last_image = net.far_cores(net.last(near_image))
    sums_feed, grad_context, last_image = tie(sums_feed, grad_context, last_image)
    sums_feed = net.to_sides(sums_feed)
    far_image = net.far_cores(near_image[:3])

    keep, send, grad_tokens = call(
        attention_back_kernel,
        seqs,
        (where_ref, qkv, softs, grad_context, normed_one, tokens, masked, vector, params, sums)
        + tuple(pieces),
        [
            by_step((SEQ, 3 * D)),
            by_step((1, H // 2, SEQ, 2 * SEQ)),
            by_step((SEQ, D)),
            whole((rows, D)),
            by_step((SEQ, D)),
            by_step((1, 8, SEQ)),
            whole((1, D)),
            whole((8, D)),
            whole((8, D)),
        ]
        + [ANY] * 8,
        [((4, ROWS_QKV, D), BF16), ((4, ROWS_QKV, D), BF16), ((seqs * LEN, D), F32)],
        [ANY, ANY, whole((seqs * LEN, D))],
        [
            pltpu.VMEM((D, 3 * D), BF16),
            pltpu.VMEM((8, D), F32),
            pltpu.VMEM((rows, 3 * D), BF16),
            pltpu.VMEM((8, ROWS_QKV, D), BF16),
            pltpu.SemaphoreType.DMA((10,)),
            pltpu.SemaphoreType.DMA((8,)),
        ],
        "attention_back",
    )
    keep, send, grad_tokens, sums_feed, far_image = tie(
        keep, send, grad_tokens, sums_feed, far_image
    )
    got = net.to_core(send)
    pieces_image = net.all_cores(near_image, far_image, last_image)
    sums_qkv = net.plane_sums(keep, got, 296)
    ring_one = net.ring_sums(sums_feed, [(4, 96), (1, 384), (1, 96)])
    sums_qkv, ring_one, after, pieces_image = tie(sums_qkv, ring_one, after, pieces_image)
    sums_qkv = net.to_plane(sums_qkv)
    ring_one = net.to_ring(ring_one, (1, 2))
    (output,) = call(
        feed_image_kernel,
        4,
        (where_ref, normed_two, after, *pieces_image),
        [whole((rows, D)), whole((rows, D))] + [ANY] * 10,
        [((seqs * LEN, D), BF16)],
        [whole((seqs * LEN, D))],
        [pltpu.VMEM((rows, D), F32)]
        + experts
        + [pltpu.SemaphoreType.DMA((40,)), pltpu.VMEM((seqs * LEN, D), F32)],
        "feed_image",
    )
    sums_qkv, ring_one, output = tie(sums_qkv, ring_one, output)
    ring_two = net.ring_sums(sums_qkv, [(3, 96), (0, 8)])
    ring_one = net.to_ring(ring_one, (3,))
    ring_two = net.to_ring(ring_two, (1, 2, 3))

    grads = net.add_ring(ring_one)
    grad_w_up = grads[: 4 * part].reshape(4, part, D).transpose(1, 0, 2).reshape(part, FF)
    grad_w_down = grads[4 * part : 8 * part]
    grad_w_out = grads[8 * part : 9 * part]
    grads = net.add_ring(ring_two)
    grad_w_qkv = grads[: 3 * part].reshape(3, part, D).transpose(1, 0, 2).reshape(part, 3 * D)
    extra = grads[3 * part :]
    owned = lax.dynamic_slice_in_dim(extra, net.index * part, part, 1)

    return (
        output,
        grad_tokens,
        extra[2],
        owned[3],
        owned[4],
        grad_w_qkv,
        grad_w_out,
        owned[0],
        owned[1],
        grad_w_up,
        grad_w_down,
    )


def solution(mesh):
    if (mesh.shape["dp"], mesh.shape["fsdp"]) == (8, 4):
        mesh = Mesh(mesh.devices.reshape(2, 2, 2, 4), Cube.axes)
        make = Cube
    else:
        make = functools.partial(Flat, mesh.size)
    axes = Cube.axes if make is Cube else Flat.axes
    row, flat = P(axes, None), P(axes)
    middle = P(None, axes, None)
    in_specs = (row, flat, flat, row, P(), flat, flat, row, row, flat, flat, middle, middle)
    out_specs = (row, row, P(), flat, flat, row, row, flat, flat, row, row)
    return jax.shard_map(
        functools.partial(layer, make),
        mesh=mesh,
        in_specs=in_specs,
        out_specs=out_specs,
        check_vma=False,
    )
```

```python
import functools
import math

import jax
import jax.numpy as jnp
from jax import lax
from jax.experimental import pallas as pl
from jax.experimental.pallas import tpu as pltpu
from jax.sharding import Mesh, PartitionSpec as P

H = 12
HD = 64
LEN = 237
PATCHES = 197
HEAD = 208
TAIL = 48
SEQ = HEAD + TAIL
D = H * HD
FF = 4 * D
BLK = 256
EPS = 1e-05
F32 = jnp.float32
BF16 = jnp.bfloat16
MIB = 1 << 20
ROWS_ONE = 864
ROWS_QKV = 304


def dot(a, b):
    return jnp.dot(a, b, preferred_element_type=F32)


def dot_nt(a, b):
    return lax.dot_general(a, b, (((1,), (1,)), ((), ())), preferred_element_type=F32)


def dot_tn(a, b):
    return lax.dot_general(a, b, (((0,), (0,)), ((), ())), preferred_element_type=F32)


def mean(rows):
    return jnp.mean(rows, -1, keepdims=True)


def normalize(rows):
    centred = rows - mean(rows)
    inverse = lax.rsqrt(mean(centred * centred) + EPS)
    return centred * inverse, inverse


def normalize_back(grad, unit, inverse, gain):
    scaled = grad * gain
    return inverse * (scaled - mean(scaled) - unit * mean(scaled * unit))


def total(rows):
    return jnp.sum(rows, 0, keepdims=True)


def halves(pair):
    lane = lax.broadcasted_iota(jnp.int32, pair.shape, 1)
    zero = jnp.zeros_like(pair)
    return jnp.concatenate(
        [jnp.where(lane < HD, pair, zero), jnp.where(lane < HD, zero, pair)], 0
    )


def key_bias():
    key = lax.broadcasted_iota(jnp.int32, (1, SEQ), 1)
    valid = (key < PATCHES) | ((key >= HEAD) & (key < HEAD + LEN - PATCHES))
    return jnp.where(valid, 0.0, -1e30)


def softmax_pair(queries, keys_cat, bias):
    scores = dot_nt(queries, keys_cat)
    out = []
    for head in range(2):
        own = scores[:, head * SEQ : (head + 1) * SEQ] + bias
        powers = jnp.exp(own - jnp.max(own, -1, keepdims=True))
        out.append(powers * (1.0 / jnp.sum(powers, -1, keepdims=True)))
    return jnp.concatenate(out, 1)


def spans(where_ref, pieces, rows):
    if len(pieces) == 8:
        for j in range(8):
            yield pieces[j], where_ref[j], 0, rows
        return
    for side in range(2):
        for j in range(5):
            block = where_ref[4 * side + min(j, 3)]
            size = rows if j < 3 else rows // 2
            yield pieces[5 * side + j], block, (size if j == 4 else 0), size


def started(copies, sems, start=True):
    copies = [
        pltpu.make_async_copy(source, target, sems.at[j])
        for j, (source, target) in enumerate(copies)
    ]
    if start:
        for copy in copies:
            copy.start()
    return copies


def load_pieces(where_ref, pieces, target, sems, columns, start=True):
    return started(
        [
            (
                piece.at[:, pl.ds(columns[0], columns[1])],
                target.at[pl.ds(pl.multiple_of(block * 96 + first, 16), size), :],
            )
            for piece, block, first, size in spans(where_ref, pieces, 96)
        ],
        sems,
        start,
    )


def expert_copies(where_ref, pieces, up, down, sems):
    ups, downs = [[], [], [], []], []
    for piece, block, first, size in spans(where_ref, pieces, 768):
        if first == 0:
            for chunk in range(4):
                target = up.at[chunk, pl.ds(pl.multiple_of(block * 96, 96), 96), :]
                ups[chunk].append((piece.at[pl.ds(chunk * 96, 96), :], target))
        if first + size == 768:
            target = down.at[pl.ds(pl.multiple_of(block * 384, 384), 384), :]
            downs.append((block, piece.at[pl.ds(384 - first, 384), :], target))
    count = iter(range(40))
    ups = [[pltpu.make_async_copy(a, b, sems.at[next(count)]) for a, b in each] for each in ups]
    downs = [(k, pltpu.make_async_copy(a, b, sems.at[next(count)])) for k, a, b in downs]
    return ups, downs


def start_expert(copies):
    ups, downs = copies
    for copy in [*ups[0], *(copy for _, copy in downs), *ups[1], *ups[2], *ups[3]]:
        copy.start()


def wait_expert(copies, step):
    ups, downs = copies
    for chunk in range(4):
        pl.when(step == chunk)(functools.partial(wait_all, ups[chunk]))
    for block, copy in downs:
        pl.when(block // 2 == step)(copy.wait)


def wait_all(copies):
    for copy in copies:
        copy.wait()


def column(masked, seq):
    return jnp.transpose(masked[seq])[:, :1]


def attention_kernel(where_ref, tokens, masked, vector, *rest):
    pieces, rest = rest[:8], rest[8:]
    qkv, softs, context, normed_one, params, weights, sems = rest

    @pl.when(pl.program_id(0) == 0)
    def _():
        wait_all(load_pieces(where_ref, pieces, weights, sems, (0, weights.shape[1])))
        columns = weights[:, 4 * D : 4 * D + 128].astype(F32)
        params[...] = jnp.transpose(columns)[:8]

    start = jnp.where(column(masked, 0) == 1.0, vector[...], tokens[...].astype(F32))
    unit, _ = normalize(start)
    first = (unit * params[0:1] + params[1:2]).astype(BF16)
    normed_one[...] = first
    for third in range(3):
        at = pl.ds(third * D, D)
        qkv[:, at] = dot(first, weights[:, at]).astype(BF16)
    bias = key_bias()
    for pair in range(H // 2):
        queries = qkv[:, pl.ds(pair * 128, 128)] * BF16(1.0 / math.sqrt(HD))
        keys = halves(qkv[:, pl.ds(D + pair * 128, 128)])
        values = halves(qkv[:, pl.ds(2 * D + pair * 128, 128)])
        soft = softmax_pair(queries, keys, bias)
        softs[0, pair] = soft
        attention = soft.astype(BF16)
        context[:, pl.ds(pair * 128, 128)] = dot(attention, values).astype(BF16)


def chosen(place, block):
    row = lax.broadcasted_iota(jnp.int32, (BLK, place.shape[1]), 0) + block * BLK
    return jnp.where(row == place[...], 1.0, 0.0).astype(BF16)


def rows_of(block):
    return pl.ds(pl.multiple_of(block * BLK, BLK), BLK)


def feed_back_kernel(where_ref, place, vector, cotangent, context, params, *rest):
    pieces, attention_pieces, rest = rest[:10], rest[10:18], rest[18:]
    keep, send, send_far, grad_context, sums = rest[:5]
    rows_two, rows_hidden, rows_cot, rows_context, grad_two = rest[5:10]
    (sum_up, sum_down, w_up, w_down, w_out, stage) = rest[10:16]
    sems, attention_sems, out_sems = rest[16:]
    step = pl.program_id(0)
    blocks = where_ref[10]
    core = where_ref[8]

    expert_loads = expert_copies(where_ref, pieces, w_up, w_down, sems)

    @pl.when(step == 0)
    def _():
        copies = load_pieces(where_ref, attention_pieces, w_out, attention_sems, (3 * D, D))
        start_expert(expert_loads)

        def gather(block, _):
            pick, at = chosen(place, block), rows_of(block)
            rows_cot[at, :] = dot(pick, cotangent[...]).astype(BF16)
            rows_context[at, :] = dot(pick, context[...]).astype(BF16)
            grad_two[at, :] = jnp.zeros((BLK, D), F32)
            return 0

        def norm(block, _):
            at = rows_of(block)
            rows = vector[...] + dot(rows_context[at, :], w_out[...])
            rows_hidden[at, :] = rows
            unit, _ = normalize(rows)
            rows_two[at, :] = (unit * params[2:3] + params[3:4]).astype(BF16)
            return 0

        lax.fori_loop(0, blocks, gather, 0)
        wait_all(copies)
        lax.fori_loop(0, blocks, norm, 0)

    wait_expert(expert_loads, step)
    up = w_up.at[step]
    down = w_down.at[pl.ds(pl.multiple_of(step * D, D), D), :]

    up_at = pl.ds(pl.multiple_of(step * 96, 96), 96)
    mine = jnp.bitwise_xor(step, where_ref[9])

    def put(down_grad, up_grad):
        for block in range(8):
            side = jnp.bitwise_xor(block & 1, core)
            j = jnp.bitwise_xor(block >> 1, where_ref[9])
            stage[side, j, up_at, :] = up_grad[block * 96 : (block + 1) * 96].astype(BF16)
        for half in range(2):
            side = jnp.bitwise_xor(half, core)
            rows = down_grad[half * 384 : (half + 1) * 384]
            stage[side, mine, pl.ds(384, 384), :] = rows.astype(BF16)

    def expert(block, _):
        at = rows_of(block)
        rows, grads = rows_two[at, :], rows_cot[at, :]
        pre = dot(rows, up[...])
        chance = 0.5 * (1.0 + lax.erf(pre * math.sqrt(0.5)))
        activated = (pre * chance).astype(BF16)
        slope = chance + pre * (jnp.exp(-0.5 * pre * pre) * (1.0 / math.sqrt(2.0 * math.pi)))
        grad_pre = (dot_nt(grads, down[...]) * slope).astype(BF16)
        grad_two[at, :] += dot_nt(grad_pre, up[...])

        @pl.when(blocks == 1)
        def _():
            put(dot_tn(activated, grads), dot_tn(rows, grad_pre))

        @pl.when((blocks > 1) & (block == 0))
        def _():
            sum_down[...] = dot_tn(activated, grads)
            sum_up[...] = dot_tn(rows, grad_pre)

        @pl.when(block > 0)
        def _():
            sum_down[...] += dot_tn(activated, grads)
            sum_up[...] += dot_tn(rows, grad_pre)

        return 0

    lax.fori_loop(0, blocks, expert, 0)

    def leaving(at_step):
        rows = pl.ds(pl.multiple_of(at_step * 96, 96), 96)
        columns = pl.ds(384, 384)
        mine = jnp.bitwise_xor(at_step, where_ref[9])
        near = jnp.minimum(mine, 2)
        sem = out_sems.at[at_step]
        return [
            (None, stage.at[0, :, rows, :], keep.at[:, rows, :], sem.at[0]),
            (None, stage.at[0, mine, columns, :], keep.at[mine, columns, :], sem.at[1]),
            (None, stage.at[1, pl.ds(0, 3), rows, :], send.at[:, rows, :], sem.at[2]),
            (None, stage.at[1, 3, rows, :], send_far.at[rows, :], sem.at[3]),
            (mine < 3, stage.at[1, near, columns, :], send.at[near, columns, :], sem.at[4]),
            (mine == 3, stage.at[1, 3, columns, :], send_far.at[columns, :], sem.at[4]),
        ]

    def each(copies, act):
        for when, source, target, sem in copies:
            copy = pltpu.make_async_copy(source, target, sem)
            if when is None:
                act(copy)
            else:
                pl.when(when)(functools.partial(act, copy))

    @pl.when(blocks > 1)
    def _():
        put(sum_down[...], sum_up[...])

    each(leaving(step), lambda copy: copy.start())

    @pl.when(step == pl.num_programs(0) - 1)
    def _():
        sums[...] = jnp.zeros_like(sums)

        def back(block, _):
            at = rows_of(block)
            unit, inverse = normalize(rows_hidden[at, :])
            grad = grad_two[at, :]
            grad_hidden = rows_cot[at, :].astype(F32) + normalize_back(
                grad, unit, inverse, params[2:3]
            )
            sums[0:1] += total(grad * unit)
            sums[1:2] += total(grad)
            sums[2:3] += total(grad_hidden)
            grad_attn = grad_hidden.astype(BF16)
            rows_two[at, :] = grad_attn

            @pl.when(block == 0)
            def _():
                sum_up[...] = dot_tn(rows_context[at, :], grad_attn)

            @pl.when(block > 0)
            def _():
                sum_up[...] += dot_tn(rows_context[at, :], grad_attn)

            return 0

        def spread(block, _):
            rows = dot_nt(rows_two[rows_of(block), :], w_out[...]).astype(BF16)

            @pl.when(block == 0)
            def _():
                grad_context[...] = dot_tn(chosen(place, block), rows).astype(BF16)

            @pl.when(block > 0)
            def _():
                grad_context[...] += dot_tn(chosen(place, block), rows).astype(BF16)

            return 0

        lax.fori_loop(0, blocks, back, 0)
        for side in range(2):
            for j in range(4):
                source = pl.ds(pl.multiple_of(where_ref[4 * side + j] * 96, 96), 96)
                stage[side, j, pl.ds(768, 96), :] = sum_up[source, :].astype(BF16)
        rows = pl.ds(768, 96)
        sem = out_sems.at[4]
        last = [
            (None, stage.at[0, :, rows, :], keep.at[:, rows, :], sem.at[0]),
            (None, stage.at[1, pl.ds(0, 3), rows, :], send.at[:, rows, :], sem.at[1]),
            (None, stage.at[1, 3, rows, :], send_far.at[rows, :], sem.at[2]),
        ]
        each(last, lambda copy: copy.start())
        lax.fori_loop(0, blocks, spread, 0)
        each(last, lambda copy: copy.wait())
        for at_step in range(4):
            each(leaving(at_step), lambda copy: copy.wait())


def put_rows(target, rows, seq):
    target[seq * LEN : seq * LEN + PATCHES] = rows[:PATCHES]
    target[seq * LEN + PATCHES : (seq + 1) * LEN] = rows[HEAD : HEAD + LEN - PATCHES]


def attention_back_kernel(
    where_ref, qkv, softs, grad_context, normed_one, tokens, masked, vector, params, before, *rest
):
    pieces = rest[:8]
    keep, send, grad_tokens = rest[8:11]
    weights, sums, grad_qkv, stage, sems, out_sems = rest[11:]
    step = pl.program_id(0)
    here = pl.ds(pl.multiple_of(step * SEQ, SEQ), SEQ)

    def copies():
        return load_pieces(where_ref, pieces, weights, sems, (0, 3 * D), False)

    @pl.when(step == 0)
    def _():
        for copy in copies():
            copy.start()
        sums[...] = before[...]

    inv_root = 1.0 / math.sqrt(HD)
    top = lax.broadcasted_iota(jnp.int32, (128, SEQ), 0) < HD
    for pair in range(H // 2):
        queries = qkv[:, pl.ds(pair * 128, 128)]
        keys = halves(qkv[:, pl.ds(D + pair * 128, 128)])
        values = halves(qkv[:, pl.ds(2 * D + pair * 128, 128)])
        grads = grad_context[:, pl.ds(pair * 128, 128)]
        grad_soft = dot_nt(grads, values)
        parts = []
        for head in range(2):
            span = slice(head * SEQ, (head + 1) * SEQ)
            own, grad = softs[0, pair, :, span], grad_soft[:, span]
            parts.append(own * (grad - jnp.sum(own * grad, -1, keepdims=True)))
        grad_scores = jnp.concatenate(parts, 1).astype(BF16)
        grad_qkv[here, pl.ds(pair * 128, 128)] = (dot(grad_scores, keys) * inv_root).astype(BF16)
        by_key = dot_tn(queries, grad_scores) * inv_root
        by_key = jnp.where(top, by_key[:, :SEQ], by_key[:, SEQ:])
        grad_qkv[here, pl.ds(D + pair * 128, 128)] = jnp.transpose(by_key).astype(BF16)
        by_value = dot_tn(grads, softs[0, pair].astype(BF16))
        by_value = jnp.where(top, by_value[:, :SEQ], by_value[:, SEQ:])
        grad_qkv[here, pl.ds(2 * D + pair * 128, 128)] = jnp.transpose(by_value).astype(BF16)

    @pl.when(step == 0)
    def _():
        wait_all(copies())

    grad_one = dot_nt(grad_qkv[here, :], weights[...])
    hidden_row = column(masked, 0) == 1.0
    start = jnp.where(hidden_row, vector[...], tokens[...].astype(F32))
    unit, inverse = normalize(start)
    grad_start = normalize_back(grad_one, unit, inverse, params[0:1])
    sums[3:4] += total(grad_one * unit)
    sums[4:5] += total(grad_one)
    sums[2:3] += total(jnp.where(hidden_row, grad_start, 0.0))
    kept = jnp.where(hidden_row, 0.0, grad_start)
    for seq in range(normed_one.shape[0] // SEQ):
        pl.when(step == seq)(functools.partial(put_rows, grad_tokens, kept, seq))

    @pl.when(step == pl.num_programs(0) - 1)
    def _():
        extra = jnp.concatenate([sums[...], jnp.zeros_like(sums[...])], 0).astype(BF16)
        for third in range(3):
            for part in range(3):
                at = pl.ds(third * D + part * SEQ, SEQ)
                add = dot_tn(normed_one[...], grad_qkv[:, at]).astype(BF16)
                for block in range(8):
                    stage[block, pl.ds(third * 96, 96), pl.ds(part * SEQ, SEQ)] = add[
                        block * 96 : (block + 1) * 96
                    ]
        out_copies = []
        for side, out in enumerate((keep, send)):
            for j in range(4):
                block = where_ref[4 * side + j]
                stage[block, pl.ds(3 * 96, 16), :] = extra
                out_copies.append((stage.at[block], out.at[j]))
        wait_all(started(out_copies, out_sems))


def gelu(pre):
    return (pre * (0.5 * (1.0 + lax.erf(pre * math.sqrt(0.5))))).astype(BF16)


def feed(text, where_ref, rows_in, sums, up, down, tails):
    seqs = rows_in.shape[0] // SEQ
    for seq in range(seqs):
        head = pl.ds(seq * SEQ, HEAD)

        @pl.when(where_ref[11 + seq] == int(text))
        def _():
            activated = gelu(dot(rows_in[head, :], up[...]))
            sums[head, :] += dot(activated, down[...])

    if text:
        more = dot(gelu(dot(tails[...], up[...])), down[...])
        for seq in range(seqs):
            sums[pl.ds(seq * SEQ + HEAD, TAIL), :] += more[seq * TAIL : (seq + 1) * TAIL]


def feed_text_kernel(where_ref, tokens, masked, vector, context, params, *rest):
    pieces, attention_pieces, rest = rest[:10], rest[10:18], rest[18:]
    out, normed_two, w_up, w_down, w_out, sems, attention_sems, tails = rest
    step = pl.program_id(0)

    expert_loads = expert_copies(where_ref, pieces, w_up, w_down, sems)

    @pl.when(step == 0)
    def _():
        copies = load_pieces(where_ref, attention_pieces, w_out, attention_sems, (3 * D, D))
        start_expert(expert_loads)
        wait_all(copies)
        for seq in range(tokens.shape[0] // SEQ):
            at = pl.ds(seq * SEQ, SEQ)
            start = jnp.where(column(masked, seq) == 1.0, vector[...], tokens[at, :].astype(F32))
            hidden = start + dot(context[at, :], w_out[...])
            out[at, :] = hidden
            unit, _ = normalize(hidden)
            second = (unit * params[2:3] + params[3:4]).astype(BF16)
            normed_two[at, :] = second
            tails[pl.ds(seq * TAIL, TAIL), :] = second[HEAD:]

    wait_expert(expert_loads, step)
    down = w_down.at[pl.ds(pl.multiple_of(step * D, D), D), :]
    feed(True, where_ref, normed_two, out, w_up.at[step], down, tails)


def feed_image_kernel(where_ref, rows_in, before, *rest):
    pieces, (out, sums, w_up, w_down, sems, flat) = rest[:10], rest[10:]
    step = pl.program_id(0)

    expert_loads = expert_copies(where_ref, pieces, w_up, w_down, sems)

    @pl.when(step == 0)
    def _():
        start_expert(expert_loads)
        sums[...] = before[...]

    wait_expert(expert_loads, step)
    down = w_down.at[pl.ds(pl.multiple_of(step * D, D), D), :]
    feed(False, where_ref, rows_in, sums, w_up.at[step], down, None)

    @pl.when(step == pl.num_programs(0) - 1)
    def _():
        for seq in range(rows_in.shape[0] // SEQ):
            put_rows(flat, sums[pl.ds(seq * SEQ, SEQ), :], seq)
        out[...] = flat[...].astype(BF16)


def whole(shape):
    return pl.BlockSpec(shape, lambda *_: (0,) * len(shape), pipeline_mode=pl.Buffered(1))


def by_step(shape):
    return pl.BlockSpec(shape, lambda i, *_: (i,) + (0,) * (len(shape) - 1))


ANY = pl.BlockSpec(memory_space=pl.ANY)


def call(kernel, steps, ins, in_specs, outs, out_specs, scratch, name):
    run = pl.pallas_call(
        kernel,
        out_shape=tuple(jax.ShapeDtypeStruct(s, d) for s, d in outs),
        grid_spec=pltpu.PrefetchScalarGridSpec(
            num_scalar_prefetch=1,
            grid=(steps,),
            in_specs=in_specs,
            out_specs=out_specs,
            scratch_shapes=scratch,
        ),
        compiler_params=pltpu.CompilerParams(vmem_limit_bytes=60 * MIB),
        cost_estimate=pl.CostEstimate(flops=1, bytes_accessed=1, transcendentals=0),
        name=name,
    )
    return run(*ins)


def lay(rows, seqs):
    rows = rows.reshape(seqs, LEN, -1)
    return jnp.concatenate(
        [
            jnp.pad(rows[:, :PATCHES], ((0, 0), (0, HEAD - PATCHES), (0, 0))),
            jnp.pad(rows[:, PATCHES:], ((0, 0), (0, TAIL - LEN + PATCHES), (0, 0))),
        ],
        1,
    ).reshape(seqs * SEQ, -1)


def tie(*trees):
    return lax.optimization_barrier(trees)


def in_order(rows, part, blocks=0, axis=0):
    rows = jnp.moveaxis(rows, axis, blocks)
    shape, columns = rows.shape[:blocks], rows.shape[-1]
    count, size = rows.shape[blocks], rows.shape[blocks + 1]
    if size == part:
        return rows.reshape(*shape, count * part, columns)
    up = rows[..., : 4 * part, :].reshape(*shape, count, 4, part, columns)
    up = jnp.swapaxes(up, blocks, blocks + 1).reshape(*shape, 4 * count * part, columns)
    down = rows[..., 4 * part :, :].reshape(*shape, count * (size - 4 * part), columns)
    return jnp.concatenate([up, down], -2)


class Cube:
    axes = ("y", "x", "core", "z")
    swap = [(0, 1), (1, 0)]

    def __init__(self):
        y, x, core, z = (lax.axis_index(a) for a in self.axes)
        self.z, self.core, self.flat = z, core, y * 2 + x
        self.index = ((y * 2 + x) * 2 + core) * 4 + z

    def turn(self, block, k):
        return lax.ppermute(block, "z", [(i, (i + k) % 4) for i in range(4)])

    def turns(self, block):
        return [block] + [self.turn(block, k) for k in (1, 2, 3)]

    def ring(self, ring, part):
        out = []
        for place in range(4):
            k = lax.rem(self.z + 4 - place, 4)
            out.append(
                jnp.where(
                    k == 0,
                    ring[0],
                    jnp.where(k == 1, ring[1], jnp.where(k == 2, ring[2], ring[3])),
                )
            )
        return in_order(jnp.stack(out), part)

    def swapped(self, block, axis):
        return lax.ppermute(block, axis, self.swap)

    def sides(self, own):
        return own, self.swapped(own, "x"), self.swapped(own, "y")

    def halves(self, near):
        half = near[0].shape[0] // 2
        return near[1][:half], near[2][half:]

    def to_corners(self, near, halves):
        return (*near, self.swapped(halves[0], "y"), self.swapped(halves[1], "x"))

    def corner(self, near):
        return self.to_corners(near, self.halves(near))

    def cores(self, near):
        return [*near] + [self.swapped(b, "core") for b in near]

    def plane(self, j, block):
        if j == 1:
            return self.swapped(block, "x")
        if j == 2:
            return self.swapped(block, "y")
        return lax.ppermute(block, ("y", "x"), [(i, 3 - i) for i in range(4)])

    def to_core(self, block):
        return self.swapped(block, "core")

    def far_sums(self, keep, got):
        half = got.shape[0] // 2
        return [
            (keep[3, at].astype(F32) + got[at].astype(F32)).astype(BF16)
            for at in (slice(half), slice(half, None))
        ]

    def to_corner(self, both):
        return self.swapped(both[0], "x"), self.swapped(both[1], "y")

    def side_sums(self, keep, got, corner):
        half = corner[0].shape[0]
        by_x = jnp.pad(corner[0], ((0, half), (0, 0))).astype(F32)
        by_y = jnp.pad(corner[1], ((half, 0), (0, 0))).astype(F32)
        to_x = keep[1].astype(F32) + got[1].astype(F32) + by_y
        to_y = keep[2].astype(F32) + got[2].astype(F32) + by_x
        return [keep, got, to_x.astype(BF16), to_y.astype(BF16)]

    def to_sides(self, sums):
        return [*sums[:2], self.swapped(sums[2], "x"), self.swapped(sums[3], "y")]

    def plane_sums(self, keep, got, rows):
        both = [keep[j, :rows].astype(F32) + got[j, :rows].astype(F32) for j in (1, 2, 3)]
        return [keep, got] + [b.astype(BF16) for b in both]

    def to_plane(self, sums):
        return sums[:2] + [self.plane(j, sums[j + 1]) for j in (1, 2, 3)]

    def square(self, own):
        return [own] + [self.plane(j, own) for j in (1, 2, 3)]

    def square_cores(self, near):
        return [*near] + [self.swapped(b, "core") for b in near]

    def last(self, near):
        return near[3:]

    def cores_of(self, near, last):
        return self.cores([*near[:3], *last])

    def far_cores(self, near):
        return [self.swapped(b, "core") for b in near]

    def all_cores(self, near, far, last):
        return [*near, *far, *last]

    def ring_sums(self, group, fields):
        keep, got, *more = group
        rows = more[0].shape[0]
        mine = sum(m.astype(F32) for m in (keep[0, :rows], got[0, :rows], *more))
        rounded = lax.optimization_barrier(mine.astype(BF16))
        return [cut(mine, fields, self.z)] + [
            cut(rounded, fields, lax.rem(self.z + k, 4)) for k in (1, 2, 3)
        ]

    def to_ring(self, parts, which):
        return [self.turn(p, k) if k in which else p for k, p in enumerate(parts)]

    def add_ring(self, ring):
        return ring[0] + sum(m.astype(F32) for m in ring[1:])


class Flat:
    axes = ("dp", "fsdp")

    def __init__(self, count):
        self.flat = self.core = jnp.int32(0)
        self.index = lax.axis_index(self.axes)
        self.count = count

    def turns(self, block):
        return lax.all_gather(block, self.axes, axis=0)

    def ring(self, full, part):
        return in_order(full.reshape((8, -1) + full.shape[1:]), part, 1, 1)

    def sides(self, own):
        return own

    def halves(self, near):
        return ()

    def to_corners(self, near, halves):
        return near

    def corner(self, near):
        return near

    def cores(self, near):
        half = near.shape[1] // 2
        out = []
        for side in range(2):
            out += [near[side], near[2 + side], near[4 + side]]
            out += [near[6 + side, :half], near[6 + side, half:]]
        return out

    def to_core(self, block):
        return block

    def far_sums(self, keep, got):
        return got

    def to_corner(self, both):
        return both

    def side_sums(self, keep, got, corner):
        return self.plane_sums(keep, jnp.concatenate([got, corner[None]]), None)

    def to_sides(self, sums):
        return sums

    def plane_sums(self, keep, got, rows):
        return [jnp.stack([keep, got], 1).reshape((8,) + keep.shape[1:])]

    def to_plane(self, sums):
        return sums

    def square(self, own):
        return own

    def square_cores(self, near):
        return [near[b] for b in (0, 2, 4, 6, 1, 3, 5, 7)]

    def last(self, near):
        return ()

    def cores_of(self, near, last):
        return self.cores(near)

    def far_cores(self, near):
        return ()

    def all_cores(self, near, far, last):
        return self.cores(near)

    def ring_sums(self, group, fields):
        ways = self.count // 8
        parts = [[cut(block, fields, w, ways) for w in range(ways)] for block in group[0]]
        return jnp.stack([p for block in parts for p in block]).astype(F32)

    def to_ring(self, parts, which):
        if 3 not in which:
            return parts
        return lax.psum_scatter(parts, self.axes, scatter_dimension=0, tiled=False)

    def add_ring(self, ring):
        return ring


def pack_expert(up, down):
    part = up.shape[0]
    up = up.reshape(part, 4, D).transpose(1, 0, 2).reshape(4 * part, D)
    return jnp.concatenate([up, down], 0)


def cut(rows, fields, place, ways=4):
    out, at = [], 0
    for groups, size in fields:
        part = rows[at : at + max(groups, 1) * size]
        at += max(groups, 1) * size
        if groups:
            part = part.reshape(groups, ways, size // ways, D)
            part = lax.dynamic_index_in_dim(part, place, 1, keepdims=False).reshape(-1, D)
        out.append(part)
    return jnp.concatenate(out)


def layer(
    make,
    tokens,
    modality,
    token_mask,
    cotangent,
    mask_vector,
    ln_one_gain,
    ln_one_shift,
    w_qkv,
    w_out,
    ln_two_gain,
    ln_two_shift,
    w_up,
    w_down,
):
    net = make()
    part = w_qkv.shape[0]
    seqs = tokens.shape[0] // LEN
    rows = seqs * SEQ
    columns = jnp.stack([ln_one_gain, ln_one_shift, ln_two_gain, ln_two_shift], 1)
    packed = jnp.concatenate([w_qkv, w_out, jnp.pad(columns, ((0, 0), (0, 124)))], 1)
    n_columns = packed.shape[1]
    ring = net.turns(packed)

    seq_masks = token_mask.reshape(seqs, LEN)
    masked = jnp.concatenate(
        [
            jnp.pad(seq_masks[:, :PATCHES], ((0, 0), (0, HEAD - PATCHES))),
            jnp.pad(seq_masks[:, PATCHES:], ((0, 0), (0, TAIL - LEN + PATCHES))),
        ],
        1,
    ).reshape(1, rows)
    order = jnp.cumsum(masked, 1)
    place = jnp.where(masked == 1, order - 1, -1)
    blocks = jnp.maximum((order[0, rows - 1] + BLK - 1) // BLK, 1)
    near = jnp.arange(8, dtype=jnp.int32)
    near = jnp.bitwise_xor(net.flat, near & 3) * 2 + jnp.bitwise_xor(net.core, near >> 2)
    where_ref = jnp.concatenate(
        [
            near,
            jnp.stack([net.core, net.flat, blocks]).astype(jnp.int32),
            modality.reshape(seqs, LEN)[:, 0],
        ]
    )
    masked = jnp.broadcast_to(masked.reshape(seqs, 1, SEQ), (seqs, 8, SEQ)).astype(F32)
    ring, where_ref = tie(ring, where_ref)

    own = net.ring(ring, part)
    near = net.square(own)
    text, _ = tie(pack_expert(w_up[1], w_down[1]), own)
    ring_text = net.turns(text)
    tokens, cotangent, _ = tie(tokens, cotangent, own)
    tokens = lay(tokens, seqs)
    cotangent = lay(cotangent, seqs)
    vector = mask_vector.astype(F32).reshape(1, D)
    near, place, tokens, cotangent, vector = tie(near, place, tokens, cotangent, vector)
    pieces = net.square_cores(near)
    own_text = net.ring(ring_text, part)
    pieces, own_text, image = tie(pieces, own_text, pack_expert(w_up[0], w_down[0]))
    near_text = net.sides(own_text)
    image = net.turns(image)

    qkv, softs, context, normed_one, params = call(
        attention_kernel,
        seqs,
        (where_ref, tokens, masked, vector, *pieces),
        [by_step((SEQ, D)), by_step((1, 8, SEQ)), whole((1, D))] + [ANY] * 8,
        [
            ((rows, 3 * D), BF16),
            ((seqs, H // 2, SEQ, 2 * SEQ), F32),
            ((rows, D), BF16),
            ((rows, D), BF16),
            ((8, D), F32),
        ],
        [
            by_step((SEQ, 3 * D)),
            by_step((1, H // 2, SEQ, 2 * SEQ)),
            by_step((SEQ, D)),
            by_step((SEQ, D)),
            pl.BlockSpec((8, D), lambda i, *_: (0, 0)),
        ],
        [pltpu.VMEM((D, n_columns), BF16), pltpu.SemaphoreType.DMA((10,))],
        "attention",
    )

    near_text, image, qkv, softs, context, normed_one, params = tie(
        near_text, image, qkv, softs, context, normed_one, params
    )
    near_text = net.corner(near_text)
    last, image = tie(net.last(near_text), net.ring(image, part))
    pieces_text = net.cores_of(near_text, last)
    near_image = net.sides(image)

    block = (ROWS_ONE, D)
    keep, send, send_far, grad_context, sums = call(
        feed_back_kernel,
        4,
        (where_ref, place, vector, cotangent, context, params, *pieces_text, *pieces),
        [whole((1, rows)), whole((1, D)), whole((rows, D)), whole((rows, D)), whole((8, D))]
        + [ANY] * 18,
        [((4, *block), BF16), ((3, *block), BF16), (block, BF16), ((rows, D), BF16), ((8, D), F32)],
        [ANY] * 3 + [whole((rows, D)), whole((8, D))],
        [
            pltpu.VMEM((rows, D), BF16),
            pltpu.VMEM((rows, D), F32),
            pltpu.VMEM((rows, D), BF16),
            pltpu.VMEM((rows, D), BF16),
            pltpu.VMEM((rows, D), F32),
        ]
        + [pltpu.VMEM((D, D), F32)] * 2
        + [
            pltpu.VMEM((4, D, D), BF16),
            pltpu.VMEM((FF, D), BF16),
            pltpu.VMEM((D, D), BF16),
            pltpu.VMEM((2, 4, *block), BF16),
            pltpu.SemaphoreType.DMA((40,)),
            pltpu.SemaphoreType.DMA((10,)),
            pltpu.SemaphoreType.DMA((5, 5)),
        ],
        "feed_back",
    )
    near_image, keep, send, send_far, grad_context, sums = tie(
        near_image, keep, send, send_far, grad_context, sums
    )
    far = net.far_sums(keep, net.to_core(send_far))
    halves_image = net.halves(near_image)
    far, send, context, halves_image = tie(far, send, context, halves_image)
    got = net.to_core(send)
    corner = net.to_corner(far)
    near_image = net.to_corners(near_image, halves_image)
    experts = [pltpu.VMEM((4, D, D), BF16), pltpu.VMEM((FF, D), BF16)]
    after, normed_two = call(
        feed_text_kernel,
        4,
        (where_ref, tokens, masked, vector, context, params, *pieces_text, *pieces),
        [whole((rows, D)), whole((seqs, 8, SEQ)), whole((1, D)), whole((rows, D)), whole((8, D))]
        + [ANY] * 18,
        [((rows, D), F32), ((rows, D), BF16)],
        [whole((rows, D))] * 2,
        experts
        + [
            pltpu.VMEM((D, D), BF16),
            pltpu.SemaphoreType.DMA((40,)),
            pltpu.SemaphoreType.DMA((10,)),
            pltpu.VMEM((seqs * TAIL, D), BF16),
        ],
        "feed_text",
    )
    corner, got, near_image, after = tie(corner, got, near_image, after)
    sums_feed = net.side_sums(keep, got, corner)
    last_image = net.far_cores(net.last(near_image))
    sums_feed, grad_context, last_image = tie(sums_feed, grad_context, last_image)
    sums_feed = net.to_sides(sums_feed)
    far_image = net.far_cores(near_image[:3])

    keep, send, grad_tokens = call(
        attention_back_kernel,
        seqs,
        (where_ref, qkv, softs, grad_context, normed_one, tokens, masked, vector, params, sums)
        + tuple(pieces),
        [
            by_step((SEQ, 3 * D)),
            by_step((1, H // 2, SEQ, 2 * SEQ)),
            by_step((SEQ, D)),
            whole((rows, D)),
            by_step((SEQ, D)),
            by_step((1, 8, SEQ)),
            whole((1, D)),
            whole((8, D)),
            whole((8, D)),
        ]
        + [ANY] * 8,
        [((4, ROWS_QKV, D), BF16), ((4, ROWS_QKV, D), BF16), ((seqs * LEN, D), F32)],
        [ANY, ANY, whole((seqs * LEN, D))],
        [
            pltpu.VMEM((D, 3 * D), BF16),
            pltpu.VMEM((8, D), F32),
            pltpu.VMEM((rows, 3 * D), BF16),
            pltpu.VMEM((8, ROWS_QKV, D), BF16),
            pltpu.SemaphoreType.DMA((10,)),
            pltpu.SemaphoreType.DMA((8,)),
        ],
        "attention_back",
    )
    keep, send, grad_tokens, sums_feed, far_image = tie(
        keep, send, grad_tokens, sums_feed, far_image
    )
    got = net.to_core(send)
    pieces_image = net.all_cores(near_image, far_image, last_image)
    sums_qkv = net.plane_sums(keep, got, 296)
    ring_one = net.ring_sums(sums_feed, [(4, 96), (1, 384), (1, 96)])
    sums_qkv, ring_one, after, pieces_image = tie(sums_qkv, ring_one, after, pieces_image)
    sums_qkv = net.to_plane(sums_qkv)
    ring_one = net.to_ring(ring_one, (1, 2))
    (output,) = call(
        feed_image_kernel,
        4,
        (where_ref, normed_two, after, *pieces_image),
        [whole((rows, D)), whole((rows, D))] + [ANY] * 10,
        [((seqs * LEN, D), BF16)],
        [whole((seqs * LEN, D))],
        [pltpu.VMEM((rows, D), F32)]
        + experts
        + [pltpu.SemaphoreType.DMA((40,)), pltpu.VMEM((seqs * LEN, D), F32)],
        "feed_image",
    )
    sums_qkv, ring_one, output = tie(sums_qkv, ring_one, output)
    ring_two = net.ring_sums(sums_qkv, [(3, 96), (0, 8)])
    ring_one = net.to_ring(ring_one, (3,))
    ring_two = net.to_ring(ring_two, (1, 2, 3))

    grads = net.add_ring(ring_one)
    grad_w_up = grads[: 4 * part].reshape(4, part, D).transpose(1, 0, 2).reshape(part, FF)
    grad_w_down = grads[4 * part : 8 * part]
    grad_w_out = grads[8 * part : 9 * part]
    grads = net.add_ring(ring_two)
    grad_w_qkv = grads[: 3 * part].reshape(3, part, D).transpose(1, 0, 2).reshape(part, 3 * D)
    extra = grads[3 * part :]
    owned = lax.dynamic_slice_in_dim(extra, net.index * part, part, 1)

    return (
        output,
        grad_tokens,
        extra[2],
        owned[3],
        owned[4],
        grad_w_qkv,
        grad_w_out,
        owned[0],
        owned[1],
        grad_w_up,
        grad_w_down,
    )


def solution(mesh):
    if (mesh.shape["dp"], mesh.shape["fsdp"]) == (8, 4):
        mesh = Mesh(mesh.devices.reshape(2, 2, 2, 4), Cube.axes)
        make = Cube
    else:
        make = functools.partial(Flat, mesh.size)
    axes = Cube.axes if make is Cube else Flat.axes
    row, flat = P(axes, None), P(axes)
    middle = P(None, axes, None)
    in_specs = (row, flat, flat, row, P(), flat, flat, row, row, flat, flat, middle, middle)
    out_specs = (row, row, P(), flat, flat, row, row, flat, flat, row, row)
    return jax.shard_map(
        functools.partial(layer, make),
        mesh=mesh,
        in_specs=in_specs,
        out_specs=out_specs,
        check_vma=False,
    )
```

```python
import functools
import math

import jax
import jax.numpy as jnp
from jax import lax
from jax.experimental import pallas as pl
from jax.experimental.pallas import tpu as pltpu
from jax.sharding import Mesh, PartitionSpec as P

H = 12
HD = 64
LEN = 237
PATCHES = 197
HEAD = 208
TAIL = 48
SEQ = HEAD + TAIL
D = H * HD
FF = 4 * D
BLK = 256
EPS = 1e-05
F32 = jnp.float32
BF16 = jnp.bfloat16
MIB = 1 << 20
ROWS_ONE = 864
ROWS_QKV = 304


def dot(a, b):
    return jnp.dot(a, b, preferred_element_type=F32)


def dot_nt(a, b):
    return lax.dot_general(a, b, (((1,), (1,)), ((), ())), preferred_element_type=F32)


def dot_tn(a, b):
    return lax.dot_general(a, b, (((0,), (0,)), ((), ())), preferred_element_type=F32)


def mean(rows):
    return jnp.mean(rows, -1, keepdims=True)


def normalize(rows):
    centred = rows - mean(rows)
    inverse = lax.rsqrt(mean(centred * centred) + EPS)
    return centred * inverse, inverse


def normalize_back(grad, unit, inverse, gain):
    scaled = grad * gain
    return inverse * (scaled - mean(scaled) - unit * mean(scaled * unit))


def total(rows):
    return jnp.sum(rows, 0, keepdims=True)


def halves(pair):
    lane = lax.broadcasted_iota(jnp.int32, pair.shape, 1)
    zero = jnp.zeros_like(pair)
    return jnp.concatenate(
        [jnp.where(lane < HD, pair, zero), jnp.where(lane < HD, zero, pair)], 0
    )


def key_bias():
    key = lax.broadcasted_iota(jnp.int32, (1, SEQ), 1)
    valid = (key < PATCHES) | ((key >= HEAD) & (key < HEAD + LEN - PATCHES))
    return jnp.where(valid, 0.0, -1e30)


def softmax_pair(queries, keys_cat, bias):
    scores = dot_nt(queries, keys_cat)
    out = []
    for head in range(2):
        own = scores[:, head * SEQ : (head + 1) * SEQ] + bias
        powers = jnp.exp(own - jnp.max(own, -1, keepdims=True))
        out.append(powers * (1.0 / jnp.sum(powers, -1, keepdims=True)))
    return jnp.concatenate(out, 1)


def spans(where_ref, pieces, rows):
    if len(pieces) == 8:
        for j in range(8):
            yield pieces[j], where_ref[j], 0, rows
        return
    for side in range(2):
        for j in range(5):
            block = where_ref[4 * side + min(j, 3)]
            size = rows if j < 3 else rows // 2
            yield pieces[5 * side + j], block, (size if j == 4 else 0), size


def started(copies, sems, start=True):
    copies = [
        pltpu.make_async_copy(source, target, sems.at[j])
        for j, (source, target) in enumerate(copies)
    ]
    if start:
        for copy in copies:
            copy.start()
    return copies


def load_pieces(where_ref, pieces, target, sems, columns, start=True):
    return started(
        [
            (
                piece.at[:, pl.ds(columns[0], columns[1])],
                target.at[pl.ds(pl.multiple_of(block * 96 + first, 16), size), :],
            )
            for piece, block, first, size in spans(where_ref, pieces, 96)
        ],
        sems,
        start,
    )


def expert_copies(where_ref, pieces, up, down, sems):
    ups, downs = [[], [], [], []], []
    for piece, block, first, size in spans(where_ref, pieces, 768):
        if first == 0:
            for chunk in range(4):
                target = up.at[chunk, pl.ds(pl.multiple_of(block * 96, 96), 96), :]
                ups[chunk].append((piece.at[pl.ds(chunk * 96, 96), :], target))
        if first + size == 768:
            target = down.at[pl.ds(pl.multiple_of(block * 384, 384), 384), :]
            downs.append((block, piece.at[pl.ds(384 - first, 384), :], target))
    count = iter(range(40))
    ups = [[pltpu.make_async_copy(a, b, sems.at[next(count)]) for a, b in each] for each in ups]
    downs = [(k, pltpu.make_async_copy(a, b, sems.at[next(count)])) for k, a, b in downs]
    return ups, downs


def start_expert(copies):
    ups, downs = copies
    for copy in [*ups[0], *(copy for _, copy in downs), *ups[1], *ups[2], *ups[3]]:
        copy.start()


def wait_expert(copies, step):
    ups, downs = copies
    for chunk in range(4):
        pl.when(step == chunk)(functools.partial(wait_all, ups[chunk]))
    for block, copy in downs:
        pl.when(block // 2 == step)(copy.wait)


def wait_all(copies):
    for copy in copies:
        copy.wait()


def column(masked, seq):
    return jnp.transpose(masked[seq])[:, :1]


def attention_kernel(where_ref, tokens, masked, vector, *rest):
    pieces, rest = rest[:8], rest[8:]
    qkv, softs, context, normed_one, params, weights, sems = rest

    @pl.when(pl.program_id(0) == 0)
    def _():
        wait_all(load_pieces(where_ref, pieces, weights, sems, (0, weights.shape[1])))
        columns = weights[:, 4 * D : 4 * D + 128].astype(F32)
        params[...] = jnp.transpose(columns)[:8]

    start = jnp.where(column(masked, 0) == 1.0, vector[...], tokens[...].astype(F32))
    unit, _ = normalize(start)
    first = (unit * params[0:1] + params[1:2]).astype(BF16)
    normed_one[...] = first
    for third in range(3):
        at = pl.ds(third * D, D)
        qkv[:, at] = dot(first, weights[:, at]).astype(BF16)
    bias = key_bias()
    for pair in range(H // 2):
        queries = qkv[:, pl.ds(pair * 128, 128)] * BF16(1.0 / math.sqrt(HD))
        keys = halves(qkv[:, pl.ds(D + pair * 128, 128)])
        values = halves(qkv[:, pl.ds(2 * D + pair * 128, 128)])
        soft = softmax_pair(queries, keys, bias)
        softs[0, pair] = soft
        attention = soft.astype(BF16)
        context[:, pl.ds(pair * 128, 128)] = dot(attention, values).astype(BF16)


def chosen(place, block):
    row = lax.broadcasted_iota(jnp.int32, (BLK, place.shape[1]), 0) + block * BLK
    return jnp.where(row == place[...], 1.0, 0.0).astype(BF16)


def rows_of(block):
    return pl.ds(pl.multiple_of(block * BLK, BLK), BLK)


def feed_back_kernel(where_ref, place, vector, cotangent, context, params, *rest):
    pieces, attention_pieces, rest = rest[:10], rest[10:18], rest[18:]
    keep, send, send_far, grad_context, sums = rest[:5]
    rows_two, rows_hidden, rows_cot, rows_context, grad_two = rest[5:10]
    (sum_up, sum_down, w_up, w_down, w_out, stage) = rest[10:16]
    sems, attention_sems, out_sems = rest[16:]
    step = pl.program_id(0)
    blocks = where_ref[10]
    core = where_ref[8]

    expert_loads = expert_copies(where_ref, pieces, w_up, w_down, sems)

    @pl.when(step == 0)
    def _():
        copies = load_pieces(where_ref, attention_pieces, w_out, attention_sems, (3 * D, D))
        start_expert(expert_loads)

        def gather(block, _):
            pick, at = chosen(place, block), rows_of(block)
            rows_cot[at, :] = dot(pick, cotangent[...]).astype(BF16)
            rows_context[at, :] = dot(pick, context[...]).astype(BF16)
            grad_two[at, :] = jnp.zeros((BLK, D), F32)
            return 0

        def norm(block, _):
            at = rows_of(block)
            rows = vector[...] + dot(rows_context[at, :], w_out[...])
            rows_hidden[at, :] = rows
            unit, _ = normalize(rows)
            rows_two[at, :] = (unit * params[2:3] + params[3:4]).astype(BF16)
            return 0

        lax.fori_loop(0, blocks, gather, 0)
        wait_all(copies)
        lax.fori_loop(0, blocks, norm, 0)

    wait_expert(expert_loads, step)
    up = w_up.at[step]
    down = w_down.at[pl.ds(pl.multiple_of(step * D, D), D), :]

    up_at = pl.ds(pl.multiple_of(step * 96, 96), 96)
    mine = jnp.bitwise_xor(step, where_ref[9])

    def put(down_grad, up_grad):
        for block in range(8):
            side = jnp.bitwise_xor(block & 1, core)
            j = jnp.bitwise_xor(block >> 1, where_ref[9])
            stage[side, j, up_at, :] = up_grad[block * 96 : (block + 1) * 96].astype(BF16)
        for half in range(2):
            side = jnp.bitwise_xor(half, core)
            rows = down_grad[half * 384 : (half + 1) * 384]
            stage[side, mine, pl.ds(384, 384), :] = rows.astype(BF16)

    def expert(block, _):
        at = rows_of(block)
        rows, grads = rows_two[at, :], rows_cot[at, :]
        pre = dot(rows, up[...])
        chance = 0.5 * (1.0 + lax.erf(pre * math.sqrt(0.5)))
        activated = (pre * chance).astype(BF16)
        slope = chance + pre * (jnp.exp(-0.5 * pre * pre) * (1.0 / math.sqrt(2.0 * math.pi)))
        grad_pre = (dot_nt(grads, down[...]) * slope).astype(BF16)
        grad_two[at, :] += dot_nt(grad_pre, up[...])

        @pl.when(blocks == 1)
        def _():
            put(dot_tn(activated, grads), dot_tn(rows, grad_pre))

        @pl.when((blocks > 1) & (block == 0))
        def _():
            sum_down[...] = dot_tn(activated, grads)
            sum_up[...] = dot_tn(rows, grad_pre)

        @pl.when(block > 0)
        def _():
            sum_down[...] += dot_tn(activated, grads)
            sum_up[...] += dot_tn(rows, grad_pre)

        return 0

    lax.fori_loop(0, blocks, expert, 0)

    def leaving(at_step):
        rows = pl.ds(pl.multiple_of(at_step * 96, 96), 96)
        columns = pl.ds(384, 384)
        mine = jnp.bitwise_xor(at_step, where_ref[9])
        near = jnp.minimum(mine, 2)
        sem = out_sems.at[at_step]
        return [
            (None, stage.at[0, :, rows, :], keep.at[:, rows, :], sem.at[0]),
            (None, stage.at[0, mine, columns, :], keep.at[mine, columns, :], sem.at[1]),
            (None, stage.at[1, pl.ds(0, 3), rows, :], send.at[:, rows, :], sem.at[2]),
            (None, stage.at[1, 3, rows, :], send_far.at[rows, :], sem.at[3]),
            (mine < 3, stage.at[1, near, columns, :], send.at[near, columns, :], sem.at[4]),
            (mine == 3, stage.at[1, 3, columns, :], send_far.at[columns, :], sem.at[4]),
        ]

    def each(copies, act):
        for when, source, target, sem in copies:
            copy = pltpu.make_async_copy(source, target, sem)
            if when is None:
                act(copy)
            else:
                pl.when(when)(functools.partial(act, copy))

    @pl.when(blocks > 1)
    def _():
        put(sum_down[...], sum_up[...])

    each(leaving(step), lambda copy: copy.start())

    @pl.when(step == pl.num_programs(0) - 1)
    def _():
        sums[...] = jnp.zeros_like(sums)

        def back(block, _):
            at = rows_of(block)
            unit, inverse = normalize(rows_hidden[at, :])
            grad = grad_two[at, :]
            grad_hidden = rows_cot[at, :].astype(F32) + normalize_back(
                grad, unit, inverse, params[2:3]
            )
            sums[0:1] += total(grad * unit)
            sums[1:2] += total(grad)
            sums[2:3] += total(grad_hidden)
            grad_attn = grad_hidden.astype(BF16)
            rows_two[at, :] = grad_attn

            @pl.when(block == 0)
            def _():
                sum_up[...] = dot_tn(rows_context[at, :], grad_attn)

            @pl.when(block > 0)
            def _():
                sum_up[...] += dot_tn(rows_context[at, :], grad_attn)

            return 0

        def spread(block, _):
            rows = dot_nt(rows_two[rows_of(block), :], w_out[...]).astype(BF16)

            @pl.when(block == 0)
            def _():
                grad_context[...] = dot_tn(chosen(place, block), rows).astype(BF16)

            @pl.when(block > 0)
            def _():
                grad_context[...] += dot_tn(chosen(place, block), rows).astype(BF16)

            return 0

        lax.fori_loop(0, blocks, back, 0)
        for side in range(2):
            for j in range(4):
                source = pl.ds(pl.multiple_of(where_ref[4 * side + j] * 96, 96), 96)
                stage[side, j, pl.ds(768, 96), :] = sum_up[source, :].astype(BF16)
        rows = pl.ds(768, 96)
        sem = out_sems.at[4]
        last = [
            (None, stage.at[0, :, rows, :], keep.at[:, rows, :], sem.at[0]),
            (None, stage.at[1, pl.ds(0, 3), rows, :], send.at[:, rows, :], sem.at[1]),
            (None, stage.at[1, 3, rows, :], send_far.at[rows, :], sem.at[2]),
        ]
        each(last, lambda copy: copy.start())
        lax.fori_loop(0, blocks, spread, 0)
        each(last, lambda copy: copy.wait())
        for at_step in range(4):
            each(leaving(at_step), lambda copy: copy.wait())


def put_rows(target, rows, seq):
    target[seq * LEN : seq * LEN + PATCHES] = rows[:PATCHES]
    target[seq * LEN + PATCHES : (seq + 1) * LEN] = rows[HEAD : HEAD + LEN - PATCHES]


def attention_back_kernel(
    where_ref, qkv, softs, grad_context, normed_one, tokens, masked, vector, params, before, *rest
):
    pieces = rest[:8]
    keep, send, grad_tokens = rest[8:11]
    weights, sums, grad_qkv, stage, flat, sems, out_sems = rest[11:]
    step = pl.program_id(0)
    here = pl.ds(pl.multiple_of(step * SEQ, SEQ), SEQ)

    def copies():
        return load_pieces(where_ref, pieces, weights, sems, (0, 3 * D), False)

    @pl.when(step == 0)
    def _():
        for copy in copies():
            copy.start()
        sums[...] = before[...]

    inv_root = 1.0 / math.sqrt(HD)
    top = lax.broadcasted_iota(jnp.int32, (128, SEQ), 0) < HD
    for pair in range(H // 2):
        queries = qkv[:, pl.ds(pair * 128, 128)]
        keys = halves(qkv[:, pl.ds(D + pair * 128, 128)])
        values = halves(qkv[:, pl.ds(2 * D + pair * 128, 128)])
        grads = grad_context[:, pl.ds(pair * 128, 128)]
        grad_soft = dot_nt(grads, values)
        parts = []
        for head in range(2):
            span = slice(head * SEQ, (head + 1) * SEQ)
            own, grad = softs[0, pair, :, span], grad_soft[:, span]
            parts.append(own * (grad - jnp.sum(own * grad, -1, keepdims=True)))
        grad_scores = jnp.concatenate(parts, 1).astype(BF16)
        grad_qkv[here, pl.ds(pair * 128, 128)] = (dot(grad_scores, keys) * inv_root).astype(BF16)
        by_key = dot_tn(queries, grad_scores) * inv_root
        by_key = jnp.where(top, by_key[:, :SEQ], by_key[:, SEQ:])
        grad_qkv[here, pl.ds(D + pair * 128, 128)] = jnp.transpose(by_key).astype(BF16)
        by_value = dot_tn(grads, softs[0, pair].astype(BF16))
        by_value = jnp.where(top, by_value[:, :SEQ], by_value[:, SEQ:])
        grad_qkv[here, pl.ds(2 * D + pair * 128, 128)] = jnp.transpose(by_value).astype(BF16)

    @pl.when(step == 0)
    def _():
        wait_all(copies())

    grad_one = dot_nt(grad_qkv[here, :], weights[...])
    hidden_row = column(masked, 0) == 1.0
    start = jnp.where(hidden_row, vector[...], tokens[...].astype(F32))
    unit, inverse = normalize(start)
    grad_start = normalize_back(grad_one, unit, inverse, params[0:1])
    sums[3:4] += total(grad_one * unit)
    sums[4:5] += total(grad_one)
    sums[2:3] += total(jnp.where(hidden_row, grad_start, 0.0))
    kept = jnp.where(hidden_row, 0.0, grad_start)
    for seq in range(normed_one.shape[0] // SEQ):
        pl.when(step == seq)(functools.partial(put_rows, flat, kept, seq))

    @pl.when(step == pl.num_programs(0) - 1)
    def _():
        extra = jnp.concatenate([sums[...], jnp.zeros_like(sums[...])], 0).astype(BF16)
        for third in range(3):
            for part in range(3):
                at = pl.ds(third * D + part * SEQ, SEQ)
                add = dot_tn(normed_one[...], grad_qkv[:, at]).astype(BF16)
                for block in range(8):
                    stage[block, pl.ds(third * 96, 96), pl.ds(part * SEQ, SEQ)] = add[
                        block * 96 : (block + 1) * 96
                    ]
        out_copies = []
        for side, out in enumerate((keep, send)):
            for j in range(4):
                block = where_ref[4 * side + j]
                stage[block, pl.ds(3 * 96, 16), :] = extra
                out_copies.append((stage.at[block], out.at[j]))
        out_copies = started(out_copies, out_sems)
        grad_tokens[...] = flat[: grad_tokens.shape[0]]
        wait_all(out_copies)


def gelu(pre):
    return (pre * (0.5 * (1.0 + lax.erf(pre * math.sqrt(0.5))))).astype(BF16)


def feed(text, where_ref, rows_in, sums, up, down, tails):
    seqs = rows_in.shape[0] // SEQ
    for seq in range(seqs):
        head = pl.ds(seq * SEQ, HEAD)

        @pl.when(where_ref[11 + seq] == int(text))
        def _():
            activated = gelu(dot(rows_in[head, :], up[...]))
            sums[head, :] += dot(activated, down[...])

    if text:
        more = dot(gelu(dot(tails[...], up[...])), down[...])
        for seq in range(seqs):
            sums[pl.ds(seq * SEQ + HEAD, TAIL), :] += more[seq * TAIL : (seq + 1) * TAIL]


def feed_text_kernel(where_ref, tokens, masked, vector, context, params, *rest):
    pieces, attention_pieces, rest = rest[:10], rest[10:18], rest[18:]
    out, normed_two, w_up, w_down, w_out, sems, attention_sems, tails = rest
    step = pl.program_id(0)

    expert_loads = expert_copies(where_ref, pieces, w_up, w_down, sems)

    @pl.when(step == 0)
    def _():
        copies = load_pieces(where_ref, attention_pieces, w_out, attention_sems, (3 * D, D))
        start_expert(expert_loads)
        wait_all(copies)
        for seq in range(tokens.shape[0] // SEQ):
            at = pl.ds(seq * SEQ, SEQ)
            start = jnp.where(column(masked, seq) == 1.0, vector[...], tokens[at, :].astype(F32))
            hidden = start + dot(context[at, :], w_out[...])
            out[at, :] = hidden
            unit, _ = normalize(hidden)
            second = (unit * params[2:3] + params[3:4]).astype(BF16)
            normed_two[at, :] = second
            tails[pl.ds(seq * TAIL, TAIL), :] = second[HEAD:]

    wait_expert(expert_loads, step)
    down = w_down.at[pl.ds(pl.multiple_of(step * D, D), D), :]
    feed(True, where_ref, normed_two, out, w_up.at[step], down, tails)


def feed_image_kernel(where_ref, rows_in, before, *rest):
    pieces, (out, sums, w_up, w_down, sems, flat) = rest[:10], rest[10:]
    step = pl.program_id(0)

    expert_loads = expert_copies(where_ref, pieces, w_up, w_down, sems)

    @pl.when(step == 0)
    def _():
        start_expert(expert_loads)
        sums[...] = before[...]

    wait_expert(expert_loads, step)
    down = w_down.at[pl.ds(pl.multiple_of(step * D, D), D), :]
    feed(False, where_ref, rows_in, sums, w_up.at[step], down, None)

    @pl.when(step == pl.num_programs(0) - 1)
    def _():
        for seq in range(rows_in.shape[0] // SEQ):
            put_rows(flat, sums[pl.ds(seq * SEQ, SEQ), :], seq)
        out[...] = flat[: out.shape[0]].astype(BF16)


def whole(shape):
    return pl.BlockSpec(shape, lambda *_: (0,) * len(shape), pipeline_mode=pl.Buffered(1))


def by_step(shape):
    return pl.BlockSpec(shape, lambda i, *_: (i,) + (0,) * (len(shape) - 1))


ANY = pl.BlockSpec(memory_space=pl.ANY)


def call(kernel, steps, ins, in_specs, outs, out_specs, scratch, name):
    run = pl.pallas_call(
        kernel,
        out_shape=tuple(jax.ShapeDtypeStruct(s, d) for s, d in outs),
        grid_spec=pltpu.PrefetchScalarGridSpec(
            num_scalar_prefetch=1,
            grid=(steps,),
            in_specs=in_specs,
            out_specs=out_specs,
            scratch_shapes=scratch,
        ),
        compiler_params=pltpu.CompilerParams(vmem_limit_bytes=60 * MIB),
        cost_estimate=pl.CostEstimate(flops=1, bytes_accessed=1, transcendentals=0),
        name=name,
    )
    return run(*ins)


def lay(rows, seqs):
    rows = rows.reshape(seqs, LEN, -1)
    return jnp.concatenate(
        [
            jnp.pad(rows[:, :PATCHES], ((0, 0), (0, HEAD - PATCHES), (0, 0))),
            jnp.pad(rows[:, PATCHES:], ((0, 0), (0, TAIL - LEN + PATCHES), (0, 0))),
        ],
        1,
    ).reshape(seqs * SEQ, -1)


def tie(*trees):
    return lax.optimization_barrier(trees)


def in_order(rows, part, blocks=0, axis=0):
    rows = jnp.moveaxis(rows, axis, blocks)
    shape, columns = rows.shape[:blocks], rows.shape[-1]
    count, size = rows.shape[blocks], rows.shape[blocks + 1]
    if size == part:
        return rows.reshape(*shape, count * part, columns)
    up = rows[..., : 4 * part, :].reshape(*shape, count, 4, part, columns)
    up = jnp.swapaxes(up, blocks, blocks + 1).reshape(*shape, 4 * count * part, columns)
    down = rows[..., 4 * part :, :].reshape(*shape, count * (size - 4 * part), columns)
    return jnp.concatenate([up, down], -2)


class Cube:
    axes = ("y", "x", "core", "z")
    swap = [(0, 1), (1, 0)]

    def __init__(self):
        y, x, core, z = (lax.axis_index(a) for a in self.axes)
        self.z, self.core, self.flat = z, core, y * 2 + x
        self.index = ((y * 2 + x) * 2 + core) * 4 + z

    def turn(self, block, k):
        return lax.ppermute(block, "z", [(i, (i + k) % 4) for i in range(4)])

    def turns(self, block):
        return [block] + [self.turn(block, k) for k in (1, 2, 3)]

    def ring(self, ring, part):
        out = []
        for place in range(4):
            k = lax.rem(self.z + 4 - place, 4)
            out.append(
                jnp.where(
                    k == 0,
                    ring[0],
                    jnp.where(k == 1, ring[1], jnp.where(k == 2, ring[2], ring[3])),
                )
            )
        return in_order(jnp.stack(out), part)

    def swapped(self, block, axis):
        return lax.ppermute(block, axis, self.swap)

    def sides(self, own):
        return own, self.swapped(own, "x"), self.swapped(own, "y")

    def halves(self, near):
        half = near[0].shape[0] // 2
        return near[1][:half], near[2][half:]

    def to_corners(self, near, halves):
        return (*near, self.swapped(halves[0], "y"), self.swapped(halves[1], "x"))

    def corner(self, near):
        return self.to_corners(near, self.halves(near))

    def cores(self, near):
        return [*near] + [self.swapped(b, "core") for b in near]

    def plane(self, j, block):
        if j == 1:
            return self.swapped(block, "x")
        if j == 2:
            return self.swapped(block, "y")
        return lax.ppermute(block, ("y", "x"), [(i, 3 - i) for i in range(4)])

    def to_core(self, block):
        return self.swapped(block, "core")

    def far_sums(self, keep, got):
        half = got.shape[0] // 2
        return [
            (keep[3, at].astype(F32) + got[at].astype(F32)).astype(BF16)
            for at in (slice(half), slice(half, None))
        ]

    def to_corner(self, both):
        return self.swapped(both[0], "x"), self.swapped(both[1], "y")

    def side_sums(self, keep, got, corner):
        half = corner[0].shape[0]
        by_x = jnp.pad(corner[0], ((0, half), (0, 0))).astype(F32)
        by_y = jnp.pad(corner[1], ((half, 0), (0, 0))).astype(F32)
        to_x = keep[1].astype(F32) + got[1].astype(F32) + by_y
        to_y = keep[2].astype(F32) + got[2].astype(F32) + by_x
        return [keep, got, to_x.astype(BF16), to_y.astype(BF16)]

    def to_sides(self, sums):
        return [*sums[:2], self.swapped(sums[2], "x"), self.swapped(sums[3], "y")]

    def plane_sums(self, keep, got, rows):
        both = [keep[j, :rows].astype(F32) + got[j, :rows].astype(F32) for j in (1, 2, 3)]
        return [keep, got] + [b.astype(BF16) for b in both]

    def to_plane(self, sums):
        return sums[:2] + [self.plane(j, sums[j + 1]) for j in (1, 2, 3)]

    def square(self, own):
        return [own] + [self.plane(j, own) for j in (1, 2, 3)]

    def square_cores(self, near):
        return [*near] + [self.swapped(b, "core") for b in near]

    def last(self, near):
        return near[3:]

    def cores_of(self, near, last):
        return self.cores([*near[:3], *last])

    def far_cores(self, near):
        return [self.swapped(b, "core") for b in near]

    def all_cores(self, near, far, last):
        return [*near, *far, *last]

    def ring_sums(self, group, fields):
        keep, got, *more = group
        rows = more[0].shape[0]
        mine = sum(m.astype(F32) for m in (keep[0, :rows], got[0, :rows], *more))
        rounded = lax.optimization_barrier(mine.astype(BF16))
        return [cut(mine, fields, self.z)] + [
            cut(rounded, fields, lax.rem(self.z + k, 4)) for k in (1, 2, 3)
        ]

    def to_ring(self, parts, which):
        return [self.turn(p, k) if k in which else p for k, p in enumerate(parts)]

    def add_ring(self, ring):
        return ring[0] + sum(m.astype(F32) for m in ring[1:])


class Flat:
    axes = ("dp", "fsdp")

    def __init__(self, count):
        self.flat = self.core = jnp.int32(0)
        self.index = lax.axis_index(self.axes)
        self.count = count

    def turns(self, block):
        return lax.all_gather(block, self.axes, axis=0)

    def ring(self, full, part):
        return in_order(full.reshape((8, -1) + full.shape[1:]), part, 1, 1)

    def sides(self, own):
        return own

    def halves(self, near):
        return ()

    def to_corners(self, near, halves):
        return near

    def corner(self, near):
        return near

    def cores(self, near):
        half = near.shape[1] // 2
        out = []
        for side in range(2):
            out += [near[side], near[2 + side], near[4 + side]]
            out += [near[6 + side, :half], near[6 + side, half:]]
        return out

    def to_core(self, block):
        return block

    def far_sums(self, keep, got):
        return got

    def to_corner(self, both):
        return both

    def side_sums(self, keep, got, corner):
        return self.plane_sums(keep, jnp.concatenate([got, corner[None]]), None)

    def to_sides(self, sums):
        return sums

    def plane_sums(self, keep, got, rows):
        return [jnp.stack([keep, got], 1).reshape((8,) + keep.shape[1:])]

    def to_plane(self, sums):
        return sums

    def square(self, own):
        return own

    def square_cores(self, near):
        return [near[b] for b in (0, 2, 4, 6, 1, 3, 5, 7)]

    def last(self, near):
        return ()

    def cores_of(self, near, last):
        return self.cores(near)

    def far_cores(self, near):
        return ()

    def all_cores(self, near, far, last):
        return self.cores(near)

    def ring_sums(self, group, fields):
        ways = self.count // 8
        parts = [[cut(block, fields, w, ways) for w in range(ways)] for block in group[0]]
        return jnp.stack([p for block in parts for p in block]).astype(F32)

    def to_ring(self, parts, which):
        if 3 not in which:
            return parts
        return lax.psum_scatter(parts, self.axes, scatter_dimension=0, tiled=False)

    def add_ring(self, ring):
        return ring


def pack_expert(up, down):
    part = up.shape[0]
    up = up.reshape(part, 4, D).transpose(1, 0, 2).reshape(4 * part, D)
    return jnp.concatenate([up, down], 0)


def cut(rows, fields, place, ways=4):
    out, at = [], 0
    for groups, size in fields:
        part = rows[at : at + max(groups, 1) * size]
        at += max(groups, 1) * size
        if groups:
            part = part.reshape(groups, ways, size // ways, D)
            part = lax.dynamic_index_in_dim(part, place, 1, keepdims=False).reshape(-1, D)
        out.append(part)
    return jnp.concatenate(out)


def layer(
    make,
    tokens,
    modality,
    token_mask,
    cotangent,
    mask_vector,
    ln_one_gain,
    ln_one_shift,
    w_qkv,
    w_out,
    ln_two_gain,
    ln_two_shift,
    w_up,
    w_down,
):
    net = make()
    part = w_qkv.shape[0]
    seqs = tokens.shape[0] // LEN
    rows = seqs * SEQ
    columns = jnp.stack([ln_one_gain, ln_one_shift, ln_two_gain, ln_two_shift], 1)
    packed = jnp.concatenate([w_qkv, w_out, jnp.pad(columns, ((0, 0), (0, 124)))], 1)
    n_columns = packed.shape[1]
    ring = net.turns(packed)

    seq_masks = token_mask.reshape(seqs, LEN)
    masked = jnp.concatenate(
        [
            jnp.pad(seq_masks[:, :PATCHES], ((0, 0), (0, HEAD - PATCHES))),
            jnp.pad(seq_masks[:, PATCHES:], ((0, 0), (0, TAIL - LEN + PATCHES))),
        ],
        1,
    ).reshape(1, rows)
    order = jnp.cumsum(masked, 1)
    place = jnp.where(masked == 1, order - 1, -1)
    blocks = jnp.maximum((order[0, rows - 1] + BLK - 1) // BLK, 1)
    near = jnp.arange(8, dtype=jnp.int32)
    near = jnp.bitwise_xor(net.flat, near & 3) * 2 + jnp.bitwise_xor(net.core, near >> 2)
    where_ref = jnp.concatenate(
        [
            near,
            jnp.stack([net.core, net.flat, blocks]).astype(jnp.int32),
            modality.reshape(seqs, LEN)[:, 0],
        ]
    )
    masked = jnp.broadcast_to(masked.reshape(seqs, 1, SEQ), (seqs, 8, SEQ)).astype(F32)
    ring, where_ref = tie(ring, where_ref)

    own = net.ring(ring, part)
    near = net.square(own)
    text, _ = tie(pack_expert(w_up[1], w_down[1]), own)
    ring_text = net.turns(text)
    tokens, cotangent, _ = tie(tokens, cotangent, own)
    tokens = lay(tokens, seqs)
    cotangent = lay(cotangent, seqs)
    vector = mask_vector.astype(F32).reshape(1, D)
    near, place, tokens, cotangent, vector = tie(near, place, tokens, cotangent, vector)
    pieces = net.square_cores(near)
    own_text = net.ring(ring_text, part)
    pieces, own_text, image = tie(pieces, own_text, pack_expert(w_up[0], w_down[0]))
    near_text = net.sides(own_text)
    image = net.turns(image)

    qkv, softs, context, normed_one, params = call(
        attention_kernel,
        seqs,
        (where_ref, tokens, masked, vector, *pieces),
        [by_step((SEQ, D)), by_step((1, 8, SEQ)), whole((1, D))] + [ANY] * 8,
        [
            ((rows, 3 * D), BF16),
            ((seqs, H // 2, SEQ, 2 * SEQ), F32),
            ((rows, D), BF16),
            ((rows, D), BF16),
            ((8, D), F32),
        ],
        [
            by_step((SEQ, 3 * D)),
            by_step((1, H // 2, SEQ, 2 * SEQ)),
            by_step((SEQ, D)),
            by_step((SEQ, D)),
            pl.BlockSpec((8, D), lambda i, *_: (0, 0)),
        ],
        [pltpu.VMEM((D, n_columns), BF16), pltpu.SemaphoreType.DMA((10,))],
        "attention",
    )

    near_text, image, qkv, softs, context, normed_one, params = tie(
        near_text, image, qkv, softs, context, normed_one, params
    )
    near_text = net.corner(near_text)
    last, image = tie(net.last(near_text), net.ring(image, part))
    pieces_text = net.cores_of(near_text, last)
    near_image = net.sides(image)

    block = (ROWS_ONE, D)
    flat_rows = (seqs * LEN + 15) // 16 * 16
    keep, send, send_far, grad_context, sums = call(
        feed_back_kernel,
        4,
        (where_ref, place, vector, cotangent, context, params, *pieces_text, *pieces),
        [whole((1, rows)), whole((1, D)), whole((rows, D)), whole((rows, D)), whole((8, D))]
        + [ANY] * 18,
        [((4, *block), BF16), ((3, *block), BF16), (block, BF16), ((rows, D), BF16), ((8, D), F32)],
        [ANY] * 3 + [whole((rows, D)), whole((8, D))],
        [
            pltpu.VMEM((rows, D), BF16),
            pltpu.VMEM((rows, D), F32),
            pltpu.VMEM((rows, D), BF16),
            pltpu.VMEM((rows, D), BF16),
            pltpu.VMEM((rows, D), F32),
        ]
        + [pltpu.VMEM((D, D), F32)] * 2
        + [
            pltpu.VMEM((4, D, D), BF16),
            pltpu.VMEM((FF, D), BF16),
            pltpu.VMEM((D, D), BF16),
            pltpu.VMEM((2, 4, *block), BF16),
            pltpu.SemaphoreType.DMA((40,)),
            pltpu.SemaphoreType.DMA((10,)),
            pltpu.SemaphoreType.DMA((5, 5)),
        ],
        "feed_back",
    )
    near_image, keep, send, send_far, grad_context, sums = tie(
        near_image, keep, send, send_far, grad_context, sums
    )
    far = net.far_sums(keep, net.to_core(send_far))
    halves_image = net.halves(near_image)
    far, send, context, halves_image = tie(far, send, context, halves_image)
    got = net.to_core(send)
    corner = net.to_corner(far)
    near_image = net.to_corners(near_image, halves_image)
    experts = [pltpu.VMEM((4, D, D), BF16), pltpu.VMEM((FF, D), BF16)]
    after, normed_two = call(
        feed_text_kernel,
        4,
        (where_ref, tokens, masked, vector, context, params, *pieces_text, *pieces),
        [whole((rows, D)), whole((seqs, 8, SEQ)), whole((1, D)), whole((rows, D)), whole((8, D))]
        + [ANY] * 18,
        [((rows, D), F32), ((rows, D), BF16)],
        [whole((rows, D))] * 2,
        experts
        + [
            pltpu.VMEM((D, D), BF16),
            pltpu.SemaphoreType.DMA((40,)),
            pltpu.SemaphoreType.DMA((10,)),
            pltpu.VMEM((seqs * TAIL, D), BF16),
        ],
        "feed_text",
    )
    corner, got, near_image, after = tie(corner, got, near_image, after)
    sums_feed = net.side_sums(keep, got, corner)
    last_image = net.far_cores(net.last(near_image))
    sums_feed, grad_context, last_image = tie(sums_feed, grad_context, last_image)
    sums_feed = net.to_sides(sums_feed)
    far_image = net.far_cores(near_image[:3])

    keep, send, grad_tokens = call(
        attention_back_kernel,
        seqs,
        (where_ref, qkv, softs, grad_context, normed_one, tokens, masked, vector, params, sums)
        + tuple(pieces),
        [
            by_step((SEQ, 3 * D)),
            by_step((1, H // 2, SEQ, 2 * SEQ)),
            by_step((SEQ, D)),
            whole((rows, D)),
            by_step((SEQ, D)),
            by_step((1, 8, SEQ)),
            whole((1, D)),
            whole((8, D)),
            whole((8, D)),
        ]
        + [ANY] * 8,
        [((4, ROWS_QKV, D), BF16), ((4, ROWS_QKV, D), BF16), ((seqs * LEN, D), F32)],
        [ANY, ANY, whole((seqs * LEN, D))],
        [
            pltpu.VMEM((D, 3 * D), BF16),
            pltpu.VMEM((8, D), F32),
            pltpu.VMEM((rows, 3 * D), BF16),
            pltpu.VMEM((8, ROWS_QKV, D), BF16),
            pltpu.VMEM((flat_rows, D), F32),
            pltpu.SemaphoreType.DMA((10,)),
            pltpu.SemaphoreType.DMA((8,)),
        ],
        "attention_back",
    )
    keep, send, grad_tokens, sums_feed, far_image = tie(
        keep, send, grad_tokens, sums_feed, far_image
    )
    got = net.to_core(send)
    pieces_image = net.all_cores(near_image, far_image, last_image)
    sums_qkv = net.plane_sums(keep, got, 296)
    ring_one = net.ring_sums(sums_feed, [(4, 96), (1, 384), (1, 96)])
    sums_qkv, ring_one, after, pieces_image = tie(sums_qkv, ring_one, after, pieces_image)
    sums_qkv = net.to_plane(sums_qkv)
    ring_one = net.to_ring(ring_one, (1, 2))
    (output,) = call(
        feed_image_kernel,
        4,
        (where_ref, normed_two, after, *pieces_image),
        [whole((rows, D)), whole((rows, D))] + [ANY] * 10,
        [((seqs * LEN, D), BF16)],
        [whole((seqs * LEN, D))],
        [pltpu.VMEM((rows, D), F32)]
        + experts
        + [pltpu.SemaphoreType.DMA((40,)), pltpu.VMEM((flat_rows, D), F32)],
        "feed_image",
    )
    sums_qkv, ring_one, output = tie(sums_qkv, ring_one, output)
    ring_two = net.ring_sums(sums_qkv, [(3, 96), (0, 8)])
    ring_one = net.to_ring(ring_one, (3,))
    ring_two = net.to_ring(ring_two, (1, 2, 3))

    grads = net.add_ring(ring_one)
    grad_w_up = grads[: 4 * part].reshape(4, part, D).transpose(1, 0, 2).reshape(part, FF)
    grad_w_down = grads[4 * part : 8 * part]
    grad_w_out = grads[8 * part : 9 * part]
    grads = net.add_ring(ring_two)
    grad_w_qkv = grads[: 3 * part].reshape(3, part, D).transpose(1, 0, 2).reshape(part, 3 * D)
    extra = grads[3 * part :]
    owned = lax.dynamic_slice_in_dim(extra, net.index * part, part, 1)

    return (
        output,
        grad_tokens,
        extra[2],
        owned[3],
        owned[4],
        grad_w_qkv,
        grad_w_out,
        owned[0],
        owned[1],
        grad_w_up,
        grad_w_down,
    )


def solution(mesh):
    if (mesh.shape["dp"], mesh.shape["fsdp"]) == (8, 4):
        mesh = Mesh(mesh.devices.reshape(2, 2, 2, 4), Cube.axes)
        make = Cube
    else:
        make = functools.partial(Flat, mesh.size)
    axes = Cube.axes if make is Cube else Flat.axes
    row, flat = P(axes, None), P(axes)
    middle = P(None, axes, None)
    in_specs = (row, flat, flat, row, P(), flat, flat, row, row, flat, flat, middle, middle)
    out_specs = (row, row, P(), flat, flat, row, row, flat, flat, row, row)
    return jax.shard_map(
        functools.partial(layer, make),
        mesh=mesh,
        in_specs=in_specs,
        out_specs=out_specs,
        check_vma=False,
    )
```
